512 devices in a mesh: gx: 16 (over z), gy: 32 (over x, y, core).
Axes of the slice: x: 4, y: 4, z: 16, core: 2. Of those that a mesh axis runs over, the one named last changes fastest.
Arguments:
- normals: bfloat16 [16384, 3, 64], P(('gx', 'gy')), may hold values from -6 to 6
- owners: int32 [16384, 1], P(('gx', 'gy')), may hold values from 0 to 31; in each aligned block of 32 rows (0 to 31, 32 to 63, ...) at most 2 rows name the same one
- cells: int32 [16384, 64], P(('gx', 'gy')), may hold values from 0 to 16383
- target: float32 [128, 256, 256], P('gx', 'gy'), may hold values from -4 to 4
Outputs:
- indicator: float32 [128, 256, 256], P('gx', 'gy')
- slope: float32 [3, 128, 256, 256], P(None, 'gx', 'gy')
- normal_grad: float32 [16384, 3, 64], P(('gx', 'gy'))
The draws below stay inside these ranges and needn't reach their ends.
Inputs may be any that keep to these rules, and one draw needn't show every extreme that they name: `owners`: among the 32 blocks of one device no owner is named more than 2 times, and some device names some owner exactly 2 times.
All inputs are finite; a program needn't handle non-finite values.
Results may differ from the reference program's by a relative error of at most 0.0004.
Values may be sent and summed in bfloat16 or wider, within the bound.
No kernel may reach another device: no remote copies, remote signals or barrier semaphores. Data moves between devices by JAX's collectives and lax.ppermute only.
A program may use at most 128 MiB of HBM per device.

```python
import math
import jax
import jax.numpy as jnp
import numpy as np

CX = 8
CY = 8
NZ = 256
BLK_DEV = 32
SPB = 64
NX = 128
NY = 256
CAP = 2
BLOCKS = 16384
N_GY = 32


def place_ends(values, own_key, smallest, top_value):
    shape = values.shape
    spot = [jax.random.randint(jax.random.fold_in(own_key, axis), (), 0, shape[axis]) for axis in range(len(shape))]
    values = values.at[tuple(spot)].set(smallest)
    longest = shape.index(max(shape))
    spot[longest] = (spot[longest] + 1) % shape[longest]
    return values.at[tuple(spot)].set(top_value)


def steps_of(stream_key, shape, shards, low, top_value):
    level, own = 1.0, jax.random.fold_in(stream_key, 6)
    for dim, blocks in shards:
        steps = jnp.exp(jax.random.uniform(jax.random.fold_in(own, dim), (blocks,), jnp.float32, low / len(shards), top_value / len(shards)))
        level = level * jnp.repeat(steps, shape[dim] // blocks).reshape([-1 if axis == dim else 1 for axis in range(len(shape))])
    return level


def shared_out(rng, own, number, rows, number_of, top, bound, lean):
    order = jax.random.permutation(rng, number_of)
    packed, ordinary = portions_of(number_of, rows * top, bound, lean, True), portions_of(number_of, rows * top, bound, lean, False)
    places = jnp.arange(number_of)

    def named(tallies, turn):
        used = int((tallies > 0).sum())
        fixed = max(1, used // 4)
        shifted = fixed + (places - fixed + turn * (used - fixed)) % max(1, number_of - fixed)
        return jnp.zeros((number_of,), jnp.int32).at[order[jnp.where(places < fixed, places, shifted)]].set(jnp.asarray(tallies, jnp.int32))

    tallies = jnp.where(number % 4 == 0, named(packed, number // 4), named(ordinary, number - number // 4 - 1))
    mixed = jax.random.permutation(jax.random.fold_in(own, 3), number_of)
    donor, receiver = mixed[0:number_of // 2 * 2:2], mixed[1:number_of // 2 * 2:2]
    room = jnp.minimum(tallies[donor] - 1, bound - tallies[receiver]) // 2
    room = jnp.where((donor == order[0]) | (receiver == order[0]) | (tallies[receiver] == 0), 0, jnp.maximum(room, 0))
    shifted = jax.random.randint(jax.random.fold_in(own, 4), (number_of // 2,), 0, 1 << 20) % (room + 1)
    tallies = tallies.at[donor].add(-shifted).at[receiver].add(shifted)
    items = jnp.searchsorted(jnp.cumsum(tallies), jnp.arange(rows * top), side="right").astype(jnp.int32)
    grid = items.reshape(top, rows).T
    grid = grid[jax.random.permutation(jax.random.fold_in(own, 1), rows)]
    turn = jax.random.randint(jax.random.fold_in(own, 2), (rows, 1), 0, top)
    return jnp.take_along_axis(grid, (jnp.arange(top)[None, :] + turn) % top, axis=1)


def portions_of(amount, total, limit, lean, full):
    loads = [(1 << 20) // math.isqrt(standing ** lean) + 1 for standing in range(1, amount + 1)]
    largest = limit if full else min(limit, max(-(-total // amount), total * loads[0] // sum(loads)))
    least = 1 if total - largest >= amount - 1 else 0
    holding, spare = [largest] + [least] * (amount - 1), total - largest - least * (amount - 1)
    while spare > 0:
        movable = [i for i in range(1, amount) if holding[i] < largest] or [i for i in range(1, amount) if holding[i] < limit]
        whole, left = sum([loads[i] for i in movable]), spare
        for i in movable:
            addition = min(limit - holding[i], max(1, left * loads[i] // whole), spare)
            holding[i] = holding[i] + addition
            spare = spare - addition
    return np.array(holding)


def noise(key, shape, deviation, most, cuts=(), held_as=jnp.bfloat16):
    result = jax.random.normal(key, shape, jnp.float32) * deviation
    if len(cuts) > 0:
        result = steps_of(key, shape, cuts, -0.22, 0.18) * result
    return jnp.clip(result, min=-most, max=most).astype(held_as)


def setup_inputs(seed: int = 0) -> dict:
    key_of = jax.random.split(jax.random.key(seed), 5)
    normals = noise(key_of[0], (BLOCKS, 3, SPB), 1.0, 6.0, ((0, 512),))
    owners_keys = jax.random.split(jax.random.fold_in(key_of[1], 1), BLOCKS // BLK_DEV)
    owners_turns = jax.random.permutation(jax.random.fold_in(key_of[1], 3), BLOCKS // BLK_DEV)
    owners = jax.vmap(lambda own, number: shared_out(jax.random.fold_in(key_of[1], 2), own, number, BLK_DEV, N_GY, 1, CAP, 2))(owners_keys, owners_turns).reshape((BLOCKS, 1))
    cells = place_ends(jax.random.randint(key_of[2], (BLOCKS, SPB), 0, CX * CY * NZ), jax.random.fold_in(key_of[2], 1), 0, (CX * CY * NZ) - 1).astype(jnp.int32)
    target = noise(key_of[3], (NX, NY, NZ), 0.5, 4.0, ((0, 16), (1, 32)), jnp.float32)
    return dict(normals=normals, owners=owners, cells=cells, target=target)


smooth_width = 64.0

def frequency(index, length):
    full = jnp.where(index < length // 2, index, index - length).astype(jnp.float32)
    odd = jnp.where(index == length // 2, jnp.zeros_like(full), full)
    return (full, odd)

def reference(normals, owners, cells, target):
    device = jnp.arange(BLOCKS, dtype=jnp.int32) // BLK_DEV
    row_x = device // N_GY
    column = cells // NZ
    place_x = row_x[:, None] * CX + column // CY
    place_y = owners[:, 0:1] * CY + column % CY
    flat = ((place_x * NY + place_y) * NZ + cells % NZ).astype(jnp.int32)
    values = jnp.moveaxis(normals.astype(jnp.float32), 1, 0).reshape(3, -1)
    field = jnp.zeros((3, NX * NY * NZ), jnp.float32).at[:, flat.reshape(-1)].add(values)
    field = field.reshape(3, NX, NY, NZ)
    full_x, odd_x = frequency(jnp.arange(NX, dtype=jnp.int32), NX)
    full_y, odd_y = frequency(jnp.arange(NY, dtype=jnp.int32), NY)
    full_z, odd_z = frequency(jnp.arange(NZ, dtype=jnp.int32), NZ)
    ksq = full_x[:, None, None] ** 2 + full_y[None, :, None] ** 2 + full_z[None, None, :] ** 2
    gain = jnp.sqrt(jnp.float32(NX * NY * NZ) * jnp.float32(CX * CY * NZ) / (jnp.float32(BLK_DEV * SPB) * 700.0))
    base = gain * jnp.exp(-ksq / (2.0 * smooth_width ** 2)) / jnp.maximum(ksq, 1.0)
    factors = (-odd_x[:, None, None] * base, -odd_y[None, :, None] * base, -odd_z[None, None, :] * base)
    spectrum = 1j * factors[0] * jnp.fft.fftn(field[0])
    spectrum = spectrum + 1j * factors[1] * jnp.fft.fftn(field[1])
    spectrum = spectrum + 1j * factors[2] * jnp.fft.fftn(field[2])
    indicator = jnp.real(jnp.fft.ifftn(spectrum)).astype(jnp.float32)
    residue = 0.25 * (indicator - target)
    residue_spec = jnp.fft.fftn(residue)
    grads = []
    for comp in range(3):
        grads.append(jnp.real(jnp.fft.ifftn(-1j * factors[comp] * residue_spec)).astype(jnp.float32))
    grad_flat = jnp.stack(grads).reshape(3, -1)
    picked = grad_flat[:, flat]
    normal_grad = jnp.moveaxis(picked, 0, 1)
    slope = jnp.stack([(jnp.roll(indicator, -1, axis) - jnp.roll(indicator, 1, axis)) * 0.5 for axis in range(3)])
    return (indicator, slope, normal_grad)
```

```python
import math

import jax
import jax.numpy as jnp
import ml_dtypes
import numpy as np
from jax import lax
from jax.experimental import pallas as pl
from jax.experimental.pallas import tpu as pltpu
from jax.sharding import PartitionSpec as P

GX, GY = 16, 32
BX, BY, NZ = 8, 8, 256
NX, NY = GX * BX, GY * BY
KZ = NZ // 2 // GY
KB = NY // BY // GX
BLOCKS, POINTS, CAP = 32, 64, 2
WIDTH = 64.0
F32, BF16 = jnp.float32, jnp.bfloat16


def halves(table):
    high = table.astype(ml_dtypes.bfloat16)
    low = (table - high.astype(np.float64)).astype(ml_dtypes.bfloat16)
    return np.stack([high, low])


def unit(turns):
    return np.exp(-2j * np.pi * turns)


def parts_of(w):
    return np.stack([np.stack([w.real, -w.imag]), np.stack([w.imag, w.real])])


Y_CLASS = np.array([[h, -h if h else 16] for h in range(GX)])
X_CLASS = np.array([k if k <= 8 else k - 16 for k in range(16)])


def make_tables():
    z = np.arange(NZ)
    kz = np.arange(NZ // 2)
    w = unit((kz[:, None] * z[None, :] % NZ) / NZ)
    zf = np.stack([w.real, w.imag])
    zf[1, 0] = np.where(z % 2 == 0, 1.0, -1.0)
    zb = 2.0 * zf
    zb[:, 0] = zf[:, 0]
    zb = zb / (NX * NY * NZ)
    order = lambda t: t.reshape(2, GY, KZ, NZ).transpose(1, 0, 2, 3).reshape(NZ, NZ)
    g = np.arange(GY)
    wy = parts_of(unit(Y_CLASS.reshape(-1)[:, None] * g[None, :] / GY))
    y_rows = np.einsum("abkg,zw->akzgbw", wy, np.eye(KZ)).reshape(NZ, NZ)
    g = np.arange(GX)
    wx = parts_of(unit(X_CLASS[:, None] * g[None, :] / GX))
    x_rows = np.einsum("abkg,zw->akzgbw", wx, np.eye(KB * KZ)).reshape(NZ, NZ)
    e = np.arange(8)
    w8 = unit((e[:, None] * e[None, :] % 8) / 8)
    y_lanes = np.concatenate([np.kron(np.eye(16), w8.real), np.kron(np.eye(16), w8.imag)], 1)
    x8 = lambda t: np.kron(np.eye(2), np.kron(t, np.eye(8)))
    x_lanes = np.concatenate([x8(w8.real), x8(w8.imag)], 1)
    ty = unit(np.repeat(Y_CLASS.reshape(-1), KZ)[:, None] * np.tile(e, 16)[None, :] / NY)
    tx = unit(
        np.repeat(X_CLASS, KB * KZ)[:, None] * np.tile(np.repeat(e, 8), 2)[None, :] / NX
    )
    twist = lambda t: np.stack([t.real, -t.imag]).astype(np.float32)
    mirror = np.zeros((2, 2, 128, 128), np.float32)
    for m in range(2):
        for n in range(2):
            for f in range(2):
                for a in range(8):
                    for b in range(8):
                        src = f * 64 + (-a - m) % 8 * 8 + (-b - n) % 8
                        mirror[m, n, src, f * 64 + a * 8 + b] = 1.0
    return dict(
        zf=halves(order(zf)),
        zb=halves(order(zb)),
        y_rows=halves(y_rows),
        x_rows=halves(x_rows),
        y_lanes=halves(y_lanes),
        x_lanes=halves(x_lanes),
        ty=twist(ty),
        tx=twist(tx),
        mirror=mirror.reshape(512, 128).astype(ml_dtypes.bfloat16),
    )


TABLES = make_tables()


def split(x):
    high = x.astype(BF16)
    return high, (x - high.astype(F32)).astype(BF16)


def mm(a, b, ca=1, cb=0):
    return lax.dot_general(a, b, (((ca,), (cb,)), ((), ())), preferred_element_type=F32)


def mm3(a, b, ca=1, cb=0):
    return mm(a[0], b[0], ca, cb) + (mm(a[0], b[1], ca, cb) + mm(a[1], b[0], ca, cb))


def lanes_of(pairs, table, sign):
    stacked = jnp.concatenate([pairs[0][0], pairs[1][0], pairs[0][1], pairs[1][1]], 0)
    out = mm3(split(stacked), table)
    rows = pairs[0][0].shape[0]
    result = []
    for i in range(2):
        a = out[i * rows : (i + 1) * rows]
        b = out[(2 + i) * rows : (3 + i) * rows]
        if sign > 0:
            result.append((a[:, :128] - b[:, 128:], a[:, 128:] + b[:, :128]))
        else:
            result.append((a[:, :128] + b[:, 128:], b[:, :128] - a[:, 128:]))
    return result


def twisted(pairs, twist, sign):
    c, s = twist[0], twist[1]
    if sign > 0:
        return [(a * c + b * s, b * c - a * s) for a, b in pairs]
    return [(a * c - b * s, b * c + a * s) for a, b in pairs]


def halves_of(real, imag):
    return [(real[:, i * 128 : (i + 1) * 128], imag[:, i * 128 : (i + 1) * 128]) for i in range(2)]


def whole_of(pairs):
    return tuple(jnp.concatenate([pairs[0][c], pairs[1][c]], 1) for c in range(2))


def table_of(ref):
    return ref[0], ref[1]


def iota(shape, dim):
    return lax.broadcasted_iota(jnp.int32, shape, dim)


def places(route, first, count):
    rows = jnp.concatenate([route[s] for s in range(first, first + count)], 1)
    cell = rows[3:4]
    column = jnp.floor(cell * (1.0 / NZ))
    return rows, column, cell - column * NZ


STEP = 4


def splat_body(route, target, zf, out):
    width = STEP * CAP * POINTS
    columns = iota((BX * BY, width), 0).astype(F32)
    levels = iota((NZ, width), 0).astype(F32)
    field = jnp.zeros((3 * BX * BY, NZ), F32)
    for first in range(0, GY, STEP):
        rows, column, level = places(route, first, STEP)
        here = columns == column
        weighted = [jnp.where(here, rows[j : j + 1], 0.0) for j in range(3)]
        weighted = jnp.concatenate(weighted, 0).astype(BF16)
        hot = jnp.where(levels == level, 1.0, 0.0).astype(BF16)
        field = field + mm(weighted, hot, 1, 1)
    both = jnp.concatenate([field, target[...].reshape(BX * BY, NZ)], 0)
    out[...] = mm3(table_of(zf), split(both), 1, 1).reshape(out.shape)


def forward_y_body(got, rows, lanes, twist, out):
    x = mm3(table_of(rows), split(got[...].reshape(NZ, NZ)))
    pairs = twisted(halves_of(x[:128], x[128:]), twist, 1)
    real, imag = whole_of(lanes_of(pairs, table_of(lanes), 1))
    out[:, 0:8, :] = real.reshape(GX, 8, NZ)
    out[:, 8:16, :] = imag.reshape(GX, 8, NZ)


def filters(gx, gy):
    shape = (128, 128)
    row, lane = iota(shape, 0), iota(shape, 1)
    kxb = row >> 3
    kx = kxb + 16 * ((lane >> 3) & 7)
    second = (row >> 2) & 1
    kb = jnp.where(second == 0, gx, jnp.where(gx == 0, 16, GY - gx))
    ka = (lane & 7) - jnp.where((second == 1) & (gx != 0), 1, 0)
    ky = (kb + 32 * ka) & (NY - 1)
    kz = KZ * gy + (row & 3)
    kx = jnp.where(kxb > 8, kx - 16, kx) & (NX - 1)
    ux = jnp.where(kx < NX // 2, kx, kx - NX).astype(F32)
    uy = jnp.where(ky < NY // 2, ky, ky - NY).astype(F32)
    ox = jnp.where(kx == NX // 2, 0.0, ux)
    oy = jnp.where(ky == NY // 2, 0.0, uy)
    oz = kz.astype(F32)
    gain = math.sqrt(float(NX * NY * NZ) * float(BX * BY * NZ) / (float(BLOCKS * POINTS) * 700.0))
    plane = ux * ux + uy * uy

    def base(ksq):
        return gain * jnp.exp(ksq * (-1.0 / (2.0 * WIDTH**2))) / jnp.maximum(ksq, 1.0)

    packed = kz == 0
    base0 = base(plane + oz * oz)
    base1 = jnp.where(packed, base(plane + float(NZ // 2) ** 2), base0)
    mean, diff = (base0 + base1) * 0.5, (base0 - base1) * 0.5
    left = -jnp.where(lane < 64, ox, oy)
    right = -jnp.where(lane < 64, oz, 0.0)
    return (left * mean, right * mean), (left * diff, right * diff)


def mirrored(pairs, gx, mirror):
    shape = (128, 128)
    row, other = iota(shape, 0), iota(shape, 1)
    swap = jnp.where(gx == 0, 0, 4)
    partner = (((16 - (row >> 3)) & 15) << 3) | ((row & 7) ^ swap)
    moves = jnp.where(other == partner, 1.0, 0.0).astype(BF16)
    wide = jnp.concatenate([pairs[0][0], pairs[1][0], pairs[0][1], pairs[1][1]], 1)
    high, low = split(wide)
    moved = mm(moves, high) + mm(moves, low)
    stacked = jnp.concatenate([moved[:, i * 128 : (i + 1) * 128] for i in range(4)], 0)
    row = iota((512, 128), 0) & 127
    half_x = (row >> 3) == 8
    half_y = (((row >> 2) & 1) == 1) & (gx == 0)
    total = jnp.zeros((512, 128), F32)
    for case in range(4):
        here = (half_x == (case >= 2)) & (half_y == (case % 2 == 1))
        high, low = split(jnp.where(here, stacked, 0.0))
        table = mirror[case * 128 : (case + 1) * 128, :]
        total = total + mm(high, table) + mm(low, table)
    quarter = [total[i * 128 : (i + 1) * 128] for i in range(4)]
    return [(quarter[0], -quarter[2]), (quarter[1], -quarter[3])]


def spectrum_body(place, got, rows, lanes, twist, mirror, out):
    gx, gy = place[0], place[1]
    x = mm3(table_of(rows), split(got[...].reshape(NZ, NZ)))
    pairs = twisted(halves_of(x[:128], x[128:]), twist, 1)
    pairs = lanes_of(pairs, table_of(lanes), 1)
    mean, diff = filters(gx, gy)
    other = mirrored(pairs, gx, mirror)
    low = iota((128, 128), 1) < 64

    def summed(a, b, c):
        both = [a[0] * b[0][c] + a[1] * b[1][c]]
        return both[0] + pltpu.roll(both[0], 64, 1)

    def target_of(b, c):
        return jnp.where(low, pltpu.roll(b[1][c], 64, 1), b[1][c])

    s = [summed(mean, pairs, c) + summed(diff, other, c) for c in range(2)]
    s2 = [summed(diff, pairs, c) + summed(mean, other, c) for c in range(2)]
    t = (-target_of(pairs, 1), target_of(pairs, 0))
    t2 = (-target_of(other, 1), target_of(other, 0))
    chi = (-s[1], s[0])
    grads = []
    for i in range(2):
        grads.append(
            tuple(
                0.25 * (mean[i] * (s[c] + t[c]) + diff[i] * (s2[c] + t2[c])) for c in range(2)
            )
        )
    grads[1] = tuple(jnp.where(low, grads[1][c], chi[c]) for c in range(2))
    pairs = lanes_of(grads, table_of(lanes), -1)
    pairs = twisted(pairs, twist, -1)
    both = jnp.concatenate(whole_of(pairs), 0)
    out[...] = mm3(table_of(rows), split(both), 0, 0).reshape(out.shape)


def inverse_y_body(got, rows, lanes, twist, out):
    real = got[:, 0:8, :].reshape(128, NZ)
    imag = got[:, 8:16, :].reshape(128, NZ)
    pairs = lanes_of(halves_of(real, imag), table_of(lanes), -1)
    pairs = twisted(pairs, twist, -1)
    both = jnp.concatenate(whole_of(pairs), 0)
    out[...] = mm3(table_of(rows), split(both), 0, 0).reshape(out.shape)


def pick_body(got, zb, route, chi, edges, picked):
    values = mm3(split(got[...].reshape(NZ, NZ)), table_of(zb), 0, 0)
    cells = BX * BY
    solid = values[3 * cells :]
    chi[...] = solid.reshape(BX, BY, NZ)
    edges[0] = solid[0:BY]
    edges[1] = solid[cells - BY :]
    for x in range(BX):
        edges[2, x : x + 1, :] = solid[x * BY : x * BY + 1]
        edges[3, x : x + 1, :] = solid[x * BY + BY - 1 : x * BY + BY]
    high, low = split(values[: 3 * cells])
    width = STEP * CAP * POINTS
    columns = iota((cells, width), 0).astype(F32)
    levels = iota((NZ, width), 0).astype(F32)
    for first in range(0, GY, STEP):
        _, column, level = places(route, first, STEP)
        hot = jnp.where(levels == level, 1.0, 0.0).astype(BF16)
        at_level = mm(high, hot) + mm(low, hot)
        here = columns == column
        lines = [
            jnp.sum(jnp.where(here, at_level[j * cells : (j + 1) * cells], 0.0), 0, keepdims=True)
            for j in range(3)
        ]
        lines = jnp.concatenate(lines + [jnp.zeros((1, width), F32)], 0)
        for s in range(STEP):
            picked[first + s] = lines[:, s * 128 : (s + 1) * 128]


def slope_body(chi, x_low, x_high, y_low, y_high, out):
    for x in range(BX):
        here = chi[x]
        before = chi[x - 1] if x > 0 else x_low[0]
        after = chi[x + 1] if x < BX - 1 else x_high[0]
        out[0, x] = (after - before) * 0.5
        side = iota((BY, NZ), 0)
        up = jnp.where(side == BY - 1, y_high[0, x : x + 1, :], pltpu.roll(here, BY - 1, 0))
        down = jnp.where(side == 0, y_low[0, x : x + 1, :], pltpu.roll(here, 1, 0))
        out[1, x] = (up - down) * 0.5
        out[2, x] = (pltpu.roll(here, NZ - 1, 1) - pltpu.roll(here, 1, 1)) * 0.5


def route_body(owners, normals, cells, out, count):
    row = iota((4, 128), 0)
    half = iota((4, 128), 1) >> 6
    empty = jnp.where(row == 3, -1.0, 0.0)
    for o in range(GY):
        out[o] = empty
        count[o] = 0
    for b in range(BLOCKS):
        owner = owners[b]
        rank = count[owner]
        count[owner] = rank + 1
        value = jnp.concatenate([normals[b].astype(F32), cells[b : b + 1, :].astype(F32)], 0)
        value = jnp.concatenate([value, value], 1)
        out[owner] = jnp.where(half == rank, value, out[owner])


def return_body(owners, got, out, count):
    for o in range(GY):
        count[o] = 0
    for b in range(BLOCKS):
        owner = owners[b]
        rank = count[owner]
        count[owner] = rank + 1
        value = got[owner]
        value = jnp.where(rank == 0, value[:, :64], value[:, 64:])
        out[b] = value[0:3]


VMEM = pl.BlockSpec(memory_space=pltpu.VMEM)
SMEM = pl.BlockSpec(memory_space=pltpu.SMEM)


def call(body, name, outs, *operands, scalars=0, scratch=()):
    shapes = [jax.ShapeDtypeStruct(s, F32) for s in outs]
    single = len(shapes) == 1
    return pl.pallas_call(
        body,
        name=name,
        out_shape=shapes[0] if single else shapes,
        in_specs=[SMEM] * scalars + [VMEM] * (len(operands) - scalars),
        out_specs=VMEM if single else [VMEM] * len(shapes),
        scratch_shapes=list(scratch),
        compiler_params=pltpu.CompilerParams(vmem_limit_bytes=40 * 1024 * 1024),
    )(*operands)


def swap(x, axis):
    return lax.all_to_all(x, axis, split_axis=0, concat_axis=0, tiled=True)


def shifted(x, axis, step):
    count = lax.axis_size(axis)
    return lax.ppermute(x, axis, [(i, (i + step) % count) for i in range(count)])


def local(normals, owners, cells, target):
    table = {k: jnp.asarray(v) for k, v in TABLES.items()}
    owner = owners.reshape(BLOCKS)
    counts = (pltpu.SMEM((GY,), jnp.int32),)
    place = jnp.stack([lax.axis_index("gx"), lax.axis_index("gy")]).astype(jnp.int32)

    message = (GY, 4, CAP * POINTS)
    sent = call(route_body, "route", [message], owner, normals, cells, scalars=1, scratch=counts)
    route = swap(sent, "gy")
    by_z, by_x = (GY, 8, NZ), (GX, 16, NZ)
    spread = call(splat_body, "splat", [by_z], route, target, table["zf"])
    got = swap(spread, "gy")
    y_args = (table["y_rows"], table["y_lanes"], table["ty"])
    spread = call(forward_y_body, "forward_y", [by_x], got, *y_args)
    got = swap(spread, "gx")
    x_args = (table["x_rows"], table["x_lanes"], table["tx"], table["mirror"])
    spread = call(spectrum_body, "spectrum", [by_x], place, got, *x_args, scalars=1)
    got = swap(spread, "gx")
    spread = call(inverse_y_body, "inverse_y", [by_z], got, *y_args)
    got = swap(spread, "gy")
    chi, edges, picked = call(
        pick_body, "pick", [(BX, BY, NZ), (4, 8, NZ), message], got, table["zb"], route
    )
    returned = swap(picked, "gy")
    x_low = shifted(edges[1:2], "gx", 1)
    x_high = shifted(edges[0:1], "gx", -1)
    y_low = shifted(edges[3:4], "gy", 1)
    y_high = shifted(edges[2:3], "gy", -1)
    slope = call(slope_body, "slope", [(3, BX, BY, NZ)], chi, x_low, x_high, y_low, y_high)
    normal_grad = call(
        return_body, "deliver", [(BLOCKS, 3, POINTS)], owner, returned, scalars=1, scratch=counts
    )
    return chi, slope, normal_grad


def solution(mesh):
    placed = (
        P(("gx", "gy"), None, None),
        P(("gx", "gy"), None),
        P(("gx", "gy"), None),
        P("gx", "gy", None),
    )
    return jax.shard_map(
        local,
        mesh=mesh,
        in_specs=placed,
        out_specs=(P("gx", "gy", None), P(None, "gx", "gy", None), P(("gx", "gy"), None, None)),
        check_vma=False,
    )
```

```python
import math

import jax
import jax.numpy as jnp
import ml_dtypes
import numpy as np
from jax import lax
from jax.experimental import pallas as pl
from jax.experimental.pallas import tpu as pltpu
from jax.sharding import PartitionSpec as P

GX, GY = 16, 32
BX, BY, NZ = 8, 8, 256
NX, NY = GX * BX, GY * BY
KZ = NZ // 2 // GY
KB = NY // BY // GX
BLOCKS, POINTS, CAP = 32, 64, 2
WIDTH = 64.0
F32, BF16 = jnp.float32, jnp.bfloat16


def halves(table):
    high = table.astype(ml_dtypes.bfloat16)
    low = (table - high.astype(np.float64)).astype(ml_dtypes.bfloat16)
    return np.stack([high, low])


def unit(turns):
    return np.exp(-2j * np.pi * turns)


def parts_of(w):
    return np.stack([np.stack([w.real, -w.imag]), np.stack([w.imag, w.real])])


Y_CLASS = np.array([[h, -h if h else 16] for h in range(GX)])
X_CLASS = np.array([k if k <= 8 else k - 16 for k in range(16)])


def make_tables():
    z = np.arange(NZ)
    kz = np.arange(NZ // 2)
    w = unit((kz[:, None] * z[None, :] % NZ) / NZ)
    zf = np.stack([w.real, w.imag])
    zf[1, 0] = np.where(z % 2 == 0, 1.0, -1.0)
    zb = 2.0 * zf
    zb[:, 0] = zf[:, 0]
    zb = zb / (NX * NY * NZ)
    order = lambda t: t.reshape(2, GY, KZ, NZ).transpose(1, 0, 2, 3).reshape(NZ, NZ)
    g = np.arange(GY)
    wy = parts_of(unit(Y_CLASS.reshape(-1)[:, None] * g[None, :] / GY))
    y_rows = np.einsum("abkg,zw->akzgbw", wy, np.eye(KZ)).reshape(NZ, NZ)
    g = np.arange(GX)
    wx = parts_of(unit(X_CLASS[:, None] * g[None, :] / GX))
    x_rows = np.einsum("abkg,zw->akzgbw", wx, np.eye(KB * KZ)).reshape(NZ, NZ)
    e = np.arange(8)
    w8 = unit((e[:, None] * e[None, :] % 8) / 8)
    y_lanes = np.concatenate([np.kron(np.eye(16), w8.real), np.kron(np.eye(16), w8.imag)], 1)
    x8 = lambda t: np.kron(np.eye(2), np.kron(t, np.eye(8)))
    x_lanes = np.concatenate([x8(w8.real), x8(w8.imag)], 1)
    ty = unit(np.repeat(Y_CLASS.reshape(-1), KZ)[:, None] * np.tile(e, 16)[None, :] / NY)
    tx = unit(
        np.repeat(X_CLASS, KB * KZ)[:, None] * np.tile(np.repeat(e, 8), 2)[None, :] / NX
    )
    ky = np.repeat(Y_CLASS.reshape(-1), KZ)[:, None] + GY * e[None, :]
    slope_y = np.tile(np.sin(2 * np.pi * (ky % NY) / NY), (1, 16))
    kx = np.repeat(X_CLASS, KB * KZ)[:, None] + GX * np.repeat(e, 8)[None, :]
    slope_x = np.tile(np.sin(2 * np.pi * (kx % NX) / NX), (1, 2))
    twist = lambda t, s: np.stack([t.real, -t.imag, s]).astype(np.float32)
    mirror = np.zeros((2, 2, 128, 128), np.float32)
    for m in range(2):
        for n in range(2):
            for f in range(2):
                for a in range(8):
                    for b in range(8):
                        src = f * 64 + (-a - m) % 8 * 8 + (-b - n) % 8
                        mirror[m, n, src, f * 64 + a * 8 + b] = 1.0
    return dict(
        zf=halves(order(zf)),
        zb=halves(order(zb)),
        y_rows=halves(y_rows),
        x_rows=halves(x_rows),
        y_lanes=halves(y_lanes),
        x_lanes=halves(x_lanes),
        ty=twist(ty, slope_y),
        tx=twist(tx, slope_x),
        mirror=mirror.reshape(512, 128).astype(ml_dtypes.bfloat16),
    )


TABLES = make_tables()


def split(x):
    high = x.astype(BF16)
    return high, (x - high.astype(F32)).astype(BF16)


def mm(a, b, ca=1, cb=0):
    return lax.dot_general(a, b, (((ca,), (cb,)), ((), ())), preferred_element_type=F32)


def mm3(a, b, ca=1, cb=0):
    return mm(a[0], b[0], ca, cb) + (mm(a[0], b[1], ca, cb) + mm(a[1], b[0], ca, cb))


def lanes_of(pairs, table, sign):
    count, rows = len(pairs), pairs[0][0].shape[0]
    stacked = jnp.concatenate([p[0] for p in pairs] + [p[1] for p in pairs], 0)
    out = mm3(split(stacked), table)
    result = []
    for i in range(count):
        a = out[i * rows : (i + 1) * rows]
        b = out[(count + i) * rows : (count + i + 1) * rows]
        if sign > 0:
            result.append((a[:, :128] - b[:, 128:], a[:, 128:] + b[:, :128]))
        else:
            result.append((a[:, :128] + b[:, 128:], b[:, :128] - a[:, 128:]))
    return result


def twisted(pairs, twist, sign):
    c, s = twist[0], twist[1]
    if sign > 0:
        return [(a * c + b * s, b * c - a * s) for a, b in pairs]
    return [(a * c - b * s, b * c + a * s) for a, b in pairs]


def halves_of(real, imag):
    return [(real[:, i * 128 : (i + 1) * 128], imag[:, i * 128 : (i + 1) * 128]) for i in range(2)]


def whole_of(pairs):
    return tuple(jnp.concatenate([p[c] for p in pairs], 1) for c in range(2))


def table_of(ref):
    return ref[0], ref[1]


def iota(shape, dim):
    return lax.broadcasted_iota(jnp.int32, shape, dim)


def places(route, first, count):
    rows = jnp.concatenate([route[s] for s in range(first, first + count)], 1)
    cell = rows[3:4]
    column = jnp.floor(cell * (1.0 / NZ))
    return rows, column, cell - column * NZ


def kz_of(rows):
    row = iota((rows, 128), 0)
    return (KZ * (row >> 3) + (row & 3)).astype(F32)


def odd(k, length):
    k = k & (length - 1)
    u = jnp.where(k < length // 2, k, k - length).astype(F32)
    return u, jnp.where(k == length // 2, 0.0, u)


def ky_of(gx, row, lane):
    second = ((row >> 2) & 1) == 1
    kb = jnp.where(second, jnp.where(gx == 0, 16, -gx), gx)
    return kb + GY * (lane & 7)


def oy_of():
    row, lane = iota((128, 128), 0), iota((128, 128), 1)
    return odd(ky_of(row >> 3, row, lane), NY)[1]


STEP = 4


def splat_body(route, target, zf, out):
    width = STEP * CAP * POINTS
    columns = iota((BX * BY, width), 0).astype(F32)
    levels = iota((NZ, width), 0).astype(F32)
    field = jnp.zeros((3 * BX * BY, NZ), F32)
    for first in range(0, GY, STEP):
        rows, column, level = places(route, first, STEP)
        here = columns == column
        weighted = [jnp.where(here, rows[j : j + 1], 0.0) for j in range(3)]
        weighted = jnp.concatenate(weighted, 0).astype(BF16)
        hot = jnp.where(levels == level, 1.0, 0.0).astype(BF16)
        field = field + mm(weighted, hot, 1, 1)
    both = jnp.concatenate([field, target[...].reshape(BX * BY, NZ)], 0)
    spread = mm3(table_of(zf), split(both), 1, 1)
    right = spread[:, 128:]
    right = jnp.where(iota((NZ, 128), 1) < 64, right * kz_of(NZ), right)
    out[...] = jnp.concatenate([spread[:, :128], right], 1).reshape(out.shape)


def forward_y_body(got, rows, lanes, twist, out):
    x = mm3(table_of(rows), split(got[...].reshape(NZ, NZ)))
    pairs = twisted(halves_of(x[:128], x[128:]), twist, 1)
    left, right = lanes_of(pairs, table_of(lanes), 1)
    low = iota((128, 128), 1) < 64
    oy = oy_of()
    for c in range(2):
        both = jnp.where(low, left[c], oy * left[c] + pltpu.roll(right[c], 64, 1))
        out[:, 8 * c : 8 * c + 8, :] = both.reshape(GX, 8, 128)
    target = jnp.where(low, pltpu.roll(right[0], 64, 1), right[1])
    out[:, 16:24, :] = target.reshape(GX, 8, 128)


def filters(gx, gy):
    shape = (128, 128)
    row, lane = iota(shape, 0), iota(shape, 1)
    kxb = row >> 3
    ux, ox = odd(kxb + GX * ((lane >> 3) & 7) - jnp.where(kxb > 8, GX, 0), NX)
    uy, _ = odd(ky_of(gx, row, lane), NY)
    kz = KZ * gy + (row & 3)
    uz = kz.astype(F32)
    gain = math.sqrt(float(NX * NY * NZ) * float(BX * BY * NZ) / (float(BLOCKS * POINTS) * 700.0))
    plane = ux * ux + uy * uy

    def base(ksq):
        return gain * jnp.exp(ksq * (-1.0 / (2.0 * WIDTH**2))) / jnp.maximum(ksq, 1.0)

    base0 = base(plane + uz * uz)
    base1 = jnp.where(kz == 0, base(plane + float(NZ // 2) ** 2), base0)
    return ox, (base0 + base1) * 0.5, (base0 - base1) * 0.5


def mirrored(pair, gx, mirror):
    row, other = iota((128, 128), 0), iota((128, 128), 1)
    swap = jnp.where(gx == 0, 0, 4)
    partner = (((16 - (row >> 3)) & 15) << 3) | ((row & 7) ^ swap)
    moves = jnp.where(other == partner, 1.0, 0.0).astype(BF16)
    high, low = split(jnp.concatenate(pair, 1))
    moved = mm(moves, high) + mm(moves, low)
    stacked = jnp.concatenate([moved[:, :128], moved[:, 128:]], 0)
    row = iota((256, 128), 0) & 127
    half_x = (row >> 3) == 8
    half_y = (((row >> 2) & 1) == 1) & (gx == 0)
    total = jnp.zeros((256, 128), F32)
    for case in range(4):
        here = (half_x == (case >= 2)) & (half_y == (case % 2 == 1))
        high, low = split(jnp.where(here, stacked, 0.0))
        table = mirror[case * 128 : (case + 1) * 128, :]
        total = total + mm(high, table) + mm(low, table)
    return total[:128], -total[128:]


def turned(pair):
    return -pair[1], pair[0]


def spectrum_body(place, got, rows, lanes, twist, mirror, out):
    gx, gy = place[0], place[1]
    target = got[:, 16:24, :].reshape(128, 128)
    target = jnp.concatenate(
        [target.reshape(GX, 8, 128), pltpu.roll(target, 64, 1).reshape(GX, 8, 128)], 1
    )
    x = jnp.concatenate([got[:, 0:16, :].reshape(NZ, 128), target.reshape(NZ, 128)], 1)
    x = mm3(table_of(rows), split(x))
    pairs = twisted(halves_of(x[:128], x[128:]), twist, 1)
    left, right = lanes_of(pairs, table_of(lanes), 1)
    ox, mean, diff = filters(gx, gy)
    low = iota((128, 128), 1) < 64
    swapped = lambda x: pltpu.roll(x, 64, 1)

    div = [jnp.where(low, ox * left[c], left[c]) for c in range(2)]
    div = turned([d + swapped(d) for d in div])
    target = [jnp.where(low, right[c], swapped(right[c])) for c in range(2)]
    other = mirrored([jnp.where(low, div[c], target[c]) for c in range(2)], gx, mirror)
    div2 = [jnp.where(low, other[c], swapped(other[c])) for c in range(2)]
    target2 = [jnp.where(low, swapped(other[c]), other[c]) for c in range(2)]
    chi = [-(mean * div[c] + diff * div2[c]) for c in range(2)]
    chi2 = [-(mean * div2[c] + diff * div[c]) for c in range(2)]
    h = [
        0.25 * (mean * (chi[c] - target[c]) + diff * (chi2[c] - target2[c])) for c in range(2)
    ]
    h = turned(h)
    slope = turned([twist[2] * chi[c] for c in range(2)])
    pairs = [
        tuple(jnp.where(low, chi[c], slope[c]) for c in range(2)),
        tuple(jnp.where(low, ox * h[c], h[c]) for c in range(2)),
    ]
    pairs = twisted(lanes_of(pairs, table_of(lanes), -1), twist, -1)
    both = jnp.concatenate(whole_of(pairs), 0)
    out[...] = mm3(table_of(rows), split(both), 0, 0).reshape(out.shape)


def inverse_y_body(got, rows, lanes, twist, out):
    real = got[:, 0:8, :].reshape(128, NZ)
    imag = got[:, 8:16, :].reshape(128, NZ)
    left, right = halves_of(real, imag)
    low = iota((128, 128), 1) < 64
    oy = oy_of()
    slope = turned([twist[2] * left[c] for c in range(2)])
    third = tuple(jnp.where(low, slope[c], oy * right[c]) for c in range(2))
    pairs = lanes_of([left, right, third], table_of(lanes), -1)
    pairs = twisted(pairs, twist, -1)
    both = jnp.concatenate(whole_of(pairs), 0)
    out[...] = mm3(table_of(rows), split(both), 0, 0).reshape(out.shape)


def pick_body(got, zb, route, chi, slope, picked):
    fields = got[...].reshape(NZ, 384)
    middle = fields[:, 128:256]
    middle = jnp.where(iota((NZ, 128), 1) < 64, middle, middle * kz_of(NZ))
    fields = jnp.concatenate([fields[:, :128], middle, fields[:, 256:]], 1)
    values = mm3(split(fields), table_of(zb), 0, 0)
    cells = BX * BY
    solid, slope_x, grad_x, grad_z, slope_y, grad_y = (
        values[i * cells : (i + 1) * cells] for i in range(6)
    )
    brick = (BX, BY, NZ)
    chi[...] = solid.reshape(brick)
    slope[0] = slope_x.reshape(brick)
    slope[1] = slope_y.reshape(brick)
    slope_z = (pltpu.roll(solid, NZ - 1, 1) - pltpu.roll(solid, 1, 1)) * 0.5
    slope[2] = slope_z.reshape(brick)
    high, low = split(jnp.concatenate([grad_x, grad_y, grad_z], 0))
    width = STEP * CAP * POINTS
    columns = iota((cells, width), 0).astype(F32)
    levels = iota((NZ, width), 0).astype(F32)
    for first in range(0, GY, STEP):
        _, column, level = places(route, first, STEP)
        hot = jnp.where(levels == level, 1.0, 0.0).astype(BF16)
        at_level = mm(high, hot) + mm(low, hot)
        here = columns == column
        lines = [
            jnp.sum(jnp.where(here, at_level[j * cells : (j + 1) * cells], 0.0), 0, keepdims=True)
            for j in range(3)
        ]
        lines = jnp.concatenate(lines + [jnp.zeros((1, width), F32)], 0)
        for s in range(STEP):
            picked[first + s] = lines[:, s * 128 : (s + 1) * 128]


def route_body(owners, normals, cells, out, count):
    row = iota((4, 128), 0)
    half = iota((4, 128), 1) >> 6
    empty = jnp.where(row == 3, -1.0, 0.0)
    parts = [normals[j].astype(F32) for j in range(3)] + [cells[...].astype(F32)]
    for o in range(GY):
        out[o] = empty
        count[o] = 0
    for b in range(BLOCKS):
        owner = owners[b]
        rank = count[owner]
        count[owner] = rank + 1
        value = jnp.concatenate([p[b : b + 1] for p in parts], 0)
        value = jnp.concatenate([value, value], 1)
        out[owner] = jnp.where(half == rank, value, out[owner])


def return_body(owners, got, out, count):
    for o in range(GY):
        count[o] = 0
    for b in range(BLOCKS):
        owner = owners[b]
        rank = count[owner]
        count[owner] = rank + 1
        value = got[owner]
        value = jnp.where(rank == 0, value[:, :64], value[:, 64:])
        for j in range(3):
            out[j, b : b + 1, :] = value[j : j + 1]


VMEM = pl.BlockSpec(memory_space=pltpu.VMEM)
SMEM = pl.BlockSpec(memory_space=pltpu.SMEM)


def call(body, name, outs, *operands, scalars=0, scratch=()):
    shapes = [jax.ShapeDtypeStruct(s, F32) for s in outs]
    single = len(shapes) == 1
    return pl.pallas_call(
        body,
        name=name,
        out_shape=shapes[0] if single else shapes,
        in_specs=[SMEM] * scalars + [VMEM] * (len(operands) - scalars),
        out_specs=VMEM if single else [VMEM] * len(shapes),
        scratch_shapes=list(scratch),
        compiler_params=pltpu.CompilerParams(vmem_limit_bytes=40 * 1024 * 1024),
    )(*operands)


def swap(x, axis):
    return lax.all_to_all(x, axis, split_axis=0, concat_axis=0, tiled=True)


def local(normals, owners, cells, target):
    table = {k: jnp.asarray(v) for k, v in TABLES.items()}
    owner = owners.reshape(BLOCKS)
    counts = (pltpu.SMEM((GY,), jnp.int32),)
    place = jnp.stack([lax.axis_index("gx"), lax.axis_index("gy")]).astype(jnp.int32)

    message = (GY, 4, CAP * POINTS)
    by_part = jnp.moveaxis(normals, 1, 0)
    sent = call(route_body, "route", [message], owner, by_part, cells, scalars=1, scratch=counts)
    route = swap(sent, "gy")
    spread = call(splat_body, "splat", [(GY, 8, 256)], route, target, table["zf"])
    got = swap(spread, "gy")
    y_args = (table["y_rows"], table["y_lanes"], table["ty"])
    spread = call(forward_y_body, "forward_y", [(GX, 24, 128)], got, *y_args)
    got = swap(spread, "gx")
    x_args = (table["x_rows"], table["x_lanes"], table["tx"], table["mirror"])
    spread = call(spectrum_body, "spectrum", [(GX, 16, 256)], place, got, *x_args, scalars=1)
    got = swap(spread, "gx")
    spread = call(inverse_y_body, "inverse_y", [(GY, 8, 384)], got, *y_args)
    got = swap(spread, "gy")
    brick = (BX, BY, NZ)
    chi, slope, picked = call(
        pick_body, "pick", [brick, (3,) + brick, message], got, table["zb"], route
    )
    returned = swap(picked, "gy")
    normal_grad = call(
        return_body, "deliver", [(3, BLOCKS, POINTS)], owner, returned, scalars=1, scratch=counts
    )
    return chi, slope, jnp.moveaxis(normal_grad, 0, 1)


def solution(mesh):
    placed = (
        P(("gx", "gy"), None, None),
        P(("gx", "gy"), None),
        P(("gx", "gy"), None),
        P("gx", "gy", None),
    )
    return jax.shard_map(
        local,
        mesh=mesh,
        in_specs=placed,
        out_specs=(P("gx", "gy", None), P(None, "gx", "gy", None), P(("gx", "gy"), None, None)),
        check_vma=False,
    )
```

```python
import math

import jax
import jax.numpy as jnp
import ml_dtypes
import numpy as np
from jax import lax
from jax.experimental import pallas as pl
from jax.experimental.pallas import tpu as pltpu
from jax.sharding import PartitionSpec as P

GX, GY = 16, 32
BX, BY, NZ = 8, 8, 256
NX, NY = GX * BX, GY * BY
KZ = NZ // 2 // GY
KB = NY // BY // GX
BLOCKS, POINTS, CAP = 32, 64, 2
WIDTH = 64.0
F32, BF16 = jnp.float32, jnp.bfloat16


def halves(table):
    high = table.astype(ml_dtypes.bfloat16)
    low = (table - high.astype(np.float64)).astype(ml_dtypes.bfloat16)
    return np.stack([high, low])


def unit(turns):
    return np.exp(-2j * np.pi * turns)


def parts_of(w):
    return np.stack([np.stack([w.real, -w.imag]), np.stack([w.imag, w.real])])


Y_CLASS = np.array([[h, -h if h else 16] for h in range(GX)])
X_CLASS = np.array([k if k <= 8 else k - 16 for k in range(16)])


def make_tables():
    z = np.arange(NZ)
    kz = np.arange(NZ // 2)
    w = unit((kz[:, None] * z[None, :] % NZ) / NZ)
    zf = np.stack([w.real, w.imag])
    zf[1, 0] = np.where(z % 2 == 0, 1.0, -1.0)
    zb = 2.0 * zf
    zb[:, 0] = zf[:, 0]
    zb = zb / (NX * NY * NZ)
    order = lambda t: t.reshape(2, GY, KZ, NZ).transpose(1, 0, 2, 3).reshape(NZ, NZ)
    g = np.arange(GY)
    wy = parts_of(unit(Y_CLASS.reshape(-1)[:, None] * g[None, :] / GY))
    y_rows = np.einsum("abkg,zw->akzgbw", wy, np.eye(KZ)).reshape(NZ, NZ)
    g = np.arange(GX)
    wx = parts_of(unit(X_CLASS[:, None] * g[None, :] / GX))
    x_rows = np.einsum("abkg,zw->akzgbw", wx, np.eye(KB * KZ)).reshape(NZ, NZ)
    e = np.arange(8)
    w8 = unit((e[:, None] * e[None, :] % 8) / 8)
    y_lanes = np.concatenate([np.kron(np.eye(16), w8.real), np.kron(np.eye(16), w8.imag)], 1)
    x8 = lambda t: np.kron(np.eye(2), np.kron(t, np.eye(8)))
    x_lanes = np.concatenate([x8(w8.real), x8(w8.imag)], 1)
    ty = unit(np.repeat(Y_CLASS.reshape(-1), KZ)[:, None] * np.tile(e, 16)[None, :] / NY)
    tx = unit(
        np.repeat(X_CLASS, KB * KZ)[:, None] * np.tile(np.repeat(e, 8), 2)[None, :] / NX
    )
    ky = np.repeat(Y_CLASS.reshape(-1), KZ)[:, None] + GY * e[None, :]
    slope_y = np.tile(np.sin(2 * np.pi * (ky % NY) / NY), (1, 16))
    kx = np.repeat(X_CLASS, KB * KZ)[:, None] + GX * np.repeat(e, 8)[None, :]
    slope_x = np.tile(np.sin(2 * np.pi * (kx % NX) / NX), (1, 2))
    twist = lambda t, s: np.stack([t.real, -t.imag, s]).astype(np.float32)
    mirror = np.zeros((2, 2, 128, 128), np.float32)
    for m in range(2):
        for n in range(2):
            for f in range(2):
                for a in range(8):
                    for b in range(8):
                        src = f * 64 + (-a - m) % 8 * 8 + (-b - n) % 8
                        mirror[m, n, src, f * 64 + a * 8 + b] = 1.0
    return dict(
        zf=halves(order(zf)),
        zb=halves(order(zb)),
        y_rows=halves(y_rows),
        x_rows=halves(x_rows),
        y_lanes=halves(y_lanes),
        x_lanes=halves(x_lanes),
        ty=twist(ty, slope_y),
        tx=twist(tx, slope_x),
        mirror=mirror.reshape(512, 128).astype(ml_dtypes.bfloat16),
    )


TABLES = make_tables()


def split(x):
    high = x.astype(BF16)
    return high, (x - high.astype(F32)).astype(BF16)


def mm(a, b, ca=1, cb=0):
    return lax.dot_general(a, b, (((ca,), (cb,)), ((), ())), preferred_element_type=F32)


def mm3(a, b, ca=1, cb=0):
    return mm(a[0], b[0], ca, cb) + (mm(a[0], b[1], ca, cb) + mm(a[1], b[0], ca, cb))


def lanes_of(pairs, table, sign):
    count, rows = len(pairs), pairs[0][0].shape[0]
    stacked = jnp.concatenate([p[0] for p in pairs] + [p[1] for p in pairs], 0)
    out = mm3(split(stacked), table)
    result = []
    for i in range(count):
        a = out[i * rows : (i + 1) * rows]
        b = out[(count + i) * rows : (count + i + 1) * rows]
        if sign > 0:
            result.append((a[:, :128] - b[:, 128:], a[:, 128:] + b[:, :128]))
        else:
            result.append((a[:, :128] + b[:, 128:], b[:, :128] - a[:, 128:]))
    return result


def twisted(pairs, twist, sign):
    c, s = twist[0], twist[1]
    if sign > 0:
        return [(a * c + b * s, b * c - a * s) for a, b in pairs]
    return [(a * c - b * s, b * c + a * s) for a, b in pairs]


def halves_of(real, imag):
    return [(real[:, i * 128 : (i + 1) * 128], imag[:, i * 128 : (i + 1) * 128]) for i in range(2)]


def whole_of(pairs):
    return tuple(jnp.concatenate([p[c] for p in pairs], 1) for c in range(2))


def table_of(ref):
    return ref[0], ref[1]


def iota(shape, dim):
    return lax.broadcasted_iota(jnp.int32, shape, dim)


def places(route, first, count):
    rows = jnp.concatenate([route[s] for s in range(first, first + count)], 1)
    cell = rows[3:4]
    column = jnp.floor(cell * (1.0 / NZ))
    return rows, column, cell - column * NZ


def kz_of(rows):
    row = iota((rows, 128), 0)
    return (KZ * (row >> 3) + (row & 3)).astype(F32)


def odd(k, length):
    k = k & (length - 1)
    u = jnp.where(k < length // 2, k, k - length).astype(F32)
    return u, jnp.where(k == length // 2, 0.0, u)


def ky_of(gx, row, lane):
    second = ((row >> 2) & 1) == 1
    kb = jnp.where(second, jnp.where(gx == 0, 16, -gx), gx)
    return kb + GY * (lane & 7)


def oy_of():
    row, lane = iota((128, 128), 0), iota((128, 128), 1)
    return odd(ky_of(row >> 3, row, lane), NY)[1]


STEP = 4


def splat_body(route, target, zf, out):
    width = STEP * CAP * POINTS
    columns = iota((BX * BY, width), 0).astype(F32)
    levels = iota((NZ, width), 0).astype(F32)
    field = jnp.zeros((3 * BX * BY, NZ), F32)
    for first in range(0, GY, STEP):
        rows, column, level = places(route, first, STEP)
        here = columns == column
        weighted = [jnp.where(here, rows[j : j + 1], 0.0) for j in range(3)]
        weighted = jnp.concatenate(weighted, 0).astype(BF16)
        hot = jnp.where(levels == level, 1.0, 0.0).astype(BF16)
        field = field + mm(weighted, hot, 1, 1)
    both = jnp.concatenate([field, target[...].reshape(BX * BY, NZ)], 0)
    spread = mm3(table_of(zf), split(both), 1, 1)
    right = spread[:, 128:]
    right = jnp.where(iota((NZ, 128), 1) < 64, right * kz_of(NZ), right)
    out[...] = jnp.concatenate([spread[:, :128], right], 1).reshape(out.shape)


def forward_y_body(got, rows, lanes, twist, out):
    x = mm3(table_of(rows), split(got[...].reshape(NZ, NZ)))
    pairs = twisted(halves_of(x[:128], x[128:]), twist, 1)
    left, right = lanes_of(pairs, table_of(lanes), 1)
    low = iota((128, 128), 1) < 64
    oy = oy_of()
    for c in range(2):
        both = jnp.where(low, left[c], oy * left[c] + pltpu.roll(right[c], 64, 1))
        out[:, 8 * c : 8 * c + 8, :] = both.reshape(GX, 8, 128)
    target = jnp.where(low, pltpu.roll(right[0], 64, 1), right[1])
    out[:, 16:24, :] = target.reshape(GX, 8, 128)


def filters(gx, gy):
    shape = (128, 128)
    row, lane = iota(shape, 0), iota(shape, 1)
    kxb = row >> 3
    ux, ox = odd(kxb + GX * ((lane >> 3) & 7) - jnp.where(kxb > 8, GX, 0), NX)
    uy, _ = odd(ky_of(gx, row, lane), NY)
    kz = KZ * gy + (row & 3)
    uz = kz.astype(F32)
    gain = math.sqrt(float(NX * NY * NZ) * float(BX * BY * NZ) / (float(BLOCKS * POINTS) * 700.0))
    plane = ux * ux + uy * uy

    def base(ksq):
        value = gain * jnp.exp(ksq * (-1.0 / (2.0 * WIDTH**2))) / jnp.maximum(ksq, 1.0)
        return jnp.where(ksq == 0.0, 0.0, value)

    base0 = base(plane + uz * uz)
    base1 = jnp.where(kz == 0, base(plane + float(NZ // 2) ** 2), base0)
    return ox, (base0 + base1) * 0.5, (base0 - base1) * 0.5


def mirrored(pair, gx, mirror):
    row, other = iota((32, 128), 0), iota((32, 128), 1)
    swap = jnp.where(gx == 0, 0, 4)
    partner = (((16 - (row >> 1)) & 15) << 3) | (((row & 1) << 2) ^ swap)
    moves = jnp.where(other == partner, 1.0, 0.0).astype(BF16)
    high, low = split(jnp.concatenate(pair, 1))
    moved = mm(moves, high) + mm(moves, low)
    moved = jnp.concatenate([moved[:, :128], moved[:, 128:]], 0)
    row = iota((64, 128), 0) & 31
    half_x = (row >> 1) == 8
    half_y = ((row & 1) == 1) & (gx == 0)
    cases = [
        jnp.where((half_x == (case >= 2)) & (half_y == (case % 2 == 1)), moved, 0.0)
        for case in range(4)
    ]
    high, low = split(jnp.concatenate(cases, 1))
    turned_back = mm(high, mirror[...]) + mm(low, mirror[...])
    high, low = split(jnp.concatenate([turned_back[:32], -turned_back[32:]], 1))
    row, other = iota((128, 32), 0), iota((128, 32), 1)
    home = jnp.where(row == other * 4, 1.0, 0.0).astype(BF16)
    total = mm(home, high) + mm(home, low)
    return total[:, :128], total[:, 128:]


def turned(pair):
    return -pair[1], pair[0]


def spectrum_body(got, rows, lanes, twist, mirror, out):
    gx, gy = lax.axis_index("gx"), lax.axis_index("gy")
    target = got[:, 16:24, :].reshape(128, 128)
    target = jnp.concatenate(
        [target.reshape(GX, 8, 128), pltpu.roll(target, 64, 1).reshape(GX, 8, 128)], 1
    )
    x = jnp.concatenate([got[:, 0:16, :].reshape(NZ, 128), target.reshape(NZ, 128)], 1)
    x = mm3(table_of(rows), split(x))
    pairs = twisted(halves_of(x[:128], x[128:]), twist, 1)
    left, right = lanes_of(pairs, table_of(lanes), 1)
    ox, mean, diff = filters(gx, gy)
    low = iota((128, 128), 1) < 64
    swapped = lambda x: pltpu.roll(x, 64, 1)

    div = [jnp.where(low, ox * left[c], left[c]) for c in range(2)]
    div = turned([d + swapped(d) for d in div])
    target = [jnp.where(low, right[c], swapped(right[c])) for c in range(2)]
    other = mirrored([jnp.where(low, div[c], target[c]) for c in range(2)], gx, mirror)
    div2 = [jnp.where(low, other[c], swapped(other[c])) for c in range(2)]
    target2 = [jnp.where(low, swapped(other[c]), other[c]) for c in range(2)]
    chi = [-(mean * div[c] + diff * div2[c]) for c in range(2)]
    chi2 = [-(mean * div2[c] + diff * div[c]) for c in range(2)]
    h = [
        0.25 * (mean * (chi[c] - target[c]) + diff * (chi2[c] - target2[c])) for c in range(2)
    ]
    h = turned(h)
    slope = turned([twist[2] * chi[c] for c in range(2)])
    pairs = [
        tuple(jnp.where(low, chi[c], slope[c]) for c in range(2)),
        tuple(jnp.where(low, ox * h[c], h[c]) for c in range(2)),
    ]
    pairs = twisted(lanes_of(pairs, table_of(lanes), -1), twist, -1)
    both = jnp.concatenate(whole_of(pairs), 0)
    out[...] = mm3(table_of(rows), split(both), 0, 0).reshape(out.shape)


def inverse_y_body(got, rows, lanes, twist, out):
    real = got[:, 0:8, :].reshape(128, NZ)
    imag = got[:, 8:16, :].reshape(128, NZ)
    left, right = halves_of(real, imag)
    low = iota((128, 128), 1) < 64
    oy = oy_of()
    slope = turned([twist[2] * left[c] for c in range(2)])
    third = tuple(jnp.where(low, slope[c], oy * right[c]) for c in range(2))
    pairs = lanes_of([left, right, third], table_of(lanes), -1)
    pairs = twisted(pairs, twist, -1)
    both = jnp.concatenate(whole_of(pairs), 0)
    out[...] = mm3(table_of(rows), split(both), 0, 0).reshape(out.shape)


def pick_body(got, zb, route, chi, slope, picked):
    fields = got[...].reshape(NZ, 384)
    middle = fields[:, 128:256]
    middle = jnp.where(iota((NZ, 128), 1) < 64, middle, middle * kz_of(NZ))
    fields = jnp.concatenate([fields[:, :128], middle, fields[:, 256:]], 1)
    values = mm3(split(fields), table_of(zb), 0, 0)
    cells = BX * BY
    solid, slope_x, grad_x, grad_z, slope_y, grad_y = (
        values[i * cells : (i + 1) * cells] for i in range(6)
    )
    brick = (BX, BY, NZ)
    chi[...] = solid.reshape(brick)
    slope[0] = slope_x.reshape(brick)
    slope[1] = slope_y.reshape(brick)
    slope_z = (pltpu.roll(solid, NZ - 1, 1) - pltpu.roll(solid, 1, 1)) * 0.5
    slope[2] = slope_z.reshape(brick)
    high, low = split(jnp.concatenate([grad_x, grad_y, grad_z], 0))
    width = STEP * CAP * POINTS
    columns = iota((cells, width), 0).astype(F32)
    levels = iota((NZ, width), 0).astype(F32)
    for first in range(0, GY, STEP):
        _, column, level = places(route, first, STEP)
        hot = jnp.where(levels == level, 1.0, 0.0).astype(BF16)
        at_level = mm(high, hot) + mm(low, hot)
        here = columns == column
        lines = [
            jnp.sum(jnp.where(here, at_level[j * cells : (j + 1) * cells], 0.0), 0, keepdims=True)
            for j in range(3)
        ]
        lines = jnp.concatenate(lines + [jnp.zeros((1, width), F32)], 0)
        for s in range(STEP):
            picked[first + s] = lines[:, s * 128 : (s + 1) * 128]


def route_body(*refs):
    sources, (out, target, zf), (owners, normals, cells, count, sems) = refs[:5], refs[5:8], refs[8:]
    fetches = [
        pltpu.make_async_copy(source, place, sems.at[i])
        for i, (source, place) in enumerate(zip(sources, (owners, normals, cells, target, zf)))
    ]
    for fetch in fetches:
        fetch.start()
    row = iota((4, 128), 0)
    half = iota((4, 128), 1) >> 6
    empty = jnp.where(row == 3, -1.0, 0.0)
    for o in range(GY):
        out[o] = empty
        count[o] = 0
    for fetch in fetches[:3]:
        fetch.wait()
    parts = [normals[j].astype(F32) for j in range(3)] + [cells[...].astype(F32)]
    for b in range(BLOCKS):
        owner = owners[b]
        rank = count[owner]
        count[owner] = rank + 1
        value = jnp.concatenate([p[b : b + 1] for p in parts], 0)
        value = jnp.concatenate([value, value], 1)
        out[owner] = jnp.where(half == rank, value, out[owner])
    for fetch in fetches[3:]:
        fetch.wait()


def return_body(owners, got, out, count, rows):
    for o in range(GY):
        count[o] = 0
    for b in range(BLOCKS):
        owner = owners[b]
        rank = count[owner]
        count[owner] = rank + 1
        value = got[owner]
        rows[b] = jnp.where(rank == 0, value, pltpu.roll(value, 64, 1))
    for j in range(3):
        out[j] = rows[:, j, :][:, :64]


VMEM = pl.BlockSpec(memory_space=pltpu.VMEM)
SMEM = pl.BlockSpec(memory_space=pltpu.SMEM)
HBM = pl.BlockSpec(memory_space=pltpu.HBM)


def call(body, name, outs, *operands, specs=None, scratch=()):
    shapes = [s if hasattr(s, "dtype") else jax.ShapeDtypeStruct(s, F32) for s in outs]
    single = len(shapes) == 1
    return pl.pallas_call(
        body,
        name=name,
        out_shape=shapes[0] if single else shapes,
        in_specs=specs or [VMEM] * len(operands),
        out_specs=VMEM if single else [VMEM] * len(shapes),
        scratch_shapes=list(scratch),
        compiler_params=pltpu.CompilerParams(vmem_limit_bytes=40 * 1024 * 1024),
    )(*operands)


def kept(x):
    return pltpu.with_memory_space_constraint(x, pltpu.HBM)


def swap(x, axis):
    return lax.all_to_all(x, axis, split_axis=0, concat_axis=0, tiled=True)


def local(normals, owners, cells, target):
    table = {k: jnp.asarray(v) for k, v in TABLES.items()}
    owner = owners.reshape(BLOCKS)
    counts = pltpu.SMEM((GY,), jnp.int32)
    brick = (BX, BY, NZ)
    message = (GY, 4, CAP * POINTS)

    by_part = jnp.moveaxis(normals, 1, 0)
    scratch = (
        pltpu.SMEM(owner.shape, jnp.int32),
        pltpu.VMEM(by_part.shape, BF16),
        pltpu.VMEM(cells.shape, jnp.int32),
        counts,
        pltpu.SemaphoreType.DMA((5,)),
    )
    tables_z = jax.ShapeDtypeStruct(table["zf"].shape, BF16)
    sources = (owner, by_part, cells, target, table["zf"])
    sent, target_here, zf = call(
        route_body,
        "route",
        [message, brick, tables_z],
        *map(kept, sources),
        specs=[HBM] * 5,
        scratch=scratch,
    )
    route = swap(sent, "gy")
    spread = call(splat_body, "splat", [(GY, 8, 256)], route, target_here, zf)
    got = swap(spread, "gy")
    y_args = (table["y_rows"], table["y_lanes"], table["ty"])
    spread = call(forward_y_body, "forward_y", [(GX, 24, 128)], got, *y_args)
    got = swap(spread, "gx")
    x_args = (table["x_rows"], table["x_lanes"], table["tx"], table["mirror"])
    spread = call(spectrum_body, "spectrum", [(GX, 16, 256)], got, *x_args)
    got = swap(spread, "gx")
    spread = call(inverse_y_body, "inverse_y", [(GY, 8, 384)], got, *y_args)
    got = swap(spread, "gy")
    chi, slope, picked = call(
        pick_body, "pick", [brick, (3,) + brick, message], got, table["zb"], route
    )
    returned = swap(picked, "gy")
    normal_grad = call(
        return_body,
        "deliver",
        [(3, BLOCKS, POINTS)],
        owner,
        returned,
        specs=[SMEM, VMEM],
        scratch=(counts, pltpu.VMEM((BLOCKS, 4, CAP * POINTS), F32)),
    )
    return chi, slope, jnp.moveaxis(normal_grad, 0, 1)


def solution(mesh):
    placed = (
        P(("gx", "gy"), None, None),
        P(("gx", "gy"), None),
        P(("gx", "gy"), None),
        P("gx", "gy", None),
    )
    return jax.shard_map(
        local,
        mesh=mesh,
        in_specs=placed,
        out_specs=(P("gx", "gy", None), P(None, "gx", "gy", None), P(("gx", "gy"), None, None)),
        check_vma=False,
    )
```

```python
import math

import jax
import jax.numpy as jnp
import ml_dtypes
import numpy as np
from jax import lax
from jax.experimental import pallas as pl
from jax.experimental.pallas import tpu as pltpu
from jax.sharding import PartitionSpec as P

GX, GY = 16, 32
BX, BY, NZ = 8, 8, 256
NX, NY = GX * BX, GY * BY
KZ = NZ // 2 // GY
KB = NY // BY // GX
BLOCKS, POINTS, CAP = 32, 64, 2
WIDTH = 64.0
F32, BF16 = jnp.float32, jnp.bfloat16


def halves(table):
    high = table.astype(ml_dtypes.bfloat16)
    low = (table - high.astype(np.float64)).astype(ml_dtypes.bfloat16)
    return np.stack([high, low])


def unit(turns):
    return np.exp(-2j * np.pi * turns)


def parts_of(w):
    return np.stack([np.stack([w.real, -w.imag]), np.stack([w.imag, w.real])])


Y_CLASS = np.array([[h, -h if h else 16] for h in range(GX)])
X_CLASS = np.array([k if k <= 8 else k - 16 for k in range(16)])


def make_tables():
    z = np.arange(NZ)
    kz = np.arange(NZ // 2)
    w = unit((kz[:, None] * z[None, :] % NZ) / NZ)
    zf = np.stack([w.real, w.imag])
    zf[1, 0] = np.where(z % 2 == 0, 1.0, -1.0)
    zb = 2.0 * zf
    zb[:, 0] = zf[:, 0]
    zb = zb / (NX * NY * NZ)
    order = lambda t: t.reshape(2, GY, KZ, NZ).transpose(1, 0, 2, 3).reshape(NZ, NZ)
    g = np.arange(GY)
    wy = parts_of(unit(Y_CLASS.reshape(-1)[:, None] * g[None, :] / GY))
    y_rows = np.einsum("abkg,zw->akzgbw", wy, np.eye(KZ)).reshape(NZ, NZ)
    g = np.arange(GX)
    wx = parts_of(unit(X_CLASS[:, None] * g[None, :] / GX))
    x_rows = np.einsum("abkg,zw->akzgbw", wx, np.eye(KB * KZ)).reshape(NZ, NZ)
    e = np.arange(8)
    w8 = unit((e[:, None] * e[None, :] % 8) / 8)
    y_lanes = np.concatenate([np.kron(np.eye(16), w8.real), np.kron(np.eye(16), w8.imag)], 1)
    x8 = lambda t: np.kron(np.eye(2), np.kron(t, np.eye(8)))
    x_lanes = np.concatenate([x8(w8.real), x8(w8.imag)], 1)
    ty = unit(np.repeat(Y_CLASS.reshape(-1), KZ)[:, None] * np.tile(e, 16)[None, :] / NY)
    tx = unit(
        np.repeat(X_CLASS, KB * KZ)[:, None] * np.tile(np.repeat(e, 8), 2)[None, :] / NX
    )
    ky = np.repeat(Y_CLASS.reshape(-1), KZ)[:, None] + GY * e[None, :]
    slope_y = np.tile(np.sin(2 * np.pi * (ky % NY) / NY), (1, 16))
    kx = np.repeat(X_CLASS, KB * KZ)[:, None] + GX * np.repeat(e, 8)[None, :]
    slope_x = np.tile(np.sin(2 * np.pi * (kx % NX) / NX), (1, 2))
    twist = lambda t, s: np.stack([t.real, -t.imag, s]).astype(np.float32)
    mirror = np.zeros((2, 2, 128, 128), np.float32)
    for m in range(2):
        for n in range(2):
            for f in range(2):
                for a in range(8):
                    for b in range(8):
                        src = f * 64 + (-a - m) % 8 * 8 + (-b - n) % 8
                        mirror[m, n, src, f * 64 + a * 8 + b] = 1.0
    return dict(
        zf=halves(order(zf)),
        zb=halves(order(zb)),
        y_rows=halves(y_rows),
        x_rows=halves(x_rows),
        y_lanes=halves(y_lanes),
        x_lanes=halves(x_lanes),
        ty=twist(ty, slope_y),
        tx=twist(tx, slope_x)[:2],
        mirror=mirror.reshape(512, 128).astype(ml_dtypes.bfloat16),
    )


TABLES = make_tables()


def split(x):
    high = x.astype(BF16)
    return high, (x - high.astype(F32)).astype(BF16)


def mm(a, b, ca=1, cb=0):
    return lax.dot_general(a, b, (((ca,), (cb,)), ((), ())), preferred_element_type=F32)


def mm3(a, b, ca=1, cb=0):
    return mm(a[0], b[0], ca, cb) + (mm(a[0], b[1], ca, cb) + mm(a[1], b[0], ca, cb))


def lanes_of(pairs, table, sign):
    count, rows = len(pairs), pairs[0][0].shape[0]
    stacked = jnp.concatenate([p[0] for p in pairs] + [p[1] for p in pairs], 0)
    out = mm3(split(stacked), table)
    result = []
    for i in range(count):
        a = out[i * rows : (i + 1) * rows]
        b = out[(count + i) * rows : (count + i + 1) * rows]
        if sign > 0:
            result.append((a[:, :128] - b[:, 128:], a[:, 128:] + b[:, :128]))
        else:
            result.append((a[:, :128] + b[:, 128:], b[:, :128] - a[:, 128:]))
    return result


def twisted(pairs, twist, sign):
    c, s = twist[0], twist[1]
    if sign > 0:
        return [(a * c + b * s, b * c - a * s) for a, b in pairs]
    return [(a * c - b * s, b * c + a * s) for a, b in pairs]


def halves_of(real, imag):
    return [(real[:, i * 128 : (i + 1) * 128], imag[:, i * 128 : (i + 1) * 128]) for i in range(2)]


def whole_of(pairs):
    return tuple(jnp.concatenate([p[c] for p in pairs], 1) for c in range(2))


def table_of(ref):
    return ref[0], ref[1]


def iota(shape, dim):
    return lax.broadcasted_iota(jnp.int32, shape, dim)


def places(route, first, count):
    rows = jnp.concatenate([route[s] for s in range(first, first + count)], 1)
    cell = rows[3:4]
    column = jnp.floor(cell * (1.0 / NZ))
    return rows, column, cell - column * NZ


def kz_of(rows):
    row = iota((rows, 128), 0)
    return (KZ * (row >> 3) + (row & 3)).astype(F32)


def odd(k, length):
    k = k & (length - 1)
    u = jnp.where(k < length // 2, k, k - length).astype(F32)
    return u, jnp.where(k == length // 2, 0.0, u)


def ky_of(gx, row, lane):
    second = ((row >> 2) & 1) == 1
    kb = jnp.where(second, jnp.where(gx == 0, 16, -gx), gx)
    return kb + GY * (lane & 7)


def oy_of():
    row, lane = iota((128, 128), 0), iota((128, 128), 1)
    return odd(ky_of(row >> 3, row, lane), NY)[1]


STEP = 4


def splat_body(route, target, zf, out):
    width = STEP * CAP * POINTS
    columns = iota((BX * BY, width), 0).astype(F32)
    levels = iota((NZ, width), 0).astype(F32)
    field = jnp.zeros((3 * BX * BY, NZ), F32)
    for first in range(0, GY, STEP):
        rows, column, level = places(route, first, STEP)
        here = columns == column
        weighted = [jnp.where(here, rows[j : j + 1], 0.0) for j in range(3)]
        weighted = jnp.concatenate(weighted, 0).astype(BF16)
        hot = jnp.where(levels == level, 1.0, 0.0).astype(BF16)
        field = field + mm(weighted, hot, 1, 1)
    both = jnp.concatenate([field, target[...].reshape(BX * BY, NZ)], 0)
    spread = mm3(table_of(zf), split(both), 1, 1)
    right = spread[:, 128:]
    right = jnp.where(iota((NZ, 128), 1) < 64, right * kz_of(NZ), right)
    out[...] = jnp.concatenate([spread[:, :128], right], 1).reshape(out.shape)


def swapped(x):
    return pltpu.roll(x, 64, 1)


def low_half(rows=128):
    return iota((rows, 128), 1) < 64


def packed_of(real, imag):
    low = low_half()
    return jnp.where(low, real, swapped(imag)), jnp.where(low, swapped(real), imag)


def weight_of(gx, gy):
    row, lane = iota((128, 128), 0), iota((128, 128), 1)
    gx = row >> 3 if gx is None else gx
    uy, _ = odd(ky_of(gx, row, lane), NY)
    uz = (KZ * gy + (row & 3)).astype(F32)
    return jnp.sqrt(uy * uy + uz * uz + 1.0)


BITS, SPLIT, BIAS, EDGE_BITS = 20, 11, 128, 30
ROWS = 18


def scale_of(exponent, bits):
    return jnp.exp2((bits - exponent).astype(F32))


def exponent_of(x):
    top = jnp.max(jnp.abs(x), 1, keepdims=True)
    power = jnp.floor(jnp.log2(jnp.maximum(top, 1e-26)) + 0.001) + 1.0
    return power.astype(jnp.int32)


def fixed(x, exponent, bits):
    return jnp.floor(x * scale_of(exponent, bits) + 0.5).astype(jnp.int32)


def encode(fields, exponents):
    a, b, c = (fixed(x, e, BITS) for x, e in zip(fields, exponents))
    e = [x + BIAS for x in exponents]
    mark = e[0] | (e[1] << 8) | (e[2] << 16)
    lane = iota((128, 128), 1)
    bit = jnp.where(lane < 24, (mark >> (lane & 31)) & 1, 0)
    first = (a << SPLIT) | (c & 0x7FF)
    second = (b << SPLIT) | ((c >> SPLIT) & 0x3FF) | (bit << 10)
    return first, second


def decode(first, second):
    lane = iota((128, 128), 1)
    bit = ((second >> 10) & 1) << (lane & 7)
    exponents = []
    for i in range(3):
        here = jnp.where((lane >> 3) == i, bit, 0).astype(F32)
        exponents.append(jnp.sum(here, 1, keepdims=True).astype(jnp.int32) - BIAS)
    a, b = first >> SPLIT, second >> SPLIT
    c = (((second & 0x3FF) << 22) >> SPLIT) | (first & 0x7FF)
    fields = [x.astype(F32) / scale_of(e, BITS) for x, e in zip((a, b, c), exponents)]
    return fields, exponents


def forward_y_body(got, rows, lanes, twist, out):
    x = mm3(table_of(rows), split(got[...].reshape(NZ, NZ)))
    pairs = twisted(halves_of(x[:128], x[128:]), twist, 1)
    left, right = lanes_of(pairs, table_of(lanes), 1)
    low = low_half()
    oy = oy_of()
    real, imag = (jnp.where(low, left[c], oy * left[c] + swapped(right[c])) for c in range(2))
    target = jnp.where(low, swapped(right[0]), right[1])
    part_x, part_yz = packed_of(real, imag)
    fields = (part_x, part_yz / weight_of(None, lax.axis_index("gy")), target)
    first, second = encode(fields, [exponent_of(x) for x in fields])
    out[:, 0:8, :] = first.reshape(GX, 8, 128)
    out[:, 8:16, :] = second.reshape(GX, 8, 128)


def filters(gx, gy):
    shape = (128, 128)
    row, lane = iota(shape, 0), iota(shape, 1)
    kxb = row >> 3
    ux, ox = odd(kxb + GX * ((lane >> 3) & 7) - jnp.where(kxb > 8, GX, 0), NX)
    uy, _ = odd(ky_of(gx, row, lane), NY)
    kz = KZ * gy + (row & 3)
    uz = kz.astype(F32)
    gain = math.sqrt(float(NX * NY * NZ) * float(BX * BY * NZ) / (float(BLOCKS * POINTS) * 700.0))
    plane = ux * ux + uy * uy

    def base(ksq):
        value = gain * jnp.exp(ksq * (-1.0 / (2.0 * WIDTH**2))) / jnp.maximum(ksq, 1.0)
        return jnp.where(ksq == 0.0, 0.0, value)

    base0 = base(plane + uz * uz)
    base1 = jnp.where(kz == 0, base(plane + float(NZ // 2) ** 2), base0)
    return ox, (base0 + base1) * 0.5, (base0 - base1) * 0.5


def mirrored(pair, gx, mirror):
    row, other = iota((32, 128), 0), iota((32, 128), 1)
    swap = jnp.where(gx == 0, 0, 4)
    partner = (((16 - (row >> 1)) & 15) << 3) | (((row & 1) << 2) ^ swap)
    moves = jnp.where(other == partner, 1.0, 0.0).astype(BF16)
    high, low = split(jnp.concatenate(pair, 1))
    moved = mm(moves, high) + mm(moves, low)
    moved = jnp.concatenate([moved[:, :128], moved[:, 128:]], 0)
    row = iota((64, 128), 0) & 31
    half_x = (row >> 1) == 8
    half_y = ((row & 1) == 1) & (gx == 0)
    cases = [
        jnp.where((half_x == (case >= 2)) & (half_y == (case % 2 == 1)), moved, 0.0)
        for case in range(4)
    ]
    high, low = split(jnp.concatenate(cases, 1))
    turned_back = mm(high, mirror[...]) + mm(low, mirror[...])
    high, low = split(jnp.concatenate([turned_back[:32], -turned_back[32:]], 1))
    row, other = iota((128, 32), 0), iota((128, 32), 1)
    home = jnp.where(row == other * 4, 1.0, 0.0).astype(BF16)
    total = mm(home, high) + mm(home, low)
    return total[:, :128], total[:, 128:]


def turned(pair):
    return -pair[1], pair[0]


def spectrum_body(got, rows, lanes, twist, mirror, out, edges):
    gx, gy = lax.axis_index("gx"), lax.axis_index("gy")
    words = (got[:, i * 8 : i * 8 + 8, :].reshape(128, 128) for i in range(2))
    (part_x, part_yz, target), _ = decode(*words)
    part_yz = part_yz * weight_of(gx, gy)
    x = [*packed_of(part_x, part_yz), target, swapped(target)]
    x = [part.reshape(GX, 8, 128) for part in x]
    x = [jnp.concatenate(x[i : i + 2], 1).reshape(NZ, 128) for i in (0, 2)]
    x = jnp.concatenate(x, 1)
    x = mm3(table_of(rows), split(x))
    pairs = twisted(halves_of(x[:128], x[128:]), twist, 1)
    left, right = lanes_of(pairs, table_of(lanes), 1)
    ox, mean, diff = filters(gx, gy)
    low = low_half()

    div = [jnp.where(low, ox * left[c], left[c]) for c in range(2)]
    div = turned([d + swapped(d) for d in div])
    target = [jnp.where(low, right[c], swapped(right[c])) for c in range(2)]
    other = mirrored([jnp.where(low, div[c], target[c]) for c in range(2)], gx, mirror)
    div2 = [jnp.where(low, other[c], swapped(other[c])) for c in range(2)]
    target2 = [jnp.where(low, swapped(other[c]), other[c]) for c in range(2)]
    chi = [-(mean * div[c] + diff * div2[c]) for c in range(2)]
    chi2 = [-(mean * div2[c] + diff * div[c]) for c in range(2)]
    h = [
        0.25 * (mean * (chi[c] - target[c]) + diff * (chi2[c] - target2[c])) for c in range(2)
    ]
    h = turned(h)
    pairs = [chi, tuple(jnp.where(low, ox * h[c], h[c]) for c in range(2))]
    pairs = twisted(lanes_of(pairs, table_of(lanes), -1), twist, -1)
    both = jnp.concatenate(whole_of(pairs), 0)
    x = mm3(table_of(rows), split(both), 0, 0).reshape(GX, 16, NZ)
    chi, _ = packed_of(*(x[:, c : c + 8, :128].reshape(128, 128) for c in (0, 8)))
    gradients = packed_of(*(x[:, c : c + 8, 128:].reshape(128, 128) for c in (0, 8)))

    below = jnp.concatenate([chi[120:], chi[:120]], 0)
    above = jnp.concatenate([chi[8:], chi[:8]], 0)
    lane = iota((128, 128), 1) >> 3
    edge = jnp.where(lane == 0, pltpu.roll(below, 72, 1), 0.0)
    edge = jnp.where(lane == 1, pltpu.roll(above, 8, 1), edge)
    edge = jnp.where(lane == 2, pltpu.roll(below, 24, 1), edge)
    edge = jnp.where(lane == 3, pltpu.roll(above, 88, 1), edge)
    grad_x, h = gradients
    fields = (chi, grad_x, h * weight_of(gx, gy))
    exponents = [exponent_of(x) for x in fields]
    exponents[0] = jnp.maximum(exponents[0], exponent_of(edge))
    first, second = encode(fields, exponents)
    edges[...] = fixed(edge, exponents[0], EDGE_BITS)
    folded = edges[pl.ds(0, 32, stride=4), :]
    for i in range(1, 4):
        piece = pltpu.roll(edges[pl.ds(i, 32, stride=4), :], 32 * i, 1)
        folded = jnp.where((iota((32, 128), 1) >> 5) == i, piece, folded)
    for g in range(GX):
        at = g * ROWS
        out[at : at + 8, :] = first[g * 8 : g * 8 + 8]
        out[at + 8 : at + 16, :] = second[g * 8 : g * 8 + 8]
        out[at + 16 : at + 18, :] = folded[g * 2 : g * 2 + 2]


def inverse_y_body(got, rows, lanes, twist, out, edges):
    pick = lambda at, count: [got[g * ROWS + at : g * ROWS + at + count, :] for g in range(GX)]
    first, second = (jnp.concatenate(pick(at, 8), 0) for at in (0, 8))
    folded = jnp.concatenate(pick(16, 2), 0)
    (chi, grad_x, h), exponents = decode(first, second)
    h = h / weight_of(None, lax.axis_index("gy"))
    edges[pl.ds(0, 32, stride=4), :] = folded
    for i in range(1, 4):
        edges[pl.ds(i, 32, stride=4), :] = pltpu.roll(folded, 128 - 32 * i, 1)
    edge = edges[...].astype(F32) / scale_of(exponents[0], EDGE_BITS)
    lane = iota((128, 128), 1) >> 3
    edge48, edge96 = pltpu.roll(edge, 48, 1), pltpu.roll(edge, 96, 1)
    after = jnp.where(lane == 7, edge48, pltpu.roll(chi, 120, 1))
    after = jnp.where(lane == 15, edge96, after)
    before = jnp.where(lane == 0, edge, pltpu.roll(chi, 8, 1))
    before = jnp.where(lane == 8, edge48, before)
    left, right = packed_of(chi, (after - before) * 0.5), packed_of(grad_x, h)
    low = low_half()
    oy = oy_of()
    slope = turned([twist[2] * left[c] for c in range(2)])
    third = tuple(jnp.where(low, slope[c], oy * right[c]) for c in range(2))
    pairs = lanes_of([left, right, third], table_of(lanes), -1)
    pairs = twisted(pairs, twist, -1)
    both = jnp.concatenate(whole_of(pairs), 0)
    out[...] = mm3(table_of(rows), split(both), 0, 0).reshape(out.shape)


def pick_body(got, zb, route, chi, slope, picked):
    fields = got[...].reshape(NZ, 384)
    middle = fields[:, 128:256]
    middle = jnp.where(iota((NZ, 128), 1) < 64, middle, middle * kz_of(NZ))
    fields = jnp.concatenate([fields[:, :128], middle, fields[:, 256:]], 1)
    values = mm3(split(fields), table_of(zb), 0, 0)
    cells = BX * BY
    solid, slope_x, grad_x, grad_z, slope_y, grad_y = (
        values[i * cells : (i + 1) * cells] for i in range(6)
    )
    brick = (BX, BY, NZ)
    chi[...] = solid.reshape(brick)
    slope[0] = slope_x.reshape(brick)
    slope[1] = slope_y.reshape(brick)
    slope_z = (pltpu.roll(solid, NZ - 1, 1) - pltpu.roll(solid, 1, 1)) * 0.5
    slope[2] = slope_z.reshape(brick)
    high, low = split(jnp.concatenate([grad_x, grad_y, grad_z], 0))
    width = STEP * CAP * POINTS
    columns = iota((cells, width), 0).astype(F32)
    levels = iota((NZ, width), 0).astype(F32)
    for first in range(0, GY, STEP):
        _, column, level = places(route, first, STEP)
        hot = jnp.where(levels == level, 1.0, 0.0).astype(BF16)
        at_level = mm(high, hot) + mm(low, hot)
        here = columns == column
        lines = [
            jnp.sum(jnp.where(here, at_level[j * cells : (j + 1) * cells], 0.0), 0, keepdims=True)
            for j in range(3)
        ]
        lines = jnp.concatenate(lines + [jnp.zeros((1, width), F32)], 0)
        for s in range(STEP):
            picked[first + s] = lines[:, s * 128 : (s + 1) * 128]


def route_body(*refs):
    sources, (out, target, zf), (owners, normals, cells, count, sems) = refs[:5], refs[5:8], refs[8:]
    fetches = [
        pltpu.make_async_copy(source, place, sems.at[i])
        for i, (source, place) in enumerate(zip(sources, (owners, normals, cells, target, zf)))
    ]
    for fetch in fetches:
        fetch.start()
    row = iota((4, 128), 0)
    half = iota((4, 128), 1) >> 6
    empty = jnp.where(row == 3, -1.0, 0.0)
    for o in range(GY):
        out[o] = empty
        count[o] = 0
    for fetch in fetches[:3]:
        fetch.wait()
    parts = [normals[j].astype(F32) for j in range(3)] + [cells[...].astype(F32)]
    for b in range(BLOCKS):
        owner = owners[b]
        rank = count[owner]
        count[owner] = rank + 1
        value = jnp.concatenate([p[b : b + 1] for p in parts], 0)
        value = jnp.concatenate([value, value], 1)
        out[owner] = jnp.where(half == rank, value, out[owner])
    for fetch in fetches[3:]:
        fetch.wait()


def return_body(owners, got, out, count, rows):
    for o in range(GY):
        count[o] = 0
    for b in range(BLOCKS):
        owner = owners[b]
        rank = count[owner]
        count[owner] = rank + 1
        value = got[owner]
        rows[b] = jnp.where(rank == 0, value, pltpu.roll(value, 64, 1))
    for j in range(3):
        out[j] = rows[:, j, :][:, :64]


VMEM = pl.BlockSpec(memory_space=pltpu.VMEM)
SMEM = pl.BlockSpec(memory_space=pltpu.SMEM)
HBM = pl.BlockSpec(memory_space=pltpu.HBM)


def call(body, name, outs, *operands, specs=None, scratch=()):
    shapes = [s if hasattr(s, "dtype") else jax.ShapeDtypeStruct(s, F32) for s in outs]
    single = len(shapes) == 1
    return pl.pallas_call(
        body,
        name=name,
        out_shape=shapes[0] if single else shapes,
        in_specs=specs or [VMEM] * len(operands),
        out_specs=VMEM if single else [VMEM] * len(shapes),
        scratch_shapes=list(scratch),
        compiler_params=pltpu.CompilerParams(vmem_limit_bytes=40 * 1024 * 1024),
    )(*operands)


def kept(x):
    return pltpu.with_memory_space_constraint(x, pltpu.HBM)


def swap(x, axis):
    return lax.all_to_all(x, axis, split_axis=0, concat_axis=0, tiled=True)


def local(normals, owners, cells, target):
    table = {k: jnp.asarray(v) for k, v in TABLES.items()}
    owner = owners.reshape(BLOCKS)
    counts = pltpu.SMEM((GY,), jnp.int32)
    brick = (BX, BY, NZ)
    message = (GY, 4, CAP * POINTS)

    by_part = jnp.moveaxis(normals, 1, 0)
    scratch = (
        pltpu.SMEM(owner.shape, jnp.int32),
        pltpu.VMEM(by_part.shape, BF16),
        pltpu.VMEM(cells.shape, jnp.int32),
        counts,
        pltpu.SemaphoreType.DMA((5,)),
    )
    tables_z = jax.ShapeDtypeStruct(table["zf"].shape, BF16)
    sources = (owner, by_part, cells, target, table["zf"])
    sent, target_here, zf = call(
        route_body,
        "route",
        [message, brick, tables_z],
        *map(kept, sources),
        specs=[HBM] * 5,
        scratch=scratch,
    )
    route = swap(sent, "gy")
    spread = call(splat_body, "splat", [(GY, 8, 256)], route, target_here, zf)
    got = swap(spread, "gy")
    y_args = (table["y_rows"], table["y_lanes"], table["ty"])
    words = jax.ShapeDtypeStruct((GX, 16, 128), jnp.int32)
    spread = call(forward_y_body, "forward_y", [words], got, *y_args)
    got = swap(spread, "gx")
    x_args = (table["x_rows"], table["x_lanes"], table["tx"], table["mirror"])
    words = jax.ShapeDtypeStruct((GX * ROWS, 128), jnp.int32)
    edges = (pltpu.VMEM((128, 128), jnp.int32),)
    spread = call(spectrum_body, "spectrum", [words], got, *x_args, scratch=edges)
    got = swap(spread.reshape(GX, ROWS, 1, 128), "gx").reshape(words.shape)
    spread = call(inverse_y_body, "inverse_y", [(GY, 8, 384)], got, *y_args, scratch=edges)
    got = swap(spread, "gy")
    chi, slope, picked = call(
        pick_body, "pick", [brick, (3,) + brick, message], got, table["zb"], route
    )
    returned = swap(picked, "gy")
    normal_grad = call(
        return_body,
        "deliver",
        [(3, BLOCKS, POINTS)],
        owner,
        returned,
        specs=[SMEM, VMEM],
        scratch=(counts, pltpu.VMEM((BLOCKS, 4, CAP * POINTS), F32)),
    )
    return chi, slope, jnp.moveaxis(normal_grad, 0, 1)


def solution(mesh):
    placed = (
        P(("gx", "gy"), None, None),
        P(("gx", "gy"), None),
        P(("gx", "gy"), None),
        P("gx", "gy", None),
    )
    return jax.shard_map(
        local,
        mesh=mesh,
        in_specs=placed,
        out_specs=(P("gx", "gy", None), P(None, "gx", "gy", None), P(("gx", "gy"), None, None)),
        check_vma=False,
    )
```

```python
import math

import jax
import jax.numpy as jnp
import ml_dtypes
import numpy as np
from jax import lax
from jax.experimental import pallas as pl
from jax.experimental.pallas import tpu as pltpu
from jax.sharding import PartitionSpec as P

GX, GY = 16, 32
BX, BY, NZ = 8, 8, 256
NX, NY = GX * BX, GY * BY
KZ = NZ // 2 // GY
KB = NY // BY // GX
BLOCKS, POINTS, CAP = 32, 64, 2
WIDTH = 64.0
F32, BF16 = jnp.float32, jnp.bfloat16


def halves(table, axis):
    high = table.astype(ml_dtypes.bfloat16)
    low = (table - high.astype(np.float64)).astype(ml_dtypes.bfloat16)
    return np.concatenate([high, low, high], axis)


def unit(turns):
    return np.exp(-2j * np.pi * turns)


def parts_of(w):
    return np.stack([np.stack([w.real, -w.imag]), np.stack([w.imag, w.real])])


Y_CLASS = np.array([[h, -h if h else 16] for h in range(GX)])
X_CLASS = np.array([k if k <= 8 else k - 16 for k in range(16)])


def make_tables():
    z = np.arange(NZ)
    kz = np.arange(NZ // 2)
    w = unit((kz[:, None] * z[None, :] % NZ) / NZ)
    zf = np.stack([w.real, w.imag])
    zf[1, 0] = np.where(z % 2 == 0, 1.0, -1.0)
    zb = 2.0 * zf
    zb[:, 0] = zf[:, 0]
    zb = zb / (NX * NY * NZ)
    order = lambda t: t.reshape(2, GY, KZ, NZ).transpose(1, 0, 2, 3).reshape(NZ, NZ)
    g = np.arange(GY)
    wy = parts_of(unit(Y_CLASS.reshape(-1)[:, None] * g[None, :] / GY))
    y_rows = np.einsum("abkg,zw->akzgbw", wy, np.eye(KZ)).reshape(NZ, NZ)
    g = np.arange(GX)
    wx = parts_of(unit(X_CLASS[:, None] * g[None, :] / GX))
    x_rows = np.einsum("abkg,zw->akzgbw", wx, np.eye(KB * KZ)).reshape(NZ, NZ)
    e = np.arange(8)
    w8 = unit((e[:, None] * e[None, :] % 8) / 8)
    y_lanes = np.concatenate([np.kron(np.eye(16), w8.real), np.kron(np.eye(16), w8.imag)], 1)
    x8 = lambda t: np.kron(np.eye(2), np.kron(t, np.eye(8)))
    x_lanes = np.concatenate([x8(w8.real), x8(w8.imag)], 1)
    ty = unit(np.repeat(Y_CLASS.reshape(-1), KZ)[:, None] * np.tile(e, 16)[None, :] / NY)
    tx = unit(
        np.repeat(X_CLASS, KB * KZ)[:, None] * np.tile(np.repeat(e, 8), 2)[None, :] / NX
    )
    ky = np.repeat(Y_CLASS.reshape(-1), KZ)[:, None] + GY * e[None, :]
    slope_y = np.tile(np.sin(2 * np.pi * (ky % NY) / NY), (1, 16))
    kx = np.repeat(X_CLASS, KB * KZ)[:, None] + GX * np.repeat(e, 8)[None, :]
    slope_x = np.tile(np.sin(2 * np.pi * (kx % NX) / NX), (1, 2))
    twist = lambda t, s: np.stack([t.real, -t.imag, s]).astype(np.float32)
    mirror = np.zeros((2, 2, 128, 128), np.float32)
    for m in range(2):
        for n in range(2):
            for f in range(2):
                for a in range(8):
                    for b in range(8):
                        src = f * 64 + (-a - m) % 8 * 8 + (-b - n) % 8
                        mirror[m, n, src, f * 64 + a * 8 + b] = 1.0
    return dict(
        zf=halves(order(zf), 1),
        zb=halves(order(zb), 0),
        y_rows=halves(y_rows, 1),
        x_rows=halves(x_rows, 1),
        y_back=halves(y_rows.T, 1),
        x_back=halves(x_rows.T, 1),
        y_lanes=halves(y_lanes, 0),
        x_lanes=halves(x_lanes, 0),
        ty=twist(ty, slope_y),
        tx=twist(tx, slope_x)[:2],
        mirror=np.tile(np.concatenate([mirror[:, 0], mirror[:, 1]], 2), (1, 2, 1)).astype(
            ml_dtypes.bfloat16
        ),
    )


TABLES = make_tables()


def split(x):
    high = x.astype(BF16)
    return high, (x - high.astype(F32)).astype(BF16)


def mm(a, b, ca=1, cb=0):
    return lax.dot_general(a, b, (((ca,), (cb,)), ((), ())), preferred_element_type=F32)


def thrice(x, axis):
    high, low = split(x)
    return jnp.concatenate([high, high, low], axis)


def twice(x, axis):
    return jnp.concatenate(split(x), axis)


def lanes_of(pairs, table, sign):
    count, rows = len(pairs), pairs[0][0].shape[0]
    stacked = jnp.concatenate([p[0] for p in pairs] + [p[1] for p in pairs], 0)
    out = mm(thrice(stacked, 1), table[...])
    result = []
    for i in range(count):
        a = out[i * rows : (i + 1) * rows]
        b = out[(count + i) * rows : (count + i + 1) * rows]
        if sign > 0:
            result.append((a[:, :128] - b[:, 128:], a[:, 128:] + b[:, :128]))
        else:
            result.append((a[:, :128] + b[:, 128:], b[:, :128] - a[:, 128:]))
    return result


def twisted(pairs, twist, sign):
    c, s = twist[0], twist[1]
    if sign > 0:
        return [(a * c + b * s, b * c - a * s) for a, b in pairs]
    return [(a * c - b * s, b * c + a * s) for a, b in pairs]


def halves_of(real, imag):
    return [(real[:, i * 128 : (i + 1) * 128], imag[:, i * 128 : (i + 1) * 128]) for i in range(2)]


def whole_of(pairs):
    return tuple(jnp.concatenate([p[c] for p in pairs], 1) for c in range(2))


def iota(shape, dim):
    return lax.broadcasted_iota(jnp.int32, shape, dim)


def places(route, first, count):
    rows = jnp.concatenate([route[s] for s in range(first, first + count)], 1)
    cell = rows[3:4]
    column = jnp.floor(cell * (1.0 / NZ))
    return rows, column, cell - column * NZ


def kz_of(rows):
    row = iota((rows, 128), 0)
    return (KZ * (row >> 3) + (row & 3)).astype(F32)


def odd(k, length):
    k = k & (length - 1)
    u = jnp.where(k < length // 2, k, k - length).astype(F32)
    return u, jnp.where(k == length // 2, 0.0, u)


def ky_of(gx, row, lane):
    second = ((row >> 2) & 1) == 1
    kb = jnp.where(second, jnp.where(gx == 0, 16, -gx), gx)
    return kb + GY * (lane & 7)


def oy_of():
    row, lane = iota((128, 128), 0), iota((128, 128), 1)
    return odd(ky_of(row >> 3, row, lane), NY)[1]


STEP = 4


def splat_body(route, target, zf, out):
    width = STEP * CAP * POINTS
    columns = iota((BX * BY, width), 0).astype(F32)
    levels = iota((NZ, width), 0).astype(F32)
    field = jnp.zeros((3 * BX * BY, NZ), F32)
    for first in range(0, GY, STEP):
        rows, column, level = places(route, first, STEP)
        here = columns == column
        weighted = [jnp.where(here, rows[j : j + 1], 0.0) for j in range(3)]
        weighted = jnp.concatenate(weighted, 0).astype(BF16)
        hot = jnp.where(levels == level, 1.0, 0.0).astype(BF16)
        field = field + mm(weighted, hot, 1, 1)
    both = jnp.concatenate([field, target[...].reshape(BX * BY, NZ)], 0)
    spread = mm(zf[...], thrice(both, 1), 1, 1)
    right = spread[:, 128:]
    right = jnp.where(iota((NZ, 128), 1) < 64, right * kz_of(NZ), right)
    out[...] = jnp.concatenate([spread[:, :128], right], 1).reshape(out.shape)


def swapped(x):
    return pltpu.roll(x, 64, 1)


def low_half(rows=128):
    return iota((rows, 128), 1) < 64


def packed_of(real, imag):
    low = low_half()
    return jnp.where(low, real, swapped(imag)), jnp.where(low, swapped(real), imag)


def weight_of(gx, gy):
    row, lane = iota((128, 128), 0), iota((128, 128), 1)
    gx = row >> 3 if gx is None else gx
    uy, _ = odd(ky_of(gx, row, lane), NY)
    uz = (KZ * gy + (row & 3)).astype(F32)
    square = uy * uy + uz * uz + 1.0
    small = lax.rsqrt(square)
    return small, square * small


BITS, SPLIT, BIAS, EDGE_BITS = 20, 11, 128, 30
ROWS = 18


def scale_of(exponent, bits):
    return jnp.exp2((bits - exponent).astype(F32))


def exponent_of(x):
    top = jnp.max(jnp.abs(x), 1, keepdims=True)
    power = jnp.floor(jnp.log2(jnp.maximum(top, 1e-26)) + 0.001) + 1.0
    return power.astype(jnp.int32)


def fixed(x, exponent, bits):
    return jnp.floor(x * scale_of(exponent, bits) + 0.5).astype(jnp.int32)


def encode(fields, exponents):
    a, b, c = (fixed(x, e, BITS) for x, e in zip(fields, exponents))
    e = [x + BIAS for x in exponents]
    mark = e[0] | (e[1] << 8) | (e[2] << 16)
    lane = iota((128, 128), 1)
    bit = jnp.where(lane < 24, (mark >> (lane & 31)) & 1, 0)
    first = (a << SPLIT) | (c & 0x7FF)
    second = (b << SPLIT) | ((c >> SPLIT) & 0x3FF) | (bit << 10)
    return first, second


def decode(first, second):
    lane = iota((128, 128), 1)
    bit = ((second >> 10) & 1) << (lane & 7)
    exponents = []
    for i in range(3):
        here = jnp.where((lane >> 3) == i, bit, 0).astype(F32)
        exponents.append(jnp.sum(here, 1, keepdims=True).astype(jnp.int32) - BIAS)
    a, b = first >> SPLIT, second >> SPLIT
    c = (((second & 0x3FF) << 22) >> SPLIT) | (first & 0x7FF)
    fields = [x.astype(F32) * (1.0 / scale_of(e, BITS)) for x, e in zip((a, b, c), exponents)]
    return fields, exponents


def forward_y_body(got, rows, lanes, twist, out):
    x = mm(rows[...], thrice(got[...].reshape(NZ, NZ), 0))
    pairs = twisted(halves_of(x[:128], x[128:]), twist, 1)
    left, right = lanes_of(pairs, lanes, 1)
    low = low_half()
    oy = oy_of()
    real, imag = (jnp.where(low, left[c], oy * left[c] + swapped(right[c])) for c in range(2))
    target = jnp.where(low, swapped(right[0]), right[1])
    part_x, part_yz = packed_of(real, imag)
    fields = (part_x, part_yz * weight_of(None, lax.axis_index("gy"))[0], target)
    first, second = encode(fields, [exponent_of(x) for x in fields])
    out[:, 0:8, :] = first.reshape(GX, 8, 128)
    out[:, 8:16, :] = second.reshape(GX, 8, 128)


def filters(gx, gy):
    shape = (128, 128)
    row, lane = iota(shape, 0), iota(shape, 1)
    kxb = row >> 3
    ux, ox = odd(kxb + GX * ((lane >> 3) & 7) - jnp.where(kxb > 8, GX, 0), NX)
    uy, _ = odd(ky_of(gx, row, lane), NY)
    kz = KZ * gy + (row & 3)
    uz = kz.astype(F32)
    gain = math.sqrt(float(NX * NY * NZ) * float(BX * BY * NZ) / (float(BLOCKS * POINTS) * 700.0))
    plane = ux * ux + uy * uy

    def base(ksq):
        value = gain * jnp.exp(ksq * (-1.0 / (2.0 * WIDTH**2))) / jnp.maximum(ksq, 1.0)
        return jnp.where(ksq == 0.0, 0.0, value)

    base0 = base(plane + uz * uz)
    base1 = jnp.where(kz == 0, base(plane + float(NZ // 2) ** 2), base0)
    return ox, (base0 + base1) * 0.5, (base0 - base1) * 0.5


def mirrored(pair, gx, mirror):
    x = jnp.concatenate(pair, 0).reshape(2, GX, 8, 128)
    x = jnp.concatenate([x[:, (GX - i) % GX : (GX - i) % GX + 1] for i in range(GX)], 1)
    x = x.reshape(2 * GX, 8, 128)
    x = jnp.where(gx == 0, x, jnp.concatenate([x[:, 4:], x[:, :4]], 1)).reshape(256, 128)
    special = jnp.concatenate([x[64:72], x[192:200]], 0)
    whole, special = (mm(twice(part, 1), mirror[i]) for i, part in enumerate((x, special)))
    parts = [whole[:64], special[:8], whole[72:192], special[8:], whole[200:]]
    whole = jnp.concatenate(parts, 0)
    half_y = (((iota((256, 128), 0) >> 2) & 1) == 1) & (gx == 0)
    whole = jnp.where(half_y, whole[:, 128:], whole[:, :128])
    return whole[:128], -whole[128:]


def turned(pair):
    return -pair[1], pair[0]


def spectrum_body(got, rows, back, lanes, twist, mirror, out, edges):
    gx, gy = lax.axis_index("gx"), lax.axis_index("gy")
    words = (got[:, i * 8 : i * 8 + 8, :].reshape(128, 128) for i in range(2))
    (part_x, part_yz, target), _ = decode(*words)
    weight = weight_of(gx, gy)[1]
    part_yz = part_yz * weight
    x = [*packed_of(part_x, part_yz), target, swapped(target)]
    x = [part.reshape(GX, 8, 128) for part in x]
    x = [jnp.concatenate(x[i : i + 2], 1).reshape(NZ, 128) for i in (0, 2)]
    x = jnp.concatenate(x, 1)
    x = mm(rows[...], thrice(x, 0))
    pairs = twisted(halves_of(x[:128], x[128:]), twist, 1)
    left, right = lanes_of(pairs, lanes, 1)
    ox, mean, diff = filters(gx, gy)
    low = low_half()

    div = [jnp.where(low, ox * left[c], left[c]) for c in range(2)]
    div = turned([d + swapped(d) for d in div])
    target = [jnp.where(low, right[c], swapped(right[c])) for c in range(2)]
    other = mirrored([jnp.where(low, div[c], target[c]) for c in range(2)], gx, mirror)
    div2 = [jnp.where(low, other[c], swapped(other[c])) for c in range(2)]
    target2 = [jnp.where(low, swapped(other[c]), other[c]) for c in range(2)]
    chi = [-(mean * div[c] + diff * div2[c]) for c in range(2)]
    chi2 = [-(mean * div2[c] + diff * div[c]) for c in range(2)]
    h = [
        0.25 * (mean * (chi[c] - target[c]) + diff * (chi2[c] - target2[c])) for c in range(2)
    ]
    h = turned(h)
    pairs = [chi, tuple(jnp.where(low, ox * h[c], h[c]) for c in range(2))]
    pairs = twisted(lanes_of(pairs, lanes, -1), twist, -1)
    both = jnp.concatenate(whole_of(pairs), 0)
    x = mm(back[...], thrice(both, 0)).reshape(GX, 16, NZ)
    chi, _ = packed_of(*(x[:, c : c + 8, :128].reshape(128, 128) for c in (0, 8)))
    gradients = packed_of(*(x[:, c : c + 8, 128:].reshape(128, 128) for c in (0, 8)))

    below = jnp.concatenate([chi[120:], chi[:120]], 0)
    above = jnp.concatenate([chi[8:], chi[:8]], 0)
    lane = iota((128, 128), 1) >> 3
    edge = jnp.where(lane == 0, pltpu.roll(below, 72, 1), 0.0)
    edge = jnp.where(lane == 1, pltpu.roll(above, 8, 1), edge)
    edge = jnp.where(lane == 2, pltpu.roll(below, 24, 1), edge)
    edge = jnp.where(lane == 3, pltpu.roll(above, 88, 1), edge)
    grad_x, h = gradients
    fields = (chi, grad_x, h * weight)
    exponents = [exponent_of(x) for x in fields]
    exponents[0] = jnp.maximum(exponents[0], exponent_of(edge))
    first, second = encode(fields, exponents)
    edges[...] = fixed(edge, exponents[0], EDGE_BITS)
    folded = edges[pl.ds(0, 32, stride=4), :]
    for i in range(1, 4):
        piece = pltpu.roll(edges[pl.ds(i, 32, stride=4), :], 32 * i, 1)
        folded = jnp.where((iota((32, 128), 1) >> 5) == i, piece, folded)
    for g in range(GX):
        at = g * ROWS
        out[at : at + 8, :] = first[g * 8 : g * 8 + 8]
        out[at + 8 : at + 16, :] = second[g * 8 : g * 8 + 8]
        out[at + 16 : at + 18, :] = folded[g * 2 : g * 2 + 2]


def inverse_y_body(got, back, lanes, twist, out, edges):
    pick = lambda at, count: [got[g * ROWS + at : g * ROWS + at + count, :] for g in range(GX)]
    first, second = (jnp.concatenate(pick(at, 8), 0) for at in (0, 8))
    folded = jnp.concatenate(pick(16, 2), 0)
    (chi, grad_x, h), exponents = decode(first, second)
    h = h * weight_of(None, lax.axis_index("gy"))[0]
    edges[pl.ds(0, 32, stride=4), :] = folded
    for i in range(1, 4):
        edges[pl.ds(i, 32, stride=4), :] = pltpu.roll(folded, 128 - 32 * i, 1)
    edge = edges[...].astype(F32) * (1.0 / scale_of(exponents[0], EDGE_BITS))
    lane = iota((128, 128), 1) >> 3
    edge48, edge96 = pltpu.roll(edge, 48, 1), pltpu.roll(edge, 96, 1)
    after = jnp.where(lane == 7, edge48, pltpu.roll(chi, 120, 1))
    after = jnp.where(lane == 15, edge96, after)
    before = jnp.where(lane == 0, edge, pltpu.roll(chi, 8, 1))
    before = jnp.where(lane == 8, edge48, before)
    left, right = packed_of(chi, (after - before) * 0.5), packed_of(grad_x, h)
    low = low_half()
    oy = oy_of()
    slope = turned([twist[2] * left[c] for c in range(2)])
    third = tuple(jnp.where(low, slope[c], oy * right[c]) for c in range(2))
    pairs = lanes_of([left, right, third], lanes, -1)
    pairs = twisted(pairs, twist, -1)
    both = jnp.concatenate(whole_of(pairs), 0)
    out[...] = mm(back[...], thrice(both, 0)).reshape(out.shape)


def pick_body(got, zb, route, chi, slope, picked):
    fields = got[...].reshape(NZ, 384)
    middle = fields[:, 128:256]
    middle = jnp.where(iota((NZ, 128), 1) < 64, middle, middle * kz_of(NZ))
    fields = jnp.concatenate([fields[:, :128], middle, fields[:, 256:]], 1)
    values = mm(thrice(fields, 0), zb[...], 0, 0)
    cells = BX * BY
    solid, slope_x, grad_x, grad_z, slope_y, grad_y = (
        values[i * cells : (i + 1) * cells] for i in range(6)
    )
    brick = (BX, BY, NZ)
    chi[...] = solid.reshape(brick)
    slope[0] = slope_x.reshape(brick)
    slope[1] = slope_y.reshape(brick)
    slope_z = (pltpu.roll(solid, NZ - 1, 1) - pltpu.roll(solid, 1, 1)) * 0.5
    slope[2] = slope_z.reshape(brick)
    grads = twice(jnp.concatenate([grad_x, grad_y, grad_z], 0), 1)
    width = STEP * CAP * POINTS
    columns = iota((cells, width), 0).astype(F32)
    levels = iota((NZ, width), 0).astype(F32)
    for first in range(0, GY, STEP):
        _, column, level = places(route, first, STEP)
        hot = jnp.where(levels == level, 1.0, 0.0).astype(BF16)
        at_level = mm(grads, jnp.concatenate([hot, hot], 0))
        here = columns == column
        lines = [
            jnp.sum(jnp.where(here, at_level[j * cells : (j + 1) * cells], 0.0), 0, keepdims=True)
            for j in range(3)
        ]
        lines = jnp.concatenate(lines + [jnp.zeros((1, width), F32)], 0)
        for s in range(STEP):
            picked[first + s] = lines[:, s * 128 : (s + 1) * 128]


def route_body(*refs):
    sources, (out, target, zf, row), (owners, normals, cells, count, sems) = (
        refs[:5],
        refs[5:9],
        refs[9:],
    )
    fetches = [
        pltpu.make_async_copy(source, place, sems.at[i])
        for i, (source, place) in enumerate(
            zip(sources + sources[:1], (owners, normals, cells, target, zf, row))
        )
    ]
    for fetch in fetches:
        fetch.start()
    line = iota((4, 128), 0)
    half = iota((4, 128), 1) >> 6
    empty = jnp.where(line == 3, -1.0, 0.0)
    for o in range(GY):
        out[o] = empty
        count[o] = 0
    for fetch in fetches[:3]:
        fetch.wait()
    parts = [normals[j].astype(F32) for j in range(3)] + [cells[...].astype(F32)]
    for b in range(BLOCKS):
        owner = owners[0, b]
        rank = count[owner]
        count[owner] = rank + 1
        value = jnp.concatenate([p[b : b + 1] for p in parts], 0)
        value = jnp.concatenate([value, value], 1)
        out[owner] = jnp.where(half == rank, value, out[owner])
    for fetch in fetches[3:]:
        fetch.wait()


def return_body(owners, got, out):
    square = (BLOCKS, BLOCKS)
    row, column = iota(square, 0), iota(square, 1)
    across = jnp.broadcast_to(owners[...], square)
    down = jnp.sum(jnp.where(row == column, across, 0), 1, keepdims=True)
    earlier = (down == across) & (column < row)
    rank = jnp.sum(jnp.where(earlier, 1, 0), 1, keepdims=True)
    hot = [jnp.where((down == column) & (rank == r), 1.0, 0.0) for r in range(CAP)]
    hot = jnp.concatenate(hot, 0).astype(BF16)
    x = jnp.concatenate([got[:, j, :] for j in range(3)], 1)
    parts = []
    for _ in range(3):
        parts.append(x.astype(BF16))
        x = x - parts[-1].astype(F32)
    total = mm(jnp.concatenate([hot] * 3, 1), jnp.concatenate(parts, 0))
    for j in range(3):
        lines = total[:, j * 128 : (j + 1) * 128]
        out[j] = (lines[:BLOCKS] + swapped(lines[BLOCKS:]))[:, :POINTS]


VMEM = pl.BlockSpec(memory_space=pltpu.VMEM)
SMEM = pl.BlockSpec(memory_space=pltpu.SMEM)
HBM = pl.BlockSpec(memory_space=pltpu.HBM)


def call(body, name, outs, *operands, specs=None, scratch=()):
    shapes = [s if hasattr(s, "dtype") else jax.ShapeDtypeStruct(s, F32) for s in outs]
    single = len(shapes) == 1
    return pl.pallas_call(
        body,
        name=name,
        out_shape=shapes[0] if single else shapes,
        in_specs=specs or [VMEM] * len(operands),
        out_specs=VMEM if single else [VMEM] * len(shapes),
        scratch_shapes=list(scratch),
        compiler_params=pltpu.CompilerParams(vmem_limit_bytes=40 * 1024 * 1024),
    )(*operands)


def kept(x):
    return pltpu.with_memory_space_constraint(x, pltpu.HBM)


def swap(x, axis):
    return lax.all_to_all(x, axis, split_axis=0, concat_axis=0, tiled=True)


def local(normals, owners, cells, target):
    table = {k: jnp.asarray(v) for k, v in TABLES.items()}
    owner = owners.reshape(1, BLOCKS)
    counts = pltpu.SMEM((GY,), jnp.int32)
    brick = (BX, BY, NZ)
    message = (GY, 4, CAP * POINTS)

    by_part = jnp.moveaxis(normals, 1, 0)
    scratch = (
        pltpu.SMEM(owner.shape, jnp.int32),
        pltpu.VMEM(by_part.shape, BF16),
        pltpu.VMEM(cells.shape, jnp.int32),
        counts,
        pltpu.SemaphoreType.DMA((6,)),
    )
    tables_z = jax.ShapeDtypeStruct(table["zf"].shape, BF16)
    sources = (owner, by_part, cells, target, table["zf"])
    row = jax.ShapeDtypeStruct(owner.shape, jnp.int32)
    sent, target_here, zf, owner_here = call(
        route_body,
        "route",
        [message, brick, tables_z, row],
        *map(kept, sources),
        specs=[HBM] * 5,
        scratch=scratch,
    )
    route = swap(sent, "gy")
    spread = call(splat_body, "splat", [(GY, 8, 256)], route, target_here, zf)
    got = swap(spread, "gy")
    y_args = (table["y_lanes"], table["ty"])
    words = jax.ShapeDtypeStruct((GX, 16, 128), jnp.int32)
    spread = call(forward_y_body, "forward_y", [words], got, table["y_rows"], *y_args)
    got = swap(spread, "gx")
    x_args = [table[k] for k in ("x_rows", "x_back", "x_lanes", "tx", "mirror")]
    words = jax.ShapeDtypeStruct((GX * ROWS, 128), jnp.int32)
    edges = (pltpu.VMEM((128, 128), jnp.int32),)
    spread = call(spectrum_body, "spectrum", [words], got, *x_args, scratch=edges)
    got = swap(spread.reshape(GX, ROWS, 1, 128), "gx").reshape(words.shape)
    y_args = (table["y_back"],) + y_args
    spread = call(inverse_y_body, "inverse_y", [(GY, 8, 384)], got, *y_args, scratch=edges)
    got = swap(spread, "gy")
    chi, slope, picked = call(
        pick_body, "pick", [brick, (3,) + brick, message], got, table["zb"], route
    )
    returned = swap(picked, "gy")
    normal_grad = call(return_body, "deliver", [(3, BLOCKS, POINTS)], owner_here, returned)
    return chi, slope, jnp.moveaxis(normal_grad, 0, 1)


def solution(mesh):
    placed = (
        P(("gx", "gy"), None, None),
        P(("gx", "gy"), None),
        P(("gx", "gy"), None),
        P("gx", "gy", None),
    )
    return jax.shard_map(
        local,
        mesh=mesh,
        in_specs=placed,
        out_specs=(P("gx", "gy", None), P(None, "gx", "gy", None), P(("gx", "gy"), None, None)),
        check_vma=False,
    )
```

```python
import math

import jax
import jax.numpy as jnp
import ml_dtypes
import numpy as np
from jax import lax
from jax.experimental import pallas as pl
from jax.experimental.pallas import tpu as pltpu
from jax.sharding import PartitionSpec as P

GX, GY = 16, 32
BX, BY, NZ = 8, 8, 256
NX, NY = GX * BX, GY * BY
KZ = NZ // 2 // GY
KB = NY // BY // GX
BLOCKS, POINTS, CAP = 32, 64, 2
WIDTH = 64.0
F32, BF16 = jnp.float32, jnp.bfloat16


def halves(table, axis):
    high = table.astype(ml_dtypes.bfloat16)
    low = (table - high.astype(np.float64)).astype(ml_dtypes.bfloat16)
    return np.concatenate([high, low, high], axis)


def unit(turns):
    return np.exp(-2j * np.pi * turns)


def parts_of(w):
    return np.stack([np.stack([w.real, -w.imag]), np.stack([w.imag, w.real])])


Y_CLASS = np.array([[h, -h if h else 16] for h in range(GX)])
X_CLASS = np.array([k if k <= 8 else k - 16 for k in range(16)])


def make_tables():
    z = np.arange(NZ)
    kz = np.arange(NZ // 2)
    w = unit((kz[:, None] * z[None, :] % NZ) / NZ)
    zf = np.stack([w.real, w.imag])
    zf[1, 0] = np.where(z % 2 == 0, 1.0, -1.0)
    zb = 2.0 * zf
    zb[:, 0] = zf[:, 0]
    zb = zb / (NX * NY * NZ)
    order = lambda t: t.reshape(2, GY, KZ, NZ).transpose(1, 0, 2, 3).reshape(NZ, NZ)
    g = np.arange(GY)
    wy = parts_of(unit(Y_CLASS.reshape(-1)[:, None] * g[None, :] / GY))
    y_rows = np.einsum("abkg,zw->akzgbw", wy, np.eye(KZ)).reshape(NZ, NZ)
    g = np.arange(GX)
    wx = parts_of(unit(X_CLASS[:, None] * g[None, :] / GX))
    x_rows = np.einsum("abkg,zw->akzgbw", wx, np.eye(KB * KZ)).reshape(NZ, NZ)
    e = np.arange(8)
    w8 = unit((e[:, None] * e[None, :] % 8) / 8)
    y_lanes = np.concatenate([np.kron(np.eye(16), w8.real), np.kron(np.eye(16), w8.imag)], 1)
    x8 = lambda t: np.kron(np.eye(2), np.kron(t, np.eye(8)))
    x_lanes = np.concatenate([x8(w8.real), x8(w8.imag)], 1)
    ty = unit(np.repeat(Y_CLASS.reshape(-1), KZ)[:, None] * np.tile(e, 16)[None, :] / NY)
    tx = unit(
        np.repeat(X_CLASS, KB * KZ)[:, None] * np.tile(np.repeat(e, 8), 2)[None, :] / NX
    )
    ky = np.repeat(Y_CLASS.reshape(-1), KZ)[:, None] + GY * e[None, :]
    slope_y = np.tile(np.sin(2 * np.pi * (ky % NY) / NY), (1, 16))
    kx = np.repeat(X_CLASS, KB * KZ)[:, None] + GX * np.repeat(e, 8)[None, :]
    slope_x = np.tile(np.sin(2 * np.pi * (kx % NX) / NX), (1, 2))
    twist = lambda t, s: np.stack([t.real, -t.imag, s]).astype(np.float32)
    mirror = np.zeros((2, 2, 128, 128), np.float32)
    for m in range(2):
        for n in range(2):
            for f in range(2):
                for a in range(8):
                    for b in range(8):
                        src = f * 64 + (-a - m) % 8 * 8 + (-b - n) % 8
                        mirror[m, n, src, f * 64 + a * 8 + b] = 1.0
    return dict(
        zf=halves(order(zf), 1),
        zb=halves(order(zb), 0),
        y_rows=halves(y_rows, 1),
        x_rows=halves(x_rows, 1),
        y_back=halves(y_rows.T, 1),
        x_back=halves(x_rows.T, 1),
        y_lanes=halves(y_lanes, 0),
        x_lanes=halves(x_lanes, 0),
        ty=twist(ty, slope_y),
        tx=twist(tx, slope_x)[:2],
        mirror=np.tile(np.concatenate([mirror[:, 0], mirror[:, 1]], 2), (1, 2, 1)).astype(
            ml_dtypes.bfloat16
        ),
    )


TABLES = make_tables()


def split(x):
    high = x.astype(BF16)
    return high, (x - high.astype(F32)).astype(BF16)


def mm(a, b, ca=1, cb=0):
    return lax.dot_general(a, b, (((ca,), (cb,)), ((), ())), preferred_element_type=F32)


def thrice(x, axis):
    high, low = split(x)
    return jnp.concatenate([high, high, low], axis)


def twice(x, axis):
    return jnp.concatenate(split(x), axis)


def lanes_of(pairs, table, sign):
    count, rows = len(pairs), pairs[0][0].shape[0]
    stacked = jnp.concatenate([p[0] for p in pairs] + [p[1] for p in pairs], 0)
    out = mm(thrice(stacked, 1), table[...])
    result = []
    for i in range(count):
        a = out[i * rows : (i + 1) * rows]
        b = out[(count + i) * rows : (count + i + 1) * rows]
        if sign > 0:
            result.append((a[:, :128] - b[:, 128:], a[:, 128:] + b[:, :128]))
        else:
            result.append((a[:, :128] + b[:, 128:], b[:, :128] - a[:, 128:]))
    return result


def twisted(pairs, twist, sign):
    c, s = twist[0], twist[1]
    if sign > 0:
        return [(a * c + b * s, b * c - a * s) for a, b in pairs]
    return [(a * c - b * s, b * c + a * s) for a, b in pairs]


def halves_of(real, imag):
    return [(real[:, i * 128 : (i + 1) * 128], imag[:, i * 128 : (i + 1) * 128]) for i in range(2)]


def whole_of(pairs):
    return tuple(jnp.concatenate([p[c] for p in pairs], 1) for c in range(2))


def iota(shape, dim):
    return lax.broadcasted_iota(jnp.int32, shape, dim)


def places(route, first, count):
    rows = jnp.concatenate([route[s] for s in range(first, first + count)], 1)
    cell = rows[3:4]
    column = jnp.floor(cell * (1.0 / NZ))
    return rows.astype(BF16), column.astype(BF16), (cell - column * NZ).astype(BF16)


def hot_of(labels, values):
    return jnp.where(labels == values, jnp.ones_like(labels), jnp.zeros_like(labels))


def kz_of(rows):
    row = iota((rows, 128), 0)
    return (KZ * (row >> 3) + (row & 3)).astype(F32)


def odd(k, length):
    k = k & (length - 1)
    u = jnp.where(k < length // 2, k, k - length).astype(F32)
    return u, jnp.where(k == length // 2, 0.0, u)


def ky_of(gx, row, lane):
    second = ((row >> 2) & 1) == 1
    kb = jnp.where(second, jnp.where(gx == 0, 16, -gx), gx)
    return kb + GY * (lane & 7)


def oy_of():
    row, lane = iota((128, 128), 0), iota((128, 128), 1)
    return odd(ky_of(row >> 3, row, lane), NY)[1]


STEP = 4


def splat_body(route, target, zf, out):
    width = STEP * CAP * POINTS
    columns = iota((BX * BY, width), 0).astype(BF16)
    levels = iota((NZ, width), 0).astype(BF16)
    field = jnp.zeros((3 * BX * BY, NZ), F32)
    for first in range(0, GY, STEP):
        rows, column, level = places(route, first, STEP)
        here = hot_of(columns, column)
        weighted = jnp.concatenate([here * rows[j : j + 1] for j in range(3)], 0)
        field = field + mm(weighted, hot_of(levels, level), 1, 1)
    both = jnp.concatenate([field, target[...].reshape(BX * BY, NZ)], 0)
    spread = mm(zf[...], thrice(both, 1), 1, 1)
    right = spread[:, 128:]
    right = jnp.where(iota((NZ, 128), 1) < 64, right * kz_of(NZ), right)
    out[...] = jnp.concatenate([spread[:, :128], right], 1).reshape(out.shape)


def swapped(x):
    return pltpu.roll(x, 64, 1)


def low_half(rows=128):
    return iota((rows, 128), 1) < 64


def packed_of(real, imag):
    low = low_half()
    return jnp.where(low, real, swapped(imag)), jnp.where(low, swapped(real), imag)


def weight_of(gx, gy):
    row, lane = iota((128, 128), 0), iota((128, 128), 1)
    gx = row >> 3 if gx is None else gx
    uy, _ = odd(ky_of(gx, row, lane), NY)
    uz = (KZ * gy + (row & 3)).astype(F32)
    square = uy * uy + uz * uz + 1.0
    small = lax.rsqrt(square)
    return small, square * small


BITS, SPLIT, BIAS, EDGE_BITS = 20, 11, 128, 30
ROWS = 18


def scale_of(exponent, bits):
    return jnp.exp2((bits - exponent).astype(F32))


def exponent_of(x):
    top = jnp.broadcast_to(jnp.max(jnp.abs(x), 1, keepdims=True), x.shape)
    power = jnp.floor(jnp.log2(jnp.maximum(top, 1e-26)) + 0.001) + 1.0
    return power.astype(jnp.int32)


def fixed(x, exponent, bits):
    return jnp.floor(x * scale_of(exponent, bits) + 0.5).astype(jnp.int32)


def encode(fields, exponents):
    a, b, c = (fixed(x, e, BITS) for x, e in zip(fields, exponents))
    e = [x + BIAS for x in exponents]
    mark = e[0] | (e[1] << 8) | (e[2] << 16)
    lane = iota((128, 128), 1)
    bit = jnp.where(lane < 24, (mark >> (lane & 31)) & 1, 0)
    first = (a << SPLIT) | (c & 0x7FF)
    second = (b << SPLIT) | ((c >> SPLIT) & 0x3FF) | (bit << 10)
    return first, second


def decode(first, second):
    lane = iota((128, 128), 1)
    bit = ((second >> 10) & 1) << (lane & 7)
    exponents = []
    for i in range(3):
        here = jnp.where((lane >> 3) == i, bit, 0).astype(F32)
        total = jnp.broadcast_to(jnp.sum(here, 1, keepdims=True), here.shape)
        exponents.append(total.astype(jnp.int32) - BIAS)
    a, b = first >> SPLIT, second >> SPLIT
    c = (((second & 0x3FF) << 22) >> SPLIT) | (first & 0x7FF)
    fields = [x.astype(F32) * (1.0 / scale_of(e, BITS)) for x, e in zip((a, b, c), exponents)]
    return fields, exponents


def forward_y_body(got, rows, lanes, twist, out):
    x = mm(rows[...], thrice(got[...].reshape(NZ, NZ), 0))
    pairs = twisted(halves_of(x[:128], x[128:]), twist, 1)
    left, right = lanes_of(pairs, lanes, 1)
    low = low_half()
    oy = oy_of()
    real, imag = (jnp.where(low, left[c], oy * left[c] + swapped(right[c])) for c in range(2))
    target = jnp.where(low, swapped(right[0]), right[1])
    part_x, part_yz = packed_of(real, imag)
    fields = (part_x, part_yz * weight_of(None, lax.axis_index("gy"))[0], target)
    first, second = encode(fields, [exponent_of(x) for x in fields])
    out[:, 0:8, :] = first.reshape(GX, 8, 128)
    out[:, 8:16, :] = second.reshape(GX, 8, 128)


def filters(gx, gy):
    shape = (128, 128)
    row, lane = iota(shape, 0), iota(shape, 1)
    kxb = row >> 3
    ux, ox = odd(kxb + GX * ((lane >> 3) & 7) - jnp.where(kxb > 8, GX, 0), NX)
    uy, _ = odd(ky_of(gx, row, lane), NY)
    kz = KZ * gy + (row & 3)
    uz = kz.astype(F32)
    gain = math.sqrt(float(NX * NY * NZ) * float(BX * BY * NZ) / (float(BLOCKS * POINTS) * 700.0))
    plane = ux * ux + uy * uy

    def base(ksq):
        value = gain * jnp.exp(ksq * (-1.0 / (2.0 * WIDTH**2))) / jnp.maximum(ksq, 1.0)
        return jnp.where(ksq == 0.0, 0.0, value)

    base0 = base(plane + uz * uz)
    base1 = jnp.where(kz == 0, base(plane + float(NZ // 2) ** 2), base0)
    return ox, (base0 + base1) * 0.5, (base0 - base1) * 0.5


def mirrored(pair, gx, mirror):
    x = jnp.concatenate(pair, 0).reshape(2, GX, 8, 128)
    x = jnp.concatenate([x[:, (GX - i) % GX : (GX - i) % GX + 1] for i in range(GX)], 1)
    x = x.reshape(2 * GX, 8, 128)
    x = jnp.where(gx == 0, x, jnp.concatenate([x[:, 4:], x[:, :4]], 1)).reshape(256, 128)
    special = jnp.concatenate([x[64:72], x[192:200]], 0)
    whole, special = (mm(twice(part, 1), mirror[i]) for i, part in enumerate((x, special)))
    parts = [whole[:64], special[:8], whole[72:192], special[8:], whole[200:]]
    whole = jnp.concatenate(parts, 0)
    half_y = (((iota((256, 128), 0) >> 2) & 1) == 1) & (gx == 0)
    whole = jnp.where(half_y, whole[:, 128:], whole[:, :128])
    return whole[:128], -whole[128:]


def turned(pair):
    return -pair[1], pair[0]


def spectrum_body(got, rows, back, lanes, twist, mirror, out, edges):
    gx, gy = lax.axis_index("gx"), lax.axis_index("gy")
    words = (got[:, i * 8 : i * 8 + 8, :].reshape(128, 128) for i in range(2))
    (part_x, part_yz, target), _ = decode(*words)
    weight = weight_of(gx, gy)[1]
    part_yz = part_yz * weight
    x = [*packed_of(part_x, part_yz), target, swapped(target)]
    x = [part.reshape(GX, 8, 128) for part in x]
    x = [jnp.concatenate(x[i : i + 2], 1).reshape(NZ, 128) for i in (0, 2)]
    x = jnp.concatenate(x, 1)
    x = mm(rows[...], thrice(x, 0))
    pairs = twisted(halves_of(x[:128], x[128:]), twist, 1)
    left, right = lanes_of(pairs, lanes, 1)
    ox, mean, diff = filters(gx, gy)
    low = low_half()

    div = [jnp.where(low, ox * left[c], left[c]) for c in range(2)]
    div = turned([d + swapped(d) for d in div])
    target = [jnp.where(low, right[c], swapped(right[c])) for c in range(2)]
    other = mirrored([jnp.where(low, div[c], target[c]) for c in range(2)], gx, mirror)
    div2 = [jnp.where(low, other[c], swapped(other[c])) for c in range(2)]
    target2 = [jnp.where(low, swapped(other[c]), other[c]) for c in range(2)]
    chi = [-(mean * div[c] + diff * div2[c]) for c in range(2)]
    chi2 = [-(mean * div2[c] + diff * div[c]) for c in range(2)]
    h = [
        0.25 * (mean * (chi[c] - target[c]) + diff * (chi2[c] - target2[c])) for c in range(2)
    ]
    h = turned(h)
    pairs = [chi, tuple(jnp.where(low, ox * h[c], h[c]) for c in range(2))]
    pairs = twisted(lanes_of(pairs, lanes, -1), twist, -1)
    both = jnp.concatenate(whole_of(pairs), 0)
    x = mm(back[...], thrice(both, 0)).reshape(GX, 16, NZ)
    chi, _ = packed_of(*(x[:, c : c + 8, :128].reshape(128, 128) for c in (0, 8)))
    gradients = packed_of(*(x[:, c : c + 8, 128:].reshape(128, 128) for c in (0, 8)))

    below = jnp.concatenate([chi[120:], chi[:120]], 0)
    above = jnp.concatenate([chi[8:], chi[:8]], 0)
    lane = iota((128, 128), 1) >> 3
    edge = jnp.where(lane == 0, pltpu.roll(below, 72, 1), 0.0)
    edge = jnp.where(lane == 1, pltpu.roll(above, 8, 1), edge)
    edge = jnp.where(lane == 2, pltpu.roll(below, 24, 1), edge)
    edge = jnp.where(lane == 3, pltpu.roll(above, 88, 1), edge)
    grad_x, h = gradients
    fields = (chi, grad_x, h * weight)
    exponents = [exponent_of(x) for x in fields]
    exponents[0] = jnp.maximum(exponents[0], exponent_of(edge))
    first, second = encode(fields, exponents)
    edges[...] = fixed(edge, exponents[0], EDGE_BITS)
    folded = edges[pl.ds(0, 32, stride=4), :]
    for i in range(1, 4):
        piece = pltpu.roll(edges[pl.ds(i, 32, stride=4), :], 32 * i, 1)
        folded = jnp.where((iota((32, 128), 1) >> 5) == i, piece, folded)
    for g in range(GX):
        at = g * ROWS
        out[at : at + 8, :] = first[g * 8 : g * 8 + 8]
        out[at + 8 : at + 16, :] = second[g * 8 : g * 8 + 8]
        out[at + 16 : at + 18, :] = folded[g * 2 : g * 2 + 2]


def inverse_y_body(got, back, lanes, twist, out, edges):
    pick = lambda at, count: [got[g * ROWS + at : g * ROWS + at + count, :] for g in range(GX)]
    first, second = (jnp.concatenate(pick(at, 8), 0) for at in (0, 8))
    folded = jnp.concatenate(pick(16, 2), 0)
    (chi, grad_x, h), exponents = decode(first, second)
    h = h * weight_of(None, lax.axis_index("gy"))[0]
    edges[pl.ds(0, 32, stride=4), :] = folded
    for i in range(1, 4):
        edges[pl.ds(i, 32, stride=4), :] = pltpu.roll(folded, 128 - 32 * i, 1)
    edge = edges[...].astype(F32) * (1.0 / scale_of(exponents[0], EDGE_BITS))
    lane = iota((128, 128), 1) >> 3
    edge48, edge96 = pltpu.roll(edge, 48, 1), pltpu.roll(edge, 96, 1)
    after = jnp.where(lane == 7, edge48, pltpu.roll(chi, 120, 1))
    after = jnp.where(lane == 15, edge96, after)
    before = jnp.where(lane == 0, edge, pltpu.roll(chi, 8, 1))
    before = jnp.where(lane == 8, edge48, before)
    left, right = packed_of(chi, (after - before) * 0.5), packed_of(grad_x, h)
    low = low_half()
    oy = oy_of()
    slope = turned([twist[2] * left[c] for c in range(2)])
    third = tuple(jnp.where(low, slope[c], oy * right[c]) for c in range(2))
    pairs = lanes_of([left, right, third], lanes, -1)
    pairs = twisted(pairs, twist, -1)
    both = jnp.concatenate(whole_of(pairs), 0)
    out[...] = mm(back[...], thrice(both, 0)).reshape(out.shape)


def pick_body(got, zb, route, chi_hbm, slope_hbm, picked, chi, slope, sems):
    fields = got[...].reshape(NZ, 384)
    middle = fields[:, 128:256]
    middle = jnp.where(iota((NZ, 128), 1) < 64, middle, middle * kz_of(NZ))
    fields = jnp.concatenate([fields[:, :128], middle, fields[:, 256:]], 1)
    values = mm(thrice(fields, 0), zb[...], 0, 0)
    cells = BX * BY
    solid, slope_x, grad_x, grad_z, slope_y, grad_y = (
        values[i * cells : (i + 1) * cells] for i in range(6)
    )
    brick = (BX, BY, NZ)
    chi[...] = solid.reshape(brick)
    slope[0] = slope_x.reshape(brick)
    slope[1] = slope_y.reshape(brick)
    slope_z = (pltpu.roll(solid, NZ - 1, 1) - pltpu.roll(solid, 1, 1)) * 0.5
    slope[2] = slope_z.reshape(brick)
    writes = [
        pltpu.make_async_copy(chi, chi_hbm, sems.at[0]),
        pltpu.make_async_copy(slope, slope_hbm, sems.at[1]),
    ]
    for write in writes:
        write.start()
    grads = twice(jnp.concatenate([grad_x, grad_y, grad_z], 0), 1)
    width = STEP * CAP * POINTS
    columns = iota((cells, width), 0).astype(F32)
    levels = iota((NZ, width), 0).astype(BF16)
    for first in range(0, GY, STEP):
        _, column, level = places(route, first, STEP)
        hot = hot_of(levels, level)
        at_level = mm(grads, jnp.concatenate([hot, hot], 0))
        here = columns == column.astype(F32)
        lines = [
            jnp.sum(jnp.where(here, at_level[j * cells : (j + 1) * cells], 0.0), 0, keepdims=True)
            for j in range(3)
        ]
        lines = jnp.concatenate(lines + [jnp.zeros((1, width), F32)], 0)
        for s in range(STEP):
            picked[first + s] = lines[:, s * 128 : (s + 1) * 128]
    for write in writes:
        write.wait()


def route_body(*refs):
    sources, (out, target, zf, row), (owners, normals, cells, count, sems) = (
        refs[:5],
        refs[5:9],
        refs[9:],
    )
    fetches = [
        pltpu.make_async_copy(source, place, sems.at[i])
        for i, (source, place) in enumerate(
            zip(sources + sources[:1], (owners, normals, cells, target, zf, row))
        )
    ]
    for fetch in fetches:
        fetch.start()
    line = iota((4, 128), 0)
    half = iota((4, 128), 1) >> 6
    empty = jnp.where(line == 3, -1.0, 0.0)
    for o in range(GY):
        out[o] = empty
        count[o] = 0
    for fetch in fetches[:3]:
        fetch.wait()
    parts = [normals[j].astype(F32) for j in range(3)] + [cells[...].astype(F32)]
    for b in range(BLOCKS):
        owner = owners[0, b]
        rank = count[owner]
        count[owner] = rank + 1
        value = jnp.concatenate([p[b : b + 1] for p in parts], 0)
        value = jnp.concatenate([value, value], 1)
        out[owner] = jnp.where(half == rank, value, out[owner])
    for fetch in fetches[3:]:
        fetch.wait()


def return_body(owners, got, out):
    square = (BLOCKS, BLOCKS)
    row, column = iota(square, 0), iota(square, 1)
    across = jnp.broadcast_to(owners[...], square)
    down = jnp.sum(jnp.where(row == column, across, 0), 1, keepdims=True)
    earlier = (down == across) & (column < row)
    rank = jnp.sum(jnp.where(earlier, 1, 0), 1, keepdims=True)
    hot = [jnp.where((down == column) & (rank == r), 1.0, 0.0) for r in range(CAP)]
    hot = jnp.concatenate(hot, 0).astype(BF16)
    x = jnp.concatenate([got[:, j, :] for j in range(3)], 1)
    parts = []
    for _ in range(3):
        parts.append(x.astype(BF16))
        x = x - parts[-1].astype(F32)
    total = mm(jnp.concatenate([hot] * 3, 1), jnp.concatenate(parts, 0))
    for j in range(3):
        lines = total[:, j * 128 : (j + 1) * 128]
        out[j] = (lines[:BLOCKS] + swapped(lines[BLOCKS:]))[:, :POINTS]


VMEM = pl.BlockSpec(memory_space=pltpu.VMEM)
SMEM = pl.BlockSpec(memory_space=pltpu.SMEM)
HBM = pl.BlockSpec(memory_space=pltpu.HBM)


def call(body, name, outs, *operands, specs=None, out_specs=None, scratch=()):
    shapes = [s if hasattr(s, "dtype") else jax.ShapeDtypeStruct(s, F32) for s in outs]
    single = len(shapes) == 1
    return pl.pallas_call(
        body,
        name=name,
        out_shape=shapes[0] if single else shapes,
        in_specs=specs or [VMEM] * len(operands),
        out_specs=out_specs or (VMEM if single else [VMEM] * len(shapes)),
        scratch_shapes=list(scratch),
        compiler_params=pltpu.CompilerParams(vmem_limit_bytes=40 * 1024 * 1024),
    )(*operands)


def kept(x):
    return pltpu.with_memory_space_constraint(x, pltpu.HBM)


def swap(x, axis):
    return lax.all_to_all(x, axis, split_axis=0, concat_axis=0, tiled=True)


def local(normals, owners, cells, target):
    table = {k: jnp.asarray(v) for k, v in TABLES.items()}
    owner = owners.reshape(1, BLOCKS)
    counts = pltpu.SMEM((GY,), jnp.int32)
    brick = (BX, BY, NZ)
    message = (GY, 4, CAP * POINTS)

    by_part = jnp.moveaxis(normals, 1, 0)
    scratch = (
        pltpu.SMEM(owner.shape, jnp.int32),
        pltpu.VMEM(by_part.shape, BF16),
        pltpu.VMEM(cells.shape, jnp.int32),
        counts,
        pltpu.SemaphoreType.DMA((6,)),
    )
    tables_z = jax.ShapeDtypeStruct(table["zf"].shape, BF16)
    sources = (owner, by_part, cells, target, table["zf"])
    row = jax.ShapeDtypeStruct(owner.shape, jnp.int32)
    sent, target_here, zf, owner_here = call(
        route_body,
        "route",
        [message, brick, tables_z, row],
        *map(kept, sources),
        specs=[HBM] * 5,
        scratch=scratch,
    )
    route = swap(sent, "gy")
    spread = call(splat_body, "splat", [(GY, 8, 256)], route, target_here, zf)
    got = swap(spread, "gy")
    y_args = (table["y_lanes"], table["ty"])
    words = jax.ShapeDtypeStruct((GX, 16, 128), jnp.int32)
    spread = call(forward_y_body, "forward_y", [words], got, table["y_rows"], *y_args)
    got = swap(spread, "gx")
    x_args = [table[k] for k in ("x_rows", "x_back", "x_lanes", "tx", "mirror")]
    words = jax.ShapeDtypeStruct((GX * ROWS, 128), jnp.int32)
    edges = (pltpu.VMEM((128, 128), jnp.int32),)
    spread = call(spectrum_body, "spectrum", [words], got, *x_args, scratch=edges)
    got = swap(spread.reshape(GX, ROWS, 1, 128), "gx").reshape(words.shape)
    y_args = (table["y_back"],) + y_args
    spread = call(inverse_y_body, "inverse_y", [(GY, 8, 384)], got, *y_args, scratch=edges)
    got = swap(spread, "gy")
    bricks = (3,) + brick
    chi, slope, picked = call(
        pick_body,
        "pick",
        [brick, bricks, message],
        got,
        table["zb"],
        route,
        out_specs=[HBM, HBM, VMEM],
        scratch=(pltpu.VMEM(brick, F32), pltpu.VMEM(bricks, F32), pltpu.SemaphoreType.DMA((2,))),
    )
    returned = swap(picked, "gy")
    normal_grad = call(return_body, "deliver", [(3, BLOCKS, POINTS)], owner_here, returned)
    return chi, slope, jnp.moveaxis(normal_grad, 0, 1)


def solution(mesh):
    placed = (
        P(("gx", "gy"), None, None),
        P(("gx", "gy"), None),
        P(("gx", "gy"), None),
        P("gx", "gy", None),
    )
    return jax.shard_map(
        local,
        mesh=mesh,
        in_specs=placed,
        out_specs=(P("gx", "gy", None), P(None, "gx", "gy", None), P(("gx", "gy"), None, None)),
        check_vma=False,
    )
```

```python
import math

import jax
import jax.numpy as jnp
import ml_dtypes
import numpy as np
from jax import lax
from jax.experimental import pallas as pl
from jax.experimental.pallas import tpu as pltpu
from jax.sharding import PartitionSpec as P

GX, GY = 16, 32
BX, BY, NZ = 8, 8, 256
NX, NY = GX * BX, GY * BY
KZ = NZ // 2 // GY
KB = NY // BY // GX
BLOCKS, POINTS, CAP = 32, 64, 2
WIDTH = 64.0
F32, BF16 = jnp.float32, jnp.bfloat16


def halves(table, axis):
    high = table.astype(ml_dtypes.bfloat16)
    low = (table - high.astype(np.float64)).astype(ml_dtypes.bfloat16)
    return np.concatenate([high, low, high], axis)


def unit(turns):
    return np.exp(-2j * np.pi * turns)


def parts_of(w):
    return np.stack([np.stack([w.real, -w.imag]), np.stack([w.imag, w.real])])


Y_CLASS = np.array([[h, -h if h else 16] for h in range(GX)])
X_CLASS = np.array([k if k <= 8 else k - 16 for k in range(16)])


def make_tables():
    z = np.arange(NZ)
    kz = np.arange(NZ // 2)
    w = unit((kz[:, None] * z[None, :] % NZ) / NZ)
    zf = np.stack([w.real, w.imag])
    zf[1, 0] = np.where(z % 2 == 0, 1.0, -1.0)
    zb = 2.0 * zf
    zb[:, 0] = zf[:, 0]
    zb = zb / (NX * NY * NZ)
    order = lambda t: t.reshape(2, GY, KZ, NZ).transpose(1, 0, 2, 3).reshape(NZ, NZ)
    g = np.arange(GY)
    wy = parts_of(unit(Y_CLASS.reshape(-1)[:, None] * g[None, :] / GY))
    y_rows = np.einsum("abkg,zw->akzgbw", wy, np.eye(KZ)).reshape(NZ, NZ)
    g = np.arange(GX)
    wx = parts_of(unit(X_CLASS[:, None] * g[None, :] / GX))
    x_rows = np.einsum("abkg,zw->akzgbw", wx, np.eye(KB * KZ)).reshape(NZ, NZ)
    e = np.arange(8)
    w8 = unit((e[:, None] * e[None, :] % 8) / 8)
    y_lanes = np.concatenate([np.kron(np.eye(16), w8.real), np.kron(np.eye(16), w8.imag)], 1)
    x8 = lambda t: np.kron(np.eye(2), np.kron(t, np.eye(8)))
    x_lanes = np.concatenate([x8(w8.real), x8(w8.imag)], 1)
    ty = unit(np.repeat(Y_CLASS.reshape(-1), KZ)[:, None] * np.tile(e, 16)[None, :] / NY)
    tx = unit(
        np.repeat(X_CLASS, KB * KZ)[:, None] * np.tile(np.repeat(e, 8), 2)[None, :] / NX
    )
    ky = np.repeat(Y_CLASS.reshape(-1), KZ)[:, None] + GY * e[None, :]
    slope_y = np.tile(np.sin(2 * np.pi * (ky % NY) / NY), (1, 16))
    kx = np.repeat(X_CLASS, KB * KZ)[:, None] + GX * np.repeat(e, 8)[None, :]
    slope_x = np.tile(np.sin(2 * np.pi * (kx % NX) / NX), (1, 2))
    twist = lambda t, s: np.stack([t.real, -t.imag, s]).astype(np.float32)
    mirror = np.zeros((2, 2, 128, 128), np.float32)
    for m in range(2):
        for n in range(2):
            for f in range(2):
                for a in range(8):
                    for b in range(8):
                        src = f * 64 + (-a - m) % 8 * 8 + (-b - n) % 8
                        mirror[m, n, src, f * 64 + a * 8 + b] = 1.0
    return dict(
        zf=halves(order(zf), 1),
        zb=halves(order(zb), 0),
        y_rows=halves(y_rows, 1),
        x_rows=halves(x_rows, 1),
        y_back=halves(y_rows.T, 1),
        x_back=halves(x_rows.T, 1),
        y_lanes=halves(y_lanes, 0),
        x_lanes=halves(x_lanes, 0),
        ty=twist(ty, slope_y),
        tx=twist(tx, slope_x)[:2],
        mirror=np.tile(np.concatenate([mirror[:, 0], mirror[:, 1]], 2), (1, 2, 1)).astype(
            ml_dtypes.bfloat16
        ),
    )


TABLES = make_tables()


def split(x):
    high = x.astype(BF16)
    return high, (x - high.astype(F32)).astype(BF16)


def mm(a, b, ca=1, cb=0):
    return lax.dot_general(a, b, (((ca,), (cb,)), ((), ())), preferred_element_type=F32)


def thrice(x, axis):
    high, low = split(x)
    return jnp.concatenate([high, high, low], axis)


def twice(x, axis):
    return jnp.concatenate(split(x), axis)


def lanes_of(pairs, table, sign):
    count, rows = len(pairs), pairs[0][0].shape[0]
    stacked = jnp.concatenate([p[0] for p in pairs] + [p[1] for p in pairs], 0)
    out = mm(thrice(stacked, 1), table[...])
    result = []
    for i in range(count):
        a = out[i * rows : (i + 1) * rows]
        b = out[(count + i) * rows : (count + i + 1) * rows]
        if sign > 0:
            result.append((a[:, :128] - b[:, 128:], a[:, 128:] + b[:, :128]))
        else:
            result.append((a[:, :128] + b[:, 128:], b[:, :128] - a[:, 128:]))
    return result


def twisted(pairs, twist, sign):
    c, s = twist[0], twist[1]
    if sign > 0:
        return [(a * c + b * s, b * c - a * s) for a, b in pairs]
    return [(a * c - b * s, b * c + a * s) for a, b in pairs]


def halves_of(real, imag):
    return [(real[:, i * 128 : (i + 1) * 128], imag[:, i * 128 : (i + 1) * 128]) for i in range(2)]


def whole_of(pairs):
    return tuple(jnp.concatenate([p[c] for p in pairs], 1) for c in range(2))


def iota(shape, dim):
    return lax.broadcasted_iota(jnp.int32, shape, dim)


def places(route, first, count):
    rows = jnp.concatenate([route[s] for s in range(first, first + count)], 1)
    cell = rows[3:4]
    column = jnp.floor(cell * (1.0 / NZ))
    return rows.astype(BF16), column.astype(BF16), (cell - column * NZ).astype(BF16)


def hot_of(labels, values):
    return jnp.where(labels == values, jnp.ones_like(labels), jnp.zeros_like(labels))


def kz_of(rows):
    row = iota((rows, 128), 0)
    return (KZ * (row >> 3) + (row & 3)).astype(F32)


def odd(k, length):
    k = k & (length - 1)
    u = jnp.where(k < length // 2, k, k - length).astype(F32)
    return u, jnp.where(k == length // 2, 0.0, u)


def ky_of(gx, row, lane):
    second = ((row >> 2) & 1) == 1
    kb = jnp.where(second, jnp.where(gx == 0, 16, -gx), gx)
    return kb + GY * (lane & 7)


def oy_of():
    row, lane = iota((128, 128), 0), iota((128, 128), 1)
    return odd(ky_of(row >> 3, row, lane), NY)[1]


STEP, PICK_STEP = 8, 2


def splat_body(route, target, zf, out):
    width = STEP * CAP * POINTS
    columns = iota((BX * BY, width), 0).astype(BF16)
    levels = iota((NZ, width), 0).astype(BF16)
    cells = BX * BY
    nothing = jnp.zeros((cells, width), BF16)
    blank = jnp.zeros((3 * cells, NZ), F32)
    field = jnp.concatenate([blank, target[...].reshape(cells, NZ)], 0).T
    for first in range(0, GY, STEP):
        rows, column, level = places(route, first, STEP)
        here = hot_of(columns, column)
        weighted = [here * rows[j : j + 1] for j in range(3)] + [nothing]
        field = field + mm(hot_of(levels, level), jnp.concatenate(weighted, 0), 1, 1)
    spread = mm(zf[...], thrice(field, 0))
    right = spread[:, 128:]
    right = jnp.where(iota((NZ, 128), 1) < 64, right * kz_of(NZ), right)
    out[...] = jnp.concatenate([spread[:, :128], right], 1).reshape(out.shape)


def swapped(x):
    return pltpu.roll(x, 64, 1)


def low_half(rows=128):
    return iota((rows, 128), 1) < 64


def packed_of(real, imag):
    low = low_half()
    return jnp.where(low, real, swapped(imag)), jnp.where(low, swapped(real), imag)


def weight_of(gx, gy):
    row, lane = iota((128, 128), 0), iota((128, 128), 1)
    gx = row >> 3 if gx is None else gx
    uy, _ = odd(ky_of(gx, row, lane), NY)
    uz = (KZ * gy + (row & 3)).astype(F32)
    square = uy * uy + uz * uz + 1.0
    small = lax.rsqrt(square)
    return small, square * small


BITS, SPLIT, BIAS, EDGE_BITS = 20, 11, 128, 30
ROWS = 18


def scale_of(exponent, bits):
    return jnp.exp2((bits - exponent).astype(F32))


def exponent_of(x):
    top = jnp.broadcast_to(jnp.max(jnp.abs(x), 1, keepdims=True), x.shape)
    power = jnp.floor(jnp.log2(jnp.maximum(top, 1e-26)) + 0.001) + 1.0
    return power.astype(jnp.int32)


def fixed(x, exponent, bits):
    return jnp.floor(x * scale_of(exponent, bits) + 0.5).astype(jnp.int32)


def encode(fields, exponents):
    a, b, c = (fixed(x, e, BITS) for x, e in zip(fields, exponents))
    e = [x + BIAS for x in exponents]
    mark = e[0] | (e[1] << 8) | (e[2] << 16)
    lane = iota((128, 128), 1)
    bit = jnp.where(lane < 24, (mark >> (lane & 31)) & 1, 0)
    first = (a << SPLIT) | (c & 0x7FF)
    second = (b << SPLIT) | ((c >> SPLIT) & 0x3FF) | (bit << 10)
    return first, second


def decode(first, second):
    lane = iota((128, 128), 1)
    bit = ((second >> 10) & 1) << (lane & 7)
    exponents = []
    for i in range(3):
        here = jnp.where((lane >> 3) == i, bit, 0).astype(F32)
        total = jnp.broadcast_to(jnp.sum(here, 1, keepdims=True), here.shape)
        exponents.append(total.astype(jnp.int32) - BIAS)
    a, b = first >> SPLIT, second >> SPLIT
    c = (((second & 0x3FF) << 22) >> SPLIT) | (first & 0x7FF)
    fields = [x.astype(F32) * (1.0 / scale_of(e, BITS)) for x, e in zip((a, b, c), exponents)]
    return fields, exponents


def forward_y_body(got, rows, lanes, twist, out):
    x = mm(rows[...], thrice(got[...].reshape(NZ, NZ), 0))
    pairs = twisted(halves_of(x[:128], x[128:]), twist, 1)
    left, right = lanes_of(pairs, lanes, 1)
    low = low_half()
    oy = oy_of()
    real, imag = (jnp.where(low, left[c], oy * left[c] + swapped(right[c])) for c in range(2))
    target = jnp.where(low, swapped(right[0]), right[1])
    part_x, part_yz = packed_of(real, imag)
    fields = (part_x, part_yz * weight_of(None, lax.axis_index("gy"))[0], target)
    first, second = encode(fields, [exponent_of(x) for x in fields])
    out[:, 0:8, :] = first.reshape(GX, 8, 128)
    out[:, 8:16, :] = second.reshape(GX, 8, 128)


def filters(gx, gy):
    shape = (128, 128)
    row, lane = iota(shape, 0), iota(shape, 1)
    kxb = row >> 3
    ux, ox = odd(kxb + GX * ((lane >> 3) & 7) - jnp.where(kxb > 8, GX, 0), NX)
    uy, _ = odd(ky_of(gx, row, lane), NY)
    kz = KZ * gy + (row & 3)
    uz = kz.astype(F32)
    gain = math.sqrt(float(NX * NY * NZ) * float(BX * BY * NZ) / (float(BLOCKS * POINTS) * 700.0))
    plane = ux * ux + uy * uy

    def base(ksq):
        value = gain * jnp.exp(ksq * (-1.0 / (2.0 * WIDTH**2))) / jnp.maximum(ksq, 1.0)
        return jnp.where(ksq == 0.0, 0.0, value)

    base0 = base(plane + uz * uz)
    base1 = jnp.where(kz == 0, base(plane + float(NZ // 2) ** 2), base0)
    return ox, (base0 + base1) * 0.5, (base0 - base1) * 0.5


def mirrored(pair, gx, mirror):
    x = jnp.concatenate(pair, 0).reshape(2, GX, 8, 128)
    x = jnp.concatenate([x[:, (GX - i) % GX : (GX - i) % GX + 1] for i in range(GX)], 1)
    x = x.reshape(2 * GX, 8, 128)
    x = jnp.where(gx == 0, x, jnp.concatenate([x[:, 4:], x[:, :4]], 1)).reshape(256, 128)
    special = jnp.concatenate([x[64:72], x[192:200]], 0)
    whole, special = (mm(twice(part, 1), mirror[i]) for i, part in enumerate((x, special)))
    parts = [whole[:64], special[:8], whole[72:192], special[8:], whole[200:]]
    whole = jnp.concatenate(parts, 0)
    half_y = (((iota((256, 128), 0) >> 2) & 1) == 1) & (gx == 0)
    whole = jnp.where(half_y, whole[:, 128:], whole[:, :128])
    return whole[:128], -whole[128:]


def turned(pair):
    return -pair[1], pair[0]


def spectrum_body(got, rows, back, lanes, twist, mirror, out, edges):
    gx, gy = lax.axis_index("gx"), lax.axis_index("gy")
    words = (got[:, i * 8 : i * 8 + 8, :].reshape(128, 128) for i in range(2))
    (part_x, part_yz, target), _ = decode(*words)
    weight = weight_of(gx, gy)[1]
    part_yz = part_yz * weight
    x = [*packed_of(part_x, part_yz), target, swapped(target)]
    x = [part.reshape(GX, 8, 128) for part in x]
    x = [jnp.concatenate(x[i : i + 2], 1).reshape(NZ, 128) for i in (0, 2)]
    x = jnp.concatenate(x, 1)
    x = mm(rows[...], thrice(x, 0))
    pairs = twisted(halves_of(x[:128], x[128:]), twist, 1)
    left, right = lanes_of(pairs, lanes, 1)
    ox, mean, diff = filters(gx, gy)
    low = low_half()

    div = [jnp.where(low, ox * left[c], left[c]) for c in range(2)]
    div = turned([d + swapped(d) for d in div])
    target = [jnp.where(low, right[c], swapped(right[c])) for c in range(2)]
    other = mirrored([jnp.where(low, div[c], target[c]) for c in range(2)], gx, mirror)
    div2 = [jnp.where(low, other[c], swapped(other[c])) for c in range(2)]
    target2 = [jnp.where(low, swapped(other[c]), other[c]) for c in range(2)]
    chi = [-(mean * div[c] + diff * div2[c]) for c in range(2)]
    chi2 = [-(mean * div2[c] + diff * div[c]) for c in range(2)]
    h = [
        0.25 * (mean * (chi[c] - target[c]) + diff * (chi2[c] - target2[c])) for c in range(2)
    ]
    h = turned(h)
    pairs = [chi, tuple(jnp.where(low, ox * h[c], h[c]) for c in range(2))]
    pairs = twisted(lanes_of(pairs, lanes, -1), twist, -1)
    both = jnp.concatenate(whole_of(pairs), 0)
    x = mm(back[...], thrice(both, 0)).reshape(GX, 16, NZ)
    chi, _ = packed_of(*(x[:, c : c + 8, :128].reshape(128, 128) for c in (0, 8)))
    gradients = packed_of(*(x[:, c : c + 8, 128:].reshape(128, 128) for c in (0, 8)))

    below = jnp.concatenate([chi[120:], chi[:120]], 0)
    above = jnp.concatenate([chi[8:], chi[:8]], 0)
    lane = iota((128, 128), 1) >> 3
    edge = jnp.where(lane == 0, pltpu.roll(below, 72, 1), 0.0)
    edge = jnp.where(lane == 1, pltpu.roll(above, 8, 1), edge)
    edge = jnp.where(lane == 2, pltpu.roll(below, 24, 1), edge)
    edge = jnp.where(lane == 3, pltpu.roll(above, 88, 1), edge)
    grad_x, h = gradients
    fields = (chi, grad_x, h * weight)
    exponents = [exponent_of(x) for x in fields]
    exponents[0] = jnp.maximum(exponents[0], exponent_of(edge))
    first, second = encode(fields, exponents)
    edges[...] = fixed(edge, exponents[0], EDGE_BITS)
    folded = edges[pl.ds(0, 32, stride=4), :]
    for i in range(1, 4):
        piece = pltpu.roll(edges[pl.ds(i, 32, stride=4), :], 32 * i, 1)
        folded = jnp.where((iota((32, 128), 1) >> 5) == i, piece, folded)
    for g in range(GX):
        at = g * ROWS
        out[at : at + 8, :] = first[g * 8 : g * 8 + 8]
        out[at + 8 : at + 16, :] = second[g * 8 : g * 8 + 8]
        out[at + 16 : at + 18, :] = folded[g * 2 : g * 2 + 2]


def inverse_y_body(got, back, lanes, twist, out, edges):
    pick = lambda at, count: [got[g * ROWS + at : g * ROWS + at + count, :] for g in range(GX)]
    first, second = (jnp.concatenate(pick(at, 8), 0) for at in (0, 8))
    folded = jnp.concatenate(pick(16, 2), 0)
    (chi, grad_x, h), exponents = decode(first, second)
    h = h * weight_of(None, lax.axis_index("gy"))[0]
    edges[pl.ds(0, 32, stride=4), :] = folded
    for i in range(1, 4):
        edges[pl.ds(i, 32, stride=4), :] = pltpu.roll(folded, 128 - 32 * i, 1)
    edge = edges[...].astype(F32) * (1.0 / scale_of(exponents[0], EDGE_BITS))
    lane = iota((128, 128), 1) >> 3
    edge48, edge96 = pltpu.roll(edge, 48, 1), pltpu.roll(edge, 96, 1)
    after = jnp.where(lane == 7, edge48, pltpu.roll(chi, 120, 1))
    after = jnp.where(lane == 15, edge96, after)
    before = jnp.where(lane == 0, edge, pltpu.roll(chi, 8, 1))
    before = jnp.where(lane == 8, edge48, before)
    left, right = packed_of(chi, (after - before) * 0.5), packed_of(grad_x, h)
    low = low_half()
    oy = oy_of()
    slope = turned([twist[2] * left[c] for c in range(2)])
    third = tuple(jnp.where(low, slope[c], oy * right[c]) for c in range(2))
    pairs = lanes_of([left, right, third], lanes, -1)
    pairs = twisted(pairs, twist, -1)
    both = jnp.concatenate(whole_of(pairs), 0)
    out[...] = mm(back[...], thrice(both, 0)).reshape(out.shape)


def pick_body(got, zb, route, chi_hbm, slope_hbm, picked, chi, slope, sems):
    fields = got[...].reshape(NZ, 384)
    middle = fields[:, 128:256]
    middle = jnp.where(iota((NZ, 128), 1) < 64, middle, middle * kz_of(NZ))
    fields = jnp.concatenate([fields[:, :128], middle, fields[:, 256:]], 1)
    values = mm(thrice(fields, 0), zb[...], 0, 0)
    cells = BX * BY
    solid, slope_x, grad_x, grad_z, slope_y, grad_y = (
        values[i * cells : (i + 1) * cells] for i in range(6)
    )
    brick = (BX, BY, NZ)
    chi[...] = solid.reshape(brick)
    slope[0] = slope_x.reshape(brick)
    slope[1] = slope_y.reshape(brick)
    slope_z = (pltpu.roll(solid, NZ - 1, 1) - pltpu.roll(solid, 1, 1)) * 0.5
    slope[2] = slope_z.reshape(brick)
    writes = [
        pltpu.make_async_copy(chi, chi_hbm, sems.at[0]),
        pltpu.make_async_copy(slope, slope_hbm, sems.at[1]),
    ]
    for write in writes:
        write.start()
    grads = twice(jnp.concatenate([grad_x, grad_y, grad_z], 0), 1)
    width = PICK_STEP * CAP * POINTS
    columns = iota((cells, width), 0).astype(F32)
    levels = iota((NZ, width), 0).astype(BF16)
    for first in range(0, GY, PICK_STEP):
        _, column, level = places(route, first, PICK_STEP)
        hot = hot_of(levels, level)
        at_level = mm(grads, jnp.concatenate([hot, hot], 0))
        here = columns == column.astype(F32)
        lines = [
            jnp.sum(jnp.where(here, at_level[j * cells : (j + 1) * cells], 0.0), 0, keepdims=True)
            for j in range(3)
        ]
        lines = jnp.concatenate(lines + [jnp.zeros((1, width), F32)], 0)
        for s in range(PICK_STEP):
            picked[first + s] = lines[:, s * 128 : (s + 1) * 128]
    for write in writes:
        write.wait()


def route_body(*refs):
    sources, (out, target, zf, row), (owners, normals, cells, count, sems) = (
        refs[:5],
        refs[5:9],
        refs[9:],
    )
    fetches = [
        pltpu.make_async_copy(source, place, sems.at[i])
        for i, (source, place) in enumerate(
            zip(sources + sources[:1], (owners, normals, cells, target, zf, row))
        )
    ]
    for fetch in fetches:
        fetch.start()
    line = iota((4, 128), 0)
    half = iota((4, 128), 1) >> 6
    empty = jnp.where(line == 3, -1.0, 0.0)
    for o in range(GY):
        out[o] = empty
        count[o] = 0
    for fetch in fetches[:3]:
        fetch.wait()
    parts = [normals[j].astype(F32) for j in range(3)] + [cells[...].astype(F32)]
    for b in range(BLOCKS):
        owner = owners[0, b]
        rank = count[owner]
        count[owner] = rank + 1
        value = jnp.concatenate([p[b : b + 1] for p in parts], 0)
        value = jnp.concatenate([value, value], 1)
        out[owner] = jnp.where(half == rank, value, out[owner])
    for fetch in fetches[3:]:
        fetch.wait()


def return_body(owners, got, out):
    square = (BLOCKS, BLOCKS)
    row, column = iota(square, 0), iota(square, 1)
    across = jnp.broadcast_to(owners[...], square)
    down = jnp.sum(jnp.where(row == column, across, 0), 1, keepdims=True)
    earlier = (down == across) & (column < row)
    rank = jnp.sum(jnp.where(earlier, 1, 0), 1, keepdims=True)
    hot = [jnp.where((down == column) & (rank == r), 1.0, 0.0) for r in range(CAP)]
    hot = jnp.concatenate(hot, 0).astype(BF16)
    x = jnp.concatenate([got[:, j, :] for j in range(3)], 1)
    parts = []
    for _ in range(3):
        parts.append(x.astype(BF16))
        x = x - parts[-1].astype(F32)
    total = mm(jnp.concatenate([hot] * 3, 1), jnp.concatenate(parts, 0))
    for j in range(3):
        lines = total[:, j * 128 : (j + 1) * 128]
        out[j] = (lines[:BLOCKS] + swapped(lines[BLOCKS:]))[:, :POINTS]


VMEM = pl.BlockSpec(memory_space=pltpu.VMEM)
SMEM = pl.BlockSpec(memory_space=pltpu.SMEM)
HBM = pl.BlockSpec(memory_space=pltpu.HBM)


def call(body, name, outs, *operands, specs=None, out_specs=None, scratch=()):
    shapes = [s if hasattr(s, "dtype") else jax.ShapeDtypeStruct(s, F32) for s in outs]
    single = len(shapes) == 1
    return pl.pallas_call(
        body,
        name=name,
        out_shape=shapes[0] if single else shapes,
        in_specs=specs or [VMEM] * len(operands),
        out_specs=out_specs or (VMEM if single else [VMEM] * len(shapes)),
        scratch_shapes=list(scratch),
        compiler_params=pltpu.CompilerParams(vmem_limit_bytes=40 * 1024 * 1024),
    )(*operands)


def kept(x):
    return pltpu.with_memory_space_constraint(x, pltpu.HBM)


def swap(x, axis):
    return lax.all_to_all(x, axis, split_axis=0, concat_axis=0, tiled=True)


def local(normals, owners, cells, target):
    table = {k: jnp.asarray(v) for k, v in TABLES.items()}
    owner = owners.reshape(1, BLOCKS)
    counts = pltpu.SMEM((GY,), jnp.int32)
    brick = (BX, BY, NZ)
    message = (GY, 4, CAP * POINTS)

    by_part = jnp.moveaxis(normals, 1, 0)
    scratch = (
        pltpu.SMEM(owner.shape, jnp.int32),
        pltpu.VMEM(by_part.shape, BF16),
        pltpu.VMEM(cells.shape, jnp.int32),
        counts,
        pltpu.SemaphoreType.DMA((6,)),
    )
    tables_z = jax.ShapeDtypeStruct(table["zf"].shape, BF16)
    sources = (owner, by_part, cells, target, table["zf"])
    row = jax.ShapeDtypeStruct(owner.shape, jnp.int32)
    sent, target_here, zf, owner_here = call(
        route_body,
        "route",
        [message, brick, tables_z, row],
        *map(kept, sources),
        specs=[HBM] * 5,
        scratch=scratch,
    )
    route = swap(sent, "gy")
    spread = call(splat_body, "splat", [(GY, 8, 256)], route, target_here, zf)
    got = swap(spread, "gy")
    y_args = (table["y_lanes"], table["ty"])
    words = jax.ShapeDtypeStruct((GX, 16, 128), jnp.int32)
    spread = call(forward_y_body, "forward_y", [words], got, table["y_rows"], *y_args)
    got = swap(spread, "gx")
    x_args = [table[k] for k in ("x_rows", "x_back", "x_lanes", "tx", "mirror")]
    words = jax.ShapeDtypeStruct((GX * ROWS, 128), jnp.int32)
    edges = (pltpu.VMEM((128, 128), jnp.int32),)
    spread = call(spectrum_body, "spectrum", [words], got, *x_args, scratch=edges)
    got = swap(spread.reshape(GX, ROWS, 1, 128), "gx").reshape(words.shape)
    y_args = (table["y_back"],) + y_args
    spread = call(inverse_y_body, "inverse_y", [(GY, 8, 384)], got, *y_args, scratch=edges)
    got = swap(spread, "gy")
    bricks = (3,) + brick
    chi, slope, picked = call(
        pick_body,
        "pick",
        [brick, bricks, message],
        got,
        table["zb"],
        route,
        out_specs=[HBM, HBM, VMEM],
        scratch=(pltpu.VMEM(brick, F32), pltpu.VMEM(bricks, F32), pltpu.SemaphoreType.DMA((2,))),
    )
    returned = swap(picked, "gy")
    normal_grad = call(return_body, "deliver", [(3, BLOCKS, POINTS)], owner_here, returned)
    return chi, slope, jnp.moveaxis(normal_grad, 0, 1)


def solution(mesh):
    placed = (
        P(("gx", "gy"), None, None),
        P(("gx", "gy"), None),
        P(("gx", "gy"), None),
        P("gx", "gy", None),
    )
    return jax.shard_map(
        local,
        mesh=mesh,
        in_specs=placed,
        out_specs=(P("gx", "gy", None), P(None, "gx", "gy", None), P(("gx", "gy"), None, None)),
        check_vma=False,
    )
```

```python
import math

import jax
import jax.numpy as jnp
import ml_dtypes
import numpy as np
from jax import lax
from jax.experimental import pallas as pl
from jax.experimental.pallas import tpu as pltpu
from jax.sharding import PartitionSpec as P

GX, GY = 16, 32
BX, BY, NZ = 8, 8, 256
NX, NY = GX * BX, GY * BY
KZ = NZ // 2 // GY
KB = NY // BY // GX
BLOCKS, POINTS, CAP = 32, 64, 2
WIDTH = 64.0
F32, BF16 = jnp.float32, jnp.bfloat16


def halves(table, axis):
    high = table.astype(ml_dtypes.bfloat16)
    low = (table - high.astype(np.float64)).astype(ml_dtypes.bfloat16)
    return np.concatenate([high, low, high], axis)


def unit(turns):
    return np.exp(-2j * np.pi * turns)


def parts_of(w):
    return np.stack([np.stack([w.real, -w.imag]), np.stack([w.imag, w.real])])


Y_CLASS = np.array([[h, -h if h else 16] for h in range(GX)])
X_CLASS = np.array([k if k <= 8 else k - 16 for k in range(16)])


def make_tables():
    z = np.arange(NZ)
    kz = np.arange(NZ // 2)
    w = unit((kz[:, None] * z[None, :] % NZ) / NZ)
    zf = np.stack([w.real, w.imag])
    zf[1, 0] = np.where(z % 2 == 0, 1.0, -1.0)
    zb = 2.0 * zf
    zb[:, 0] = zf[:, 0]
    zb = zb / (NX * NY * NZ)
    order = lambda t: t.reshape(2, GY, KZ, NZ).transpose(1, 0, 2, 3).reshape(NZ, NZ)
    g = np.arange(GY)
    wy = parts_of(unit(Y_CLASS.reshape(-1)[:, None] * g[None, :] / GY))
    y_rows = np.einsum("abkg,zw->akzgbw", wy, np.eye(KZ)).reshape(NZ, NZ)
    g = np.arange(GX)
    wx = parts_of(unit(X_CLASS[:, None] * g[None, :] / GX))
    x_rows = np.einsum("abkg,zw->akzgbw", wx, np.eye(KB * KZ)).reshape(NZ, NZ)
    e = np.arange(8)
    w8 = unit((e[:, None] * e[None, :] % 8) / 8)
    y_lanes = np.concatenate([np.kron(np.eye(16), w8.real), np.kron(np.eye(16), w8.imag)], 1)
    x8 = lambda t: np.kron(np.eye(2), np.kron(t, np.eye(8)))
    x_lanes = np.concatenate([x8(w8.real), x8(w8.imag)], 1)
    ty = unit(np.repeat(Y_CLASS.reshape(-1), KZ)[:, None] * np.tile(e, 16)[None, :] / NY)
    tx = unit(
        np.repeat(X_CLASS, KB * KZ)[:, None] * np.tile(np.repeat(e, 8), 2)[None, :] / NX
    )
    ky = np.repeat(Y_CLASS.reshape(-1), KZ)[:, None] + GY * e[None, :]
    slope_y = np.tile(np.sin(2 * np.pi * (ky % NY) / NY), (1, 16))
    kx = np.repeat(X_CLASS, KB * KZ)[:, None] + GX * np.repeat(e, 8)[None, :]
    slope_x = np.tile(np.sin(2 * np.pi * (kx % NX) / NX), (1, 2))
    twist = lambda t, s: np.stack([t.real, -t.imag, s]).astype(np.float32)
    mirror = np.zeros((2, 2, 128, 128), np.float32)
    for m in range(2):
        for n in range(2):
            for f in range(2):
                for a in range(8):
                    for b in range(8):
                        src = f * 64 + (-a - m) % 8 * 8 + (-b - n) % 8
                        mirror[m, n, src, f * 64 + a * 8 + b] = 1.0
    return dict(
        zf=halves(order(zf), 1),
        zb=halves(order(zb), 0),
        y_rows=halves(y_rows, 1),
        x_rows=halves(x_rows, 1),
        y_back=halves(y_rows.T, 1),
        x_back=halves(x_rows.T, 1),
        y_lanes=halves(y_lanes, 0),
        x_lanes=halves(x_lanes, 0),
        ty=twist(ty, slope_y),
        tx=twist(tx, slope_x)[:2],
        mirror=np.tile(np.concatenate([mirror[:, 0], mirror[:, 1]], 2), (1, 2, 1)).astype(
            ml_dtypes.bfloat16
        ),
    )


TABLES = make_tables()


def split(x):
    high = x.astype(BF16)
    return high, (x - high.astype(F32)).astype(BF16)


def mm(a, b, ca=1, cb=0):
    return lax.dot_general(a, b, (((ca,), (cb,)), ((), ())), preferred_element_type=F32)


def thrice(x, axis):
    high, low = split(x)
    return jnp.concatenate([high, high, low], axis)


def twice(x, axis):
    return jnp.concatenate(split(x), axis)


def lanes_of(pairs, table, sign):
    count, rows = len(pairs), pairs[0][0].shape[0]
    stacked = jnp.concatenate([p[0] for p in pairs] + [p[1] for p in pairs], 0)
    out = mm(thrice(stacked, 1), table[...])
    result = []
    for i in range(count):
        a = out[i * rows : (i + 1) * rows]
        b = out[(count + i) * rows : (count + i + 1) * rows]
        if sign > 0:
            result.append((a[:, :128] - b[:, 128:], a[:, 128:] + b[:, :128]))
        else:
            result.append((a[:, :128] + b[:, 128:], b[:, :128] - a[:, 128:]))
    return result


def twisted(pairs, twist, sign):
    c, s = twist[0], twist[1]
    if sign > 0:
        return [(a * c + b * s, b * c - a * s) for a, b in pairs]
    return [(a * c - b * s, b * c + a * s) for a, b in pairs]


def halves_of(real, imag):
    return [(real[:, i * 128 : (i + 1) * 128], imag[:, i * 128 : (i + 1) * 128]) for i in range(2)]


def whole_of(pairs):
    return tuple(jnp.concatenate([p[c] for p in pairs], 1) for c in range(2))


def iota(shape, dim):
    return lax.broadcasted_iota(jnp.int32, shape, dim)


def places(route, first, count):
    rows = jnp.concatenate([route[s] for s in range(first, first + count)], 1)
    cell = rows[3:4]
    column = jnp.floor(cell * (1.0 / NZ))
    return rows.astype(BF16), column.astype(BF16), (cell - column * NZ).astype(BF16)


def hot_of(labels, values):
    return jnp.where(labels == values, jnp.ones_like(labels), jnp.zeros_like(labels))


def kz_of(rows):
    row = iota((rows, 128), 0)
    return (KZ * (row >> 3) + (row & 3)).astype(F32)


def odd(k, length):
    k = k & (length - 1)
    u = jnp.where(k < length // 2, k, k - length).astype(F32)
    return u, jnp.where(k == length // 2, 0.0, u)


def ky_of(gx, row, lane):
    second = ((row >> 2) & 1) == 1
    kb = jnp.where(second, jnp.where(gx == 0, 16, -gx), gx)
    return kb + GY * (lane & 7)


def oy_of():
    row, lane = iota((128, 128), 0), iota((128, 128), 1)
    return odd(ky_of(row >> 3, row, lane), NY)[1]


STEP, PICK_STEP = 8, 2


def splat_body(route, target, zf, out):
    width = STEP * CAP * POINTS
    columns = iota((BX * BY, width), 0).astype(BF16)
    levels = iota((NZ, width), 0).astype(BF16)
    cells = BX * BY
    nothing = jnp.zeros((cells, width), BF16)
    blank = jnp.zeros((3 * cells, NZ), F32)
    field = jnp.concatenate([blank, target[...].reshape(cells, NZ)], 0).T
    for first in range(0, GY, STEP):
        rows, column, level = places(route, first, STEP)
        here = hot_of(columns, column)
        weighted = [here * rows[j : j + 1] for j in range(3)] + [nothing]
        field = field + mm(hot_of(levels, level), jnp.concatenate(weighted, 0), 1, 1)
    spread = mm(zf[...], thrice(field, 0))
    right = spread[:, 128:]
    right = jnp.where(iota((NZ, 128), 1) < 64, right * kz_of(NZ), right)
    out[...] = jnp.concatenate([spread[:, :128], right], 1).reshape(out.shape)


def swapped(x):
    return pltpu.roll(x, 64, 1)


def low_half(rows=128):
    return iota((rows, 128), 1) < 64


def packed_of(real, imag):
    low = low_half()
    return jnp.where(low, real, swapped(imag)), jnp.where(low, swapped(real), imag)


def weight_of(gx, gy):
    row, lane = iota((128, 128), 0), iota((128, 128), 1)
    gx = row >> 3 if gx is None else gx
    uy, _ = odd(ky_of(gx, row, lane), NY)
    uz = (KZ * gy + (row & 3)).astype(F32)
    square = uy * uy + uz * uz + 1.0
    small = lax.rsqrt(square)
    return small, square * small


BITS, SPLIT, BIAS, EDGE_BITS = 20, 11, 128, 30
ROWS = 18


def scale_of(exponent, bits):
    return jnp.exp2((bits - exponent).astype(F32))


def exponent_of(x):
    top = jnp.broadcast_to(jnp.max(jnp.abs(x), 1, keepdims=True), x.shape)
    power = jnp.floor(jnp.log2(jnp.maximum(top, 1e-26)) + 0.001) + 1.0
    return power.astype(jnp.int32)


def fixed(x, exponent, bits):
    return jnp.floor(x * scale_of(exponent, bits) + 0.5).astype(jnp.int32)


def encode(fields, exponents):
    a, b, c = (fixed(x, e, BITS) for x, e in zip(fields, exponents))
    e = [x + BIAS for x in exponents]
    mark = e[0] | (e[1] << 8) | (e[2] << 16)
    lane = iota((128, 128), 1)
    bit = jnp.where(lane < 24, (mark >> (lane & 31)) & 1, 0)
    first = (a << SPLIT) | (c & 0x7FF)
    second = (b << SPLIT) | ((c >> SPLIT) & 0x3FF) | (bit << 10)
    return first, second


def decode(first, second):
    lane = iota((128, 128), 1)
    bit = ((second >> 10) & 1) << (lane & 7)
    exponents = []
    for i in range(3):
        here = jnp.where((lane >> 3) == i, bit, 0).astype(F32)
        total = jnp.broadcast_to(jnp.sum(here, 1, keepdims=True), here.shape)
        exponents.append(total.astype(jnp.int32) - BIAS)
    a, b = first >> SPLIT, second >> SPLIT
    c = (((second & 0x3FF) << 22) >> SPLIT) | (first & 0x7FF)
    fields = [x.astype(F32) * (1.0 / scale_of(e, BITS)) for x, e in zip((a, b, c), exponents)]
    return fields, exponents


def forward_y_body(got, rows, lanes, twist, out):
    x = mm(rows[...], thrice(got[...].reshape(NZ, NZ), 0))
    pairs = twisted(halves_of(x[:128], x[128:]), twist, 1)
    left, right = lanes_of(pairs, lanes, 1)
    low = low_half()
    oy = oy_of()
    real, imag = (jnp.where(low, left[c], oy * left[c] + swapped(right[c])) for c in range(2))
    target = jnp.where(low, swapped(right[0]), right[1])
    part_x, part_yz = packed_of(real, imag)
    fields = (part_x, part_yz * weight_of(None, lax.axis_index("gy"))[0], target)
    first, second = encode(fields, [exponent_of(x) for x in fields])
    out[:, 0:8, :] = first.reshape(GX, 8, 128)
    out[:, 8:16, :] = second.reshape(GX, 8, 128)


def filters(gx, gy):
    shape = (128, 128)
    row, lane = iota(shape, 0), iota(shape, 1)
    kxb = row >> 3
    ux, ox = odd(kxb + GX * ((lane >> 3) & 7) - jnp.where(kxb > 8, GX, 0), NX)
    uy, _ = odd(ky_of(gx, row, lane), NY)
    kz = KZ * gy + (row & 3)
    uz = kz.astype(F32)
    gain = math.sqrt(float(NX * NY * NZ) * float(BX * BY * NZ) / (float(BLOCKS * POINTS) * 700.0))
    plane = ux * ux + uy * uy

    def base(ksq):
        value = gain * jnp.exp(ksq * (-1.0 / (2.0 * WIDTH**2))) / jnp.maximum(ksq, 1.0)
        return jnp.where(ksq == 0.0, 0.0, value)

    base0 = base(plane + uz * uz)
    base1 = jnp.where(kz == 0, base(plane + float(NZ // 2) ** 2), base0)
    return ox, (base0 + base1) * 0.5, (base0 - base1) * 0.5


def mirrored(pair, gx, mirror):
    x = jnp.concatenate(pair, 0).reshape(2, GX, 8, 128)
    x = jnp.concatenate([x[:, (GX - i) % GX : (GX - i) % GX + 1] for i in range(GX)], 1)
    x = x.reshape(2 * GX, 8, 128)
    x = jnp.where(gx == 0, x, jnp.concatenate([x[:, 4:], x[:, :4]], 1)).reshape(256, 128)
    special = jnp.concatenate([x[64:72], x[192:200]], 0)
    whole, special = (mm(twice(part, 1), mirror[i]) for i, part in enumerate((x, special)))
    parts = [whole[:64], special[:8], whole[72:192], special[8:], whole[200:]]
    whole = jnp.concatenate(parts, 0)
    half_y = (((iota((256, 128), 0) >> 2) & 1) == 1) & (gx == 0)
    whole = jnp.where(half_y, whole[:, 128:], whole[:, :128])
    return whole[:128], -whole[128:]


def turned(pair):
    return -pair[1], pair[0]


def spectrum_body(got, rows, back, lanes, twist, mirror, out, edges):
    gx, gy = lax.axis_index("gx"), lax.axis_index("gy")
    words = (got[:, i * 8 : i * 8 + 8, :].reshape(128, 128) for i in range(2))
    (part_x, part_yz, target), _ = decode(*words)
    weight = weight_of(gx, gy)[1]
    part_yz = part_yz * weight
    x = [*packed_of(part_x, part_yz), target, swapped(target)]
    x = [part.reshape(GX, 8, 128) for part in x]
    x = [jnp.concatenate(x[i : i + 2], 1).reshape(NZ, 128) for i in (0, 2)]
    x = jnp.concatenate(x, 1)
    x = mm(rows[...], thrice(x, 0))
    pairs = twisted(halves_of(x[:128], x[128:]), twist, 1)
    left, right = lanes_of(pairs, lanes, 1)
    ox, mean, diff = filters(gx, gy)
    low = low_half()

    div = [jnp.where(low, ox * left[c], left[c]) for c in range(2)]
    div = turned([d + swapped(d) for d in div])
    target = [jnp.where(low, right[c], swapped(right[c])) for c in range(2)]
    other = mirrored([jnp.where(low, div[c], target[c]) for c in range(2)], gx, mirror)
    div2 = [jnp.where(low, other[c], swapped(other[c])) for c in range(2)]
    target2 = [jnp.where(low, swapped(other[c]), other[c]) for c in range(2)]
    chi = [-(mean * div[c] + diff * div2[c]) for c in range(2)]
    chi2 = [-(mean * div2[c] + diff * div[c]) for c in range(2)]
    h = [
        0.25 * (mean * (chi[c] - target[c]) + diff * (chi2[c] - target2[c])) for c in range(2)
    ]
    h = turned(h)
    pairs = [chi, tuple(jnp.where(low, ox * h[c], h[c]) for c in range(2))]
    pairs = twisted(lanes_of(pairs, lanes, -1), twist, -1)
    both = jnp.concatenate(whole_of(pairs), 0)
    x = mm(back[...], thrice(both, 0)).reshape(GX, 16, NZ)
    chi, _ = packed_of(*(x[:, c : c + 8, :128].reshape(128, 128) for c in (0, 8)))
    gradients = packed_of(*(x[:, c : c + 8, 128:].reshape(128, 128) for c in (0, 8)))

    below = jnp.concatenate([chi[120:], chi[:120]], 0)
    above = jnp.concatenate([chi[8:], chi[:8]], 0)
    lane = iota((128, 128), 1) >> 3
    edge = jnp.where(lane == 0, pltpu.roll(below, 72, 1), 0.0)
    edge = jnp.where(lane == 1, pltpu.roll(above, 8, 1), edge)
    edge = jnp.where(lane == 2, pltpu.roll(below, 24, 1), edge)
    edge = jnp.where(lane == 3, pltpu.roll(above, 88, 1), edge)
    grad_x, h = gradients
    fields = (chi, grad_x, h * weight)
    exponents = [exponent_of(x) for x in fields]
    exponents[0] = jnp.maximum(exponents[0], exponent_of(edge))
    first, second = encode(fields, exponents)
    edges[...] = fixed(edge, exponents[0], EDGE_BITS)
    folded = edges[pl.ds(0, 32, stride=4), :]
    for i in range(1, 4):
        piece = pltpu.roll(edges[pl.ds(i, 32, stride=4), :], 32 * i, 1)
        folded = jnp.where((iota((32, 128), 1) >> 5) == i, piece, folded)
    for g in range(GX):
        at = g * ROWS
        out[at : at + 8, :] = first[g * 8 : g * 8 + 8]
        out[at + 8 : at + 16, :] = second[g * 8 : g * 8 + 8]
        out[at + 16 : at + 18, :] = folded[g * 2 : g * 2 + 2]


def inverse_y_body(got, back, lanes, twist, out, edges):
    pick = lambda at, count: [got[g * ROWS + at : g * ROWS + at + count, :] for g in range(GX)]
    first, second = (jnp.concatenate(pick(at, 8), 0) for at in (0, 8))
    folded = jnp.concatenate(pick(16, 2), 0)
    (chi, grad_x, h), exponents = decode(first, second)
    h = h * weight_of(None, lax.axis_index("gy"))[0]
    edges[pl.ds(0, 32, stride=4), :] = folded
    for i in range(1, 4):
        edges[pl.ds(i, 32, stride=4), :] = pltpu.roll(folded, 128 - 32 * i, 1)
    edge = edges[...].astype(F32) * (1.0 / scale_of(exponents[0], EDGE_BITS))
    lane = iota((128, 128), 1) >> 3
    edge48, edge96 = pltpu.roll(edge, 48, 1), pltpu.roll(edge, 96, 1)
    after = jnp.where(lane == 7, edge48, pltpu.roll(chi, 120, 1))
    after = jnp.where(lane == 15, edge96, after)
    before = jnp.where(lane == 0, edge, pltpu.roll(chi, 8, 1))
    before = jnp.where(lane == 8, edge48, before)
    left, right = packed_of(chi, (after - before) * 0.5), packed_of(grad_x, h)
    low = low_half()
    oy = oy_of()
    slope = turned([twist[2] * left[c] for c in range(2)])
    third = tuple(jnp.where(low, slope[c], oy * right[c]) for c in range(2))
    pairs = lanes_of([left, right, third], lanes, -1)
    pairs = twisted(pairs, twist, -1)
    both = jnp.concatenate(whole_of(pairs), 0)
    out[...] = mm(back[...], thrice(both, 0)).reshape(out.shape)


def pick_body(got, zb, route, chi_hbm, slope_hbm, picked, chi, slope, sems):
    fields = got[...].reshape(NZ, 384)
    middle = fields[:, 128:256]
    middle = jnp.where(iota((NZ, 128), 1) < 64, middle, middle * kz_of(NZ))
    fields = jnp.concatenate([fields[:, :128], middle, fields[:, 256:]], 1)
    values = mm(thrice(fields, 0), zb[...], 0, 0)
    cells = BX * BY
    solid, slope_x, grad_x, grad_z, slope_y, grad_y = (
        values[i * cells : (i + 1) * cells] for i in range(6)
    )
    brick = (BX, BY, NZ)
    chi[...] = solid.reshape(brick)
    slope[0] = slope_x.reshape(brick)
    slope[1] = slope_y.reshape(brick)
    slope_z = (pltpu.roll(solid, NZ - 1, 1) - pltpu.roll(solid, 1, 1)) * 0.5
    slope[2] = slope_z.reshape(brick)
    writes = [
        pltpu.make_async_copy(chi, chi_hbm, sems.at[0]),
        pltpu.make_async_copy(slope, slope_hbm, sems.at[1]),
    ]
    for write in writes:
        write.start()
    grads = twice(jnp.concatenate([grad_x, grad_y, grad_z], 0), 1)
    width = PICK_STEP * CAP * POINTS
    columns = iota((cells, width), 0).astype(F32)
    levels = iota((NZ, width), 0).astype(BF16)
    for first in range(0, GY, PICK_STEP):
        _, column, level = places(route, first, PICK_STEP)
        hot = hot_of(levels, level)
        at_level = mm(grads, jnp.concatenate([hot, hot], 0))
        here = columns == column.astype(F32)
        lines = [
            jnp.sum(jnp.where(here, at_level[j * cells : (j + 1) * cells], 0.0), 0, keepdims=True)
            for j in range(3)
        ]
        lines = jnp.concatenate(lines + [jnp.zeros((1, width), F32)], 0)
        for s in range(PICK_STEP):
            picked[first + s] = lines[:, s * 128 : (s + 1) * 128]
    for write in writes:
        write.wait()


def route_body(*refs):
    sources, (out, target, zf, owners), (normals, cells, sems) = refs[:5], refs[5:9], refs[9:]
    fetches = [
        pltpu.make_async_copy(source, place, sems.at[i])
        for i, (source, place) in enumerate(zip(sources, (owners, normals, cells, target, zf)))
    ]
    for fetch in fetches:
        fetch.start()
    for fetch in fetches[:3]:
        fetch.wait()
    square = (BLOCKS, BLOCKS)
    row, column = iota(square, 0), iota(square, 1)
    across = jnp.broadcast_to(owners[...], square)
    down = jnp.sum(jnp.where(row == column, across, 0), 1, keepdims=True)
    earlier = (down == across) & (row < column)
    rank = jnp.sum(jnp.where(earlier, 1, 0), 0, keepdims=True)
    hot = [jnp.where((row == across) & (rank == r), 1.0, 0.0) for r in range(CAP)]
    hot = jnp.concatenate(hot, 1).astype(BF16)
    cell = cells[...]
    parts = [normals[j].astype(F32) for j in range(3)]
    parts += [((cell >> 8) + 1).astype(F32), (cell & 255).astype(F32)]
    blank = jnp.zeros((BLOCKS, POINTS), F32)
    first = [jnp.concatenate([p, blank], 1) for p in parts]
    second = [jnp.concatenate([blank, p], 1) for p in parts]
    values = [jnp.concatenate(lines, 1) for lines in (first, second)]
    lines = mm(hot, jnp.concatenate(values, 0).astype(BF16))
    lines = [lines[:, i * 128 : (i + 1) * 128] for i in range(5)]
    for j in range(3):
        out[:, j, :] = lines[j]
    out[:, 3, :] = (lines[3] - 1.0) * float(NZ) + lines[4]
    for fetch in fetches[3:]:
        fetch.wait()


def return_body(owners, got, out):
    square = (BLOCKS, BLOCKS)
    row, column = iota(square, 0), iota(square, 1)
    across = jnp.broadcast_to(owners[...], square)
    down = jnp.sum(jnp.where(row == column, across, 0), 1, keepdims=True)
    earlier = (down == across) & (column < row)
    rank = jnp.sum(jnp.where(earlier, 1, 0), 1, keepdims=True)
    hot = [jnp.where((down == column) & (rank == r), 1.0, 0.0) for r in range(CAP)]
    hot = jnp.concatenate(hot, 0).astype(BF16)
    x = jnp.concatenate([got[:, j, :] for j in range(3)], 1)
    parts = []
    for _ in range(3):
        parts.append(x.astype(BF16))
        x = x - parts[-1].astype(F32)
    total = mm(jnp.concatenate([hot] * 3, 1), jnp.concatenate(parts, 0))
    for j in range(3):
        lines = total[:, j * 128 : (j + 1) * 128]
        out[j] = (lines[:BLOCKS] + swapped(lines[BLOCKS:]))[:, :POINTS]


VMEM = pl.BlockSpec(memory_space=pltpu.VMEM)
SMEM = pl.BlockSpec(memory_space=pltpu.SMEM)
HBM = pl.BlockSpec(memory_space=pltpu.HBM)


def call(body, name, outs, *operands, specs=None, out_specs=None, scratch=()):
    shapes = [s if hasattr(s, "dtype") else jax.ShapeDtypeStruct(s, F32) for s in outs]
    single = len(shapes) == 1
    return pl.pallas_call(
        body,
        name=name,
        out_shape=shapes[0] if single else shapes,
        in_specs=specs or [VMEM] * len(operands),
        out_specs=out_specs or (VMEM if single else [VMEM] * len(shapes)),
        scratch_shapes=list(scratch),
        compiler_params=pltpu.CompilerParams(vmem_limit_bytes=40 * 1024 * 1024),
    )(*operands)


def kept(x):
    return pltpu.with_memory_space_constraint(x, pltpu.HBM)


def swap(x, axis):
    return lax.all_to_all(x, axis, split_axis=0, concat_axis=0, tiled=True)


def local(normals, owners, cells, target):
    table = {k: jnp.asarray(v) for k, v in TABLES.items()}
    owner = owners.reshape(1, BLOCKS)
    brick = (BX, BY, NZ)
    message = (GY, 4, CAP * POINTS)

    by_part = jnp.moveaxis(normals, 1, 0)
    scratch = (
        pltpu.VMEM(by_part.shape, BF16),
        pltpu.VMEM(cells.shape, jnp.int32),
        pltpu.SemaphoreType.DMA((5,)),
    )
    tables_z = jax.ShapeDtypeStruct(table["zf"].shape, BF16)
    sources = (owner, by_part, cells, target, table["zf"])
    row = jax.ShapeDtypeStruct(owner.shape, jnp.int32)
    sent, target_here, zf, owner_here = call(
        route_body,
        "route",
        [message, brick, tables_z, row],
        *map(kept, sources),
        specs=[HBM] * 5,
        scratch=scratch,
    )
    route = swap(sent, "gy")
    spread = call(splat_body, "splat", [(GY, 8, 256)], route, target_here, zf)
    got = swap(spread, "gy")
    y_args = (table["y_lanes"], table["ty"])
    words = jax.ShapeDtypeStruct((GX, 16, 128), jnp.int32)
    spread = call(forward_y_body, "forward_y", [words], got, table["y_rows"], *y_args)
    got = swap(spread, "gx")
    x_args = [table[k] for k in ("x_rows", "x_back", "x_lanes", "tx", "mirror")]
    words = jax.ShapeDtypeStruct((GX * ROWS, 128), jnp.int32)
    edges = (pltpu.VMEM((128, 128), jnp.int32),)
    spread = call(spectrum_body, "spectrum", [words], got, *x_args, scratch=edges)
    got = swap(spread.reshape(GX, ROWS, 1, 128), "gx").reshape(words.shape)
    y_args = (table["y_back"],) + y_args
    spread = call(inverse_y_body, "inverse_y", [(GY, 8, 384)], got, *y_args, scratch=edges)
    got = swap(spread, "gy")
    bricks = (3,) + brick
    chi, slope, picked = call(
        pick_body,
        "pick",
        [brick, bricks, message],
        got,
        table["zb"],
        route,
        out_specs=[HBM, HBM, VMEM],
        scratch=(pltpu.VMEM(brick, F32), pltpu.VMEM(bricks, F32), pltpu.SemaphoreType.DMA((2,))),
    )
    returned = swap(picked, "gy")
    normal_grad = call(return_body, "deliver", [(3, BLOCKS, POINTS)], owner_here, returned)
    return chi, slope, jnp.moveaxis(normal_grad, 0, 1)


def solution(mesh):
    placed = (
        P(("gx", "gy"), None, None),
        P(("gx", "gy"), None),
        P(("gx", "gy"), None),
        P("gx", "gy", None),
    )
    return jax.shard_map(
        local,
        mesh=mesh,
        in_specs=placed,
        out_specs=(P("gx", "gy", None), P(None, "gx", "gy", None), P(("gx", "gy"), None, None)),
        check_vma=False,
    )
```

```python
import math

import jax
import jax.numpy as jnp
import ml_dtypes
import numpy as np
from jax import lax
from jax.experimental import pallas as pl
from jax.experimental.pallas import tpu as pltpu
from jax.sharding import PartitionSpec as P

GX, GY = 16, 32
BX, BY, NZ = 8, 8, 256
NX, NY = GX * BX, GY * BY
KZ = NZ // 2 // GY
KB = NY // BY // GX
BLOCKS, POINTS, CAP = 32, 64, 2
WIDTH = 64.0
F32, BF16 = jnp.float32, jnp.bfloat16


def halves(table, axis):
    high = table.astype(ml_dtypes.bfloat16)
    low = (table - high.astype(np.float64)).astype(ml_dtypes.bfloat16)
    return np.concatenate([high, low, high], axis)


def unit(turns):
    return np.exp(-2j * np.pi * turns)


def parts_of(w):
    return np.stack([np.stack([w.real, -w.imag]), np.stack([w.imag, w.real])])


Y_CLASS = np.array([[h, -h if h else 16] for h in range(GX)])
X_CLASS = np.array([k if k <= 8 else k - 16 for k in range(16)])


def make_tables():
    z = np.arange(NZ)
    kz = np.arange(NZ // 2)
    w = unit((kz[:, None] * z[None, :] % NZ) / NZ)
    zf = np.stack([w.real, w.imag])
    zf[1, 0] = np.where(z % 2 == 0, 1.0, -1.0)
    zb = 2.0 * zf
    zb[:, 0] = zf[:, 0]
    zb = zb / (NX * NY * NZ)
    order = lambda t: t.reshape(2, GY, KZ, NZ).transpose(1, 0, 2, 3).reshape(NZ, NZ)
    g = np.arange(GY)
    wy = parts_of(unit(Y_CLASS.reshape(-1)[:, None] * g[None, :] / GY))
    y_rows = np.einsum("abkg,zw->akzgbw", wy, np.eye(KZ)).reshape(NZ, NZ)
    g = np.arange(GX)
    wx = parts_of(unit(X_CLASS[:, None] * g[None, :] / GX))
    x_rows = np.einsum("abkg,zw->akzgbw", wx, np.eye(KB * KZ)).reshape(NZ, NZ)
    e = np.arange(8)
    w8 = unit((e[:, None] * e[None, :] % 8) / 8)
    y_lanes = np.concatenate([np.kron(np.eye(16), w8.real), np.kron(np.eye(16), w8.imag)], 1)
    x8 = lambda t: np.kron(np.eye(2), np.kron(t, np.eye(8)))
    x_lanes = np.concatenate([x8(w8.real), x8(w8.imag)], 1)
    ty = unit(np.repeat(Y_CLASS.reshape(-1), KZ)[:, None] * np.tile(e, 16)[None, :] / NY)
    tx = unit(
        np.repeat(X_CLASS, KB * KZ)[:, None] * np.tile(np.repeat(e, 8), 2)[None, :] / NX
    )
    ky = np.repeat(Y_CLASS.reshape(-1), KZ)[:, None] + GY * e[None, :]
    slope_y = np.tile(np.sin(2 * np.pi * (ky % NY) / NY), (1, 16))
    kx = np.repeat(X_CLASS, KB * KZ)[:, None] + GX * np.repeat(e, 8)[None, :]
    slope_x = np.tile(np.sin(2 * np.pi * (kx % NX) / NX), (1, 2))
    twist = lambda t, s: np.stack([t.real, -t.imag, s]).astype(np.float32)
    mirror = np.zeros((2, 2, 128, 128), np.float32)
    for m in range(2):
        for n in range(2):
            for f in range(2):
                for a in range(8):
                    for b in range(8):
                        src = f * 64 + (-a - m) % 8 * 8 + (-b - n) % 8
                        mirror[m, n, src, f * 64 + a * 8 + b] = 1.0
    return dict(
        zf=halves(order(zf), 1)[:, : 2 * NZ].reshape(NZ, 2, NZ).swapaxes(0, 1),
        zb=halves(order(zb), 0),
        y_rows=halves(y_rows, 1),
        x_rows=halves(x_rows, 1),
        y_back=halves(y_rows.T, 1),
        x_back=halves(x_rows.T, 1),
        y_lanes=halves(y_lanes, 0),
        x_lanes=halves(x_lanes, 0),
        ty=twist(ty, slope_y),
        tx=twist(tx, slope_x)[:2],
        mirror=np.tile(np.concatenate([mirror[:, 0], mirror[:, 1]], 2), (1, 2, 1)).astype(
            ml_dtypes.bfloat16
        ),
    )


TABLES = make_tables()


def split(x):
    high = x.astype(BF16)
    return high, (x - high.astype(F32)).astype(BF16)


def mm(a, b, ca=1, cb=0):
    return lax.dot_general(a, b, (((ca,), (cb,)), ((), ())), preferred_element_type=F32)


def thrice(x, axis):
    high, low = split(x)
    return jnp.concatenate([high, high, low], axis)


def twice(x, axis):
    return jnp.concatenate(split(x), axis)


def lanes_of(pairs, table, sign):
    count, rows = len(pairs), pairs[0][0].shape[0]
    stacked = jnp.concatenate([p[0] for p in pairs] + [p[1] for p in pairs], 0)
    out = mm(thrice(stacked, 1), table[...])
    result = []
    for i in range(count):
        a = out[i * rows : (i + 1) * rows]
        b = out[(count + i) * rows : (count + i + 1) * rows]
        if sign > 0:
            result.append((a[:, :128] - b[:, 128:], a[:, 128:] + b[:, :128]))
        else:
            result.append((a[:, :128] + b[:, 128:], b[:, :128] - a[:, 128:]))
    return result


def twisted(pairs, twist, sign):
    c, s = twist[0], twist[1]
    if sign > 0:
        return [(a * c + b * s, b * c - a * s) for a, b in pairs]
    return [(a * c - b * s, b * c + a * s) for a, b in pairs]


def halves_of(real, imag):
    return [(real[:, i * 128 : (i + 1) * 128], imag[:, i * 128 : (i + 1) * 128]) for i in range(2)]


def whole_of(pairs):
    return tuple(jnp.concatenate([p[c] for p in pairs], 1) for c in range(2))


def iota(shape, dim):
    return lax.broadcasted_iota(jnp.int32, shape, dim)


def places(route, first, count):
    rows = jnp.concatenate([route[s] for s in range(first, first + count)], 1)
    cell = rows[3:4]
    column = jnp.floor(cell * (1.0 / NZ))
    return rows.astype(BF16), column.astype(BF16), (cell - column * NZ).astype(BF16)


def hot_of(labels, values):
    return jnp.where(labels == values, jnp.ones_like(labels), jnp.zeros_like(labels))


def kz_of(rows):
    row = iota((rows, 128), 0)
    return (KZ * (row >> 3) + (row & 3)).astype(F32)


def odd(k, length):
    k = k & (length - 1)
    u = jnp.where(k < length // 2, k, k - length).astype(F32)
    return u, jnp.where(k == length // 2, 0.0, u)


def ky_of(gx, row, lane):
    second = ((row >> 2) & 1) == 1
    kb = jnp.where(second, jnp.where(gx == 0, 16, -gx), gx)
    return kb + GY * (lane & 7)


def oy_of():
    row, lane = iota((128, 128), 0), iota((128, 128), 1)
    return odd(ky_of(row >> 3, row, lane), NY)[1]


STEP, PICK_STEP = 8, 2


def splat_body(route, target, zf, out):
    width = STEP * CAP * POINTS
    columns = iota((BX * BY, width), 0).astype(BF16)
    levels = iota((NZ, width), 0).astype(BF16)
    cells = BX * BY
    nothing = jnp.zeros((cells, width), BF16)
    blank = jnp.zeros((3 * cells, NZ), F32)
    field = jnp.concatenate([blank, target[...].reshape(cells, NZ)], 0).T
    for first in range(0, GY, STEP):
        rows, column, level = places(route, first, STEP)
        here = hot_of(columns, column)
        weighted = [here * rows[j : j + 1] for j in range(3)] + [nothing]
        field = field + mm(hot_of(levels, level), jnp.concatenate(weighted, 0), 1, 1)
    spread = mm(jnp.concatenate([zf[0], zf[1], zf[0]], 1), thrice(field, 0))
    right = spread[:, 128:]
    right = jnp.where(iota((NZ, 128), 1) < 64, right * kz_of(NZ), right)
    out[...] = jnp.concatenate([spread[:, :128], right], 1).reshape(out.shape)


def swapped(x):
    return pltpu.roll(x, 64, 1)


def low_half(rows=128):
    return iota((rows, 128), 1) < 64


def packed_of(real, imag):
    low = low_half()
    return jnp.where(low, real, swapped(imag)), jnp.where(low, swapped(real), imag)


def weight_of(gx, gy):
    row, lane = iota((128, 128), 0), iota((128, 128), 1)
    gx = row >> 3 if gx is None else gx
    uy, _ = odd(ky_of(gx, row, lane), NY)
    uz = (KZ * gy + (row & 3)).astype(F32)
    square = uy * uy + uz * uz + 1.0
    small = lax.rsqrt(square)
    return small, square * small


BITS, SPLIT, BIAS, EDGE_BITS = 20, 11, 128, 30
ROWS = 18


def scale_of(exponent, bits):
    return jnp.exp2((bits - exponent).astype(F32))


def exponent_of(x):
    top = jnp.broadcast_to(jnp.max(jnp.abs(x), 1, keepdims=True), x.shape)
    power = jnp.floor(jnp.log2(jnp.maximum(top, 1e-26)) + 0.001) + 1.0
    return power.astype(jnp.int32)


def fixed(x, exponent, bits):
    return jnp.floor(x * scale_of(exponent, bits) + 0.5).astype(jnp.int32)


def encode(fields, exponents):
    a, b, c = (fixed(x, e, BITS) for x, e in zip(fields, exponents))
    e = [x + BIAS for x in exponents]
    mark = e[0] | (e[1] << 8) | (e[2] << 16)
    lane = iota((128, 128), 1)
    bit = jnp.where(lane < 24, (mark >> (lane & 31)) & 1, 0)
    first = (a << SPLIT) | (c & 0x7FF)
    second = (b << SPLIT) | ((c >> SPLIT) & 0x3FF) | (bit << 10)
    return first, second


def decode(first, second):
    lane = iota((128, 128), 1)
    bit = ((second >> 10) & 1) << (lane & 7)
    exponents = []
    for i in range(3):
        here = jnp.where((lane >> 3) == i, bit, 0).astype(F32)
        total = jnp.broadcast_to(jnp.sum(here, 1, keepdims=True), here.shape)
        exponents.append(total.astype(jnp.int32) - BIAS)
    a, b = first >> SPLIT, second >> SPLIT
    c = (((second & 0x3FF) << 22) >> SPLIT) | (first & 0x7FF)
    fields = [x.astype(F32) * (1.0 / scale_of(e, BITS)) for x, e in zip((a, b, c), exponents)]
    return fields, exponents


def forward_y_body(got, rows, lanes, twist, out):
    x = mm(rows[...], thrice(got[...].reshape(NZ, NZ), 0))
    pairs = twisted(halves_of(x[:128], x[128:]), twist, 1)
    left, right = lanes_of(pairs, lanes, 1)
    low = low_half()
    oy = oy_of()
    real, imag = (jnp.where(low, left[c], oy * left[c] + swapped(right[c])) for c in range(2))
    target = jnp.where(low, swapped(right[0]), right[1])
    part_x, part_yz = packed_of(real, imag)
    fields = (part_x, part_yz * weight_of(None, lax.axis_index("gy"))[0], target)
    first, second = encode(fields, [exponent_of(x) for x in fields])
    out[:, 0:8, :] = first.reshape(GX, 8, 128)
    out[:, 8:16, :] = second.reshape(GX, 8, 128)


def filters(gx, gy):
    shape = (128, 128)
    row, lane = iota(shape, 0), iota(shape, 1)
    kxb = row >> 3
    ux, ox = odd(kxb + GX * ((lane >> 3) & 7) - jnp.where(kxb > 8, GX, 0), NX)
    uy, _ = odd(ky_of(gx, row, lane), NY)
    kz = KZ * gy + (row & 3)
    uz = kz.astype(F32)
    gain = math.sqrt(float(NX * NY * NZ) * float(BX * BY * NZ) / (float(BLOCKS * POINTS) * 700.0))
    plane = ux * ux + uy * uy

    def base(ksq):
        value = gain * jnp.exp(ksq * (-1.0 / (2.0 * WIDTH**2))) / jnp.maximum(ksq, 1.0)
        return jnp.where(ksq == 0.0, 0.0, value)

    base0 = base(plane + uz * uz)
    base1 = jnp.where(kz == 0, base(plane + float(NZ // 2) ** 2), base0)
    return ox, (base0 + base1) * 0.5, (base0 - base1) * 0.5


def mirrored(pair, gx, mirror):
    x = jnp.concatenate(pair, 0).reshape(2, GX, 8, 128)
    x = jnp.concatenate([x[:, (GX - i) % GX : (GX - i) % GX + 1] for i in range(GX)], 1)
    x = x.reshape(2 * GX, 8, 128)
    x = jnp.where(gx == 0, x, jnp.concatenate([x[:, 4:], x[:, :4]], 1)).reshape(256, 128)
    special = jnp.concatenate([x[64:72], x[192:200]], 0)
    whole, special = (mm(twice(part, 1), mirror[i]) for i, part in enumerate((x, special)))
    parts = [whole[:64], special[:8], whole[72:192], special[8:], whole[200:]]
    whole = jnp.concatenate(parts, 0)
    half_y = (((iota((256, 128), 0) >> 2) & 1) == 1) & (gx == 0)
    whole = jnp.where(half_y, whole[:, 128:], whole[:, :128])
    return whole[:128], -whole[128:]


def turned(pair):
    return -pair[1], pair[0]


def spectrum_body(got, rows, back, lanes, twist, mirror, out, edges):
    gx, gy = lax.axis_index("gx"), lax.axis_index("gy")
    words = (got[:, i * 8 : i * 8 + 8, :].reshape(128, 128) for i in range(2))
    (part_x, part_yz, target), _ = decode(*words)
    weight = weight_of(gx, gy)[1]
    part_yz = part_yz * weight
    x = [*packed_of(part_x, part_yz), target, swapped(target)]
    x = [part.reshape(GX, 8, 128) for part in x]
    x = [jnp.concatenate(x[i : i + 2], 1).reshape(NZ, 128) for i in (0, 2)]
    x = jnp.concatenate(x, 1)
    x = mm(rows[...], thrice(x, 0))
    pairs = twisted(halves_of(x[:128], x[128:]), twist, 1)
    left, right = lanes_of(pairs, lanes, 1)
    ox, mean, diff = filters(gx, gy)
    low = low_half()

    div = [jnp.where(low, ox * left[c], left[c]) for c in range(2)]
    div = turned([d + swapped(d) for d in div])
    target = [jnp.where(low, right[c], swapped(right[c])) for c in range(2)]
    other = mirrored([jnp.where(low, div[c], target[c]) for c in range(2)], gx, mirror)
    div2 = [jnp.where(low, other[c], swapped(other[c])) for c in range(2)]
    target2 = [jnp.where(low, swapped(other[c]), other[c]) for c in range(2)]
    chi = [-(mean * div[c] + diff * div2[c]) for c in range(2)]
    chi2 = [-(mean * div2[c] + diff * div[c]) for c in range(2)]
    h = [
        0.25 * (mean * (chi[c] - target[c]) + diff * (chi2[c] - target2[c])) for c in range(2)
    ]
    h = turned(h)
    pairs = [chi, tuple(jnp.where(low, ox * h[c], h[c]) for c in range(2))]
    pairs = twisted(lanes_of(pairs, lanes, -1), twist, -1)
    both = jnp.concatenate(whole_of(pairs), 0)
    x = mm(back[...], thrice(both, 0)).reshape(GX, 16, NZ)
    chi, _ = packed_of(*(x[:, c : c + 8, :128].reshape(128, 128) for c in (0, 8)))
    gradients = packed_of(*(x[:, c : c + 8, 128:].reshape(128, 128) for c in (0, 8)))

    below = jnp.concatenate([chi[120:], chi[:120]], 0)
    above = jnp.concatenate([chi[8:], chi[:8]], 0)
    lane = iota((128, 128), 1) >> 3
    edge = jnp.where(lane == 0, pltpu.roll(below, 72, 1), 0.0)
    edge = jnp.where(lane == 1, pltpu.roll(above, 8, 1), edge)
    edge = jnp.where(lane == 2, pltpu.roll(below, 24, 1), edge)
    edge = jnp.where(lane == 3, pltpu.roll(above, 88, 1), edge)
    grad_x, h = gradients
    fields = (chi, grad_x, h * weight)
    exponents = [exponent_of(x) for x in fields]
    exponents[0] = jnp.maximum(exponents[0], exponent_of(edge))
    first, second = encode(fields, exponents)
    edges[...] = fixed(edge, exponents[0], EDGE_BITS)
    folded = edges[pl.ds(0, 32, stride=4), :]
    for i in range(1, 4):
        piece = pltpu.roll(edges[pl.ds(i, 32, stride=4), :], 32 * i, 1)
        folded = jnp.where((iota((32, 128), 1) >> 5) == i, piece, folded)
    for g in range(GX):
        at = g * ROWS
        out[at : at + 8, :] = first[g * 8 : g * 8 + 8]
        out[at + 8 : at + 16, :] = second[g * 8 : g * 8 + 8]
        out[at + 16 : at + 18, :] = folded[g * 2 : g * 2 + 2]


def inverse_y_body(got, back, lanes, twist, out, edges):
    pick = lambda at, count: [got[g * ROWS + at : g * ROWS + at + count, :] for g in range(GX)]
    first, second = (jnp.concatenate(pick(at, 8), 0) for at in (0, 8))
    folded = jnp.concatenate(pick(16, 2), 0)
    (chi, grad_x, h), exponents = decode(first, second)
    h = h * weight_of(None, lax.axis_index("gy"))[0]
    edges[pl.ds(0, 32, stride=4), :] = folded
    for i in range(1, 4):
        edges[pl.ds(i, 32, stride=4), :] = pltpu.roll(folded, 128 - 32 * i, 1)
    edge = edges[...].astype(F32) * (1.0 / scale_of(exponents[0], EDGE_BITS))
    lane = iota((128, 128), 1) >> 3
    edge48, edge96 = pltpu.roll(edge, 48, 1), pltpu.roll(edge, 96, 1)
    after = jnp.where(lane == 7, edge48, pltpu.roll(chi, 120, 1))
    after = jnp.where(lane == 15, edge96, after)
    before = jnp.where(lane == 0, edge, pltpu.roll(chi, 8, 1))
    before = jnp.where(lane == 8, edge48, before)
    left, right = packed_of(chi, (after - before) * 0.5), packed_of(grad_x, h)
    low = low_half()
    oy = oy_of()
    slope = turned([twist[2] * left[c] for c in range(2)])
    third = tuple(jnp.where(low, slope[c], oy * right[c]) for c in range(2))
    pairs = lanes_of([left, right, third], lanes, -1)
    pairs = twisted(pairs, twist, -1)
    both = jnp.concatenate(whole_of(pairs), 0)
    out[...] = mm(back[...], thrice(both, 0)).reshape(out.shape)


def pick_body(got, zb, route, chi_hbm, slope_hbm, picked, chi, slope, sems):
    fields = got[...].reshape(NZ, 384)
    middle = fields[:, 128:256]
    middle = jnp.where(iota((NZ, 128), 1) < 64, middle, middle * kz_of(NZ))
    fields = jnp.concatenate([fields[:, :128], middle, fields[:, 256:]], 1)
    values = mm(thrice(fields, 0), zb[...], 0, 0)
    cells = BX * BY
    solid, slope_x, grad_x, grad_z, slope_y, grad_y = (
        values[i * cells : (i + 1) * cells] for i in range(6)
    )
    brick = (BX, BY, NZ)
    chi[...] = solid.reshape(brick)
    slope[0] = slope_x.reshape(brick)
    slope[1] = slope_y.reshape(brick)
    slope_z = (pltpu.roll(solid, NZ - 1, 1) - pltpu.roll(solid, 1, 1)) * 0.5
    slope[2] = slope_z.reshape(brick)
    writes = [
        pltpu.make_async_copy(chi, chi_hbm, sems.at[0]),
        pltpu.make_async_copy(slope, slope_hbm, sems.at[1]),
    ]
    for write in writes:
        write.start()
    grads = twice(jnp.concatenate([grad_x, grad_y, grad_z], 0), 1)
    width = PICK_STEP * CAP * POINTS
    columns = iota((cells, width), 0).astype(F32)
    levels = iota((NZ, width), 0).astype(BF16)
    for first in range(0, GY, PICK_STEP):
        _, column, level = places(route, first, PICK_STEP)
        hot = hot_of(levels, level)
        at_level = mm(grads, jnp.concatenate([hot, hot], 0))
        here = columns == column.astype(F32)
        lines = [
            jnp.sum(jnp.where(here, at_level[j * cells : (j + 1) * cells], 0.0), 0, keepdims=True)
            for j in range(3)
        ]
        lines = jnp.concatenate(lines + [jnp.zeros((1, width), F32)], 0)
        for s in range(PICK_STEP):
            picked[first + s] = lines[:, s * 128 : (s + 1) * 128]
    for write in writes:
        write.wait()


def route_body(*refs):
    sources, (out, target, zf, owners), (normals, cells, sems) = refs[:5], refs[5:9], refs[9:]
    fetches = [
        pltpu.make_async_copy(source, place, sems.at[i])
        for i, (source, place) in enumerate(zip(sources[:4], (owners, normals, cells, target)))
    ]
    table = sources[4]
    fetches += [pltpu.make_async_copy(table.at[i], zf.at[i], sems.at[4 + i]) for i in range(2)]
    for fetch in fetches:
        fetch.start()
    for fetch in fetches[:3]:
        fetch.wait()
    square = (BLOCKS, BLOCKS)
    row, column = iota(square, 0), iota(square, 1)
    across = jnp.broadcast_to(owners[...], square)
    down = jnp.sum(jnp.where(row == column, across, 0), 1, keepdims=True)
    earlier = (down == across) & (row < column)
    rank = jnp.sum(jnp.where(earlier, 1, 0), 0, keepdims=True)
    hot = [jnp.where((row == across) & (rank == r), 1.0, 0.0) for r in range(CAP)]
    hot = jnp.concatenate(hot, 1).astype(BF16)
    cell = cells[...]
    parts = [normals[j].astype(F32) for j in range(3)]
    parts += [((cell >> 8) + 1).astype(F32), (cell & 255).astype(F32)]
    blank = jnp.zeros((BLOCKS, POINTS), F32)
    first = [jnp.concatenate([p, blank], 1) for p in parts]
    second = [jnp.concatenate([blank, p], 1) for p in parts]
    values = [jnp.concatenate(lines, 1) for lines in (first, second)]
    lines = mm(hot, jnp.concatenate(values, 0).astype(BF16))
    lines = [lines[:, i * 128 : (i + 1) * 128] for i in range(5)]
    for j in range(3):
        out[:, j, :] = lines[j]
    out[:, 3, :] = (lines[3] - 1.0) * float(NZ) + lines[4]
    for fetch in fetches[3:]:
        fetch.wait()


def return_body(owners, got, out):
    square = (BLOCKS, BLOCKS)
    row, column = iota(square, 0), iota(square, 1)
    across = jnp.broadcast_to(owners[...], square)
    down = jnp.sum(jnp.where(row == column, across, 0), 1, keepdims=True)
    earlier = (down == across) & (column < row)
    rank = jnp.sum(jnp.where(earlier, 1, 0), 1, keepdims=True)
    hot = [jnp.where((down == column) & (rank == r), 1.0, 0.0) for r in range(CAP)]
    hot = jnp.concatenate(hot, 0).astype(BF16)
    x = jnp.concatenate([got[:, j, :] for j in range(3)], 1)
    parts = []
    for _ in range(3):
        parts.append(x.astype(BF16))
        x = x - parts[-1].astype(F32)
    total = mm(jnp.concatenate([hot] * 3, 1), jnp.concatenate(parts, 0))
    for j in range(3):
        lines = total[:, j * 128 : (j + 1) * 128]
        out[j] = (lines[:BLOCKS] + swapped(lines[BLOCKS:]))[:, :POINTS]


VMEM = pl.BlockSpec(memory_space=pltpu.VMEM)
SMEM = pl.BlockSpec(memory_space=pltpu.SMEM)
HBM = pl.BlockSpec(memory_space=pltpu.HBM)


def call(body, name, outs, *operands, specs=None, out_specs=None, scratch=()):
    shapes = [s if hasattr(s, "dtype") else jax.ShapeDtypeStruct(s, F32) for s in outs]
    single = len(shapes) == 1
    return pl.pallas_call(
        body,
        name=name,
        out_shape=shapes[0] if single else shapes,
        in_specs=specs or [VMEM] * len(operands),
        out_specs=out_specs or (VMEM if single else [VMEM] * len(shapes)),
        scratch_shapes=list(scratch),
        compiler_params=pltpu.CompilerParams(vmem_limit_bytes=40 * 1024 * 1024),
    )(*operands)


def kept(x):
    return pltpu.with_memory_space_constraint(x, pltpu.HBM)


def swap(x, axis):
    return lax.all_to_all(x, axis, split_axis=0, concat_axis=0, tiled=True)


def local(normals, owners, cells, target):
    table = {k: jnp.asarray(v) for k, v in TABLES.items()}
    owner = owners.reshape(1, BLOCKS)
    brick = (BX, BY, NZ)
    message = (GY, 4, CAP * POINTS)

    by_part = jnp.moveaxis(normals, 1, 0)
    scratch = (
        pltpu.VMEM(by_part.shape, BF16),
        pltpu.VMEM(cells.shape, jnp.int32),
        pltpu.SemaphoreType.DMA((6,)),
    )
    tables_z = jax.ShapeDtypeStruct(table["zf"].shape, BF16)
    sources = (owner, by_part, cells, target, table["zf"])
    row = jax.ShapeDtypeStruct(owner.shape, jnp.int32)
    sent, target_here, zf, owner_here = call(
        route_body,
        "route",
        [message, brick, tables_z, row],
        *map(kept, sources),
        specs=[HBM] * 5,
        scratch=scratch,
    )
    route = swap(sent, "gy")
    spread = call(splat_body, "splat", [(GY, 8, 256)], route, target_here, zf)
    got = swap(spread, "gy")
    y_args = (table["y_lanes"], table["ty"])
    words = jax.ShapeDtypeStruct((GX, 16, 128), jnp.int32)
    spread = call(forward_y_body, "forward_y", [words], got, table["y_rows"], *y_args)
    got = swap(spread, "gx")
    x_args = [table[k] for k in ("x_rows", "x_back", "x_lanes", "tx", "mirror")]
    words = jax.ShapeDtypeStruct((GX * ROWS, 128), jnp.int32)
    edges = (pltpu.VMEM((128, 128), jnp.int32),)
    spread = call(spectrum_body, "spectrum", [words], got, *x_args, scratch=edges)
    got = swap(spread.reshape(GX, ROWS, 1, 128), "gx").reshape(words.shape)
    y_args = (table["y_back"],) + y_args
    spread = call(inverse_y_body, "inverse_y", [(GY, 8, 384)], got, *y_args, scratch=edges)
    got = swap(spread, "gy")
    bricks = (3,) + brick
    chi, slope, picked = call(
        pick_body,
        "pick",
        [brick, bricks, message],
        got,
        table["zb"],
        route,
        out_specs=[HBM, HBM, VMEM],
        scratch=(pltpu.VMEM(brick, F32), pltpu.VMEM(bricks, F32), pltpu.SemaphoreType.DMA((2,))),
    )
    returned = swap(picked, "gy")
    normal_grad = call(return_body, "deliver", [(3, BLOCKS, POINTS)], owner_here, returned)
    return chi, slope, jnp.moveaxis(normal_grad, 0, 1)


def solution(mesh):
    placed = (
        P(("gx", "gy"), None, None),
        P(("gx", "gy"), None),
        P(("gx", "gy"), None),
        P("gx", "gy", None),
    )
    return jax.shard_map(
        local,
        mesh=mesh,
        in_specs=placed,
        out_specs=(P("gx", "gy", None), P(None, "gx", "gy", None), P(("gx", "gy"), None, None)),
        check_vma=False,
    )
```

```python
import math

import jax
import jax.numpy as jnp
import ml_dtypes
import numpy as np
from jax import lax
from jax.experimental import pallas as pl
from jax.experimental.pallas import tpu as pltpu
from jax.sharding import PartitionSpec as P

GX, GY = 16, 32
BX, BY, NZ = 8, 8, 256
NX, NY = GX * BX, GY * BY
KZ = NZ // 2 // GY
KB = NY // BY // GX
BLOCKS, POINTS, CAP = 32, 64, 2
WIDTH = 64.0
F32, BF16 = jnp.float32, jnp.bfloat16


def halves(table, axis):
    high = table.astype(ml_dtypes.bfloat16)
    low = (table - high.astype(np.float64)).astype(ml_dtypes.bfloat16)
    return np.concatenate([high, low, high], axis)


def unit(turns):
    return np.exp(-2j * np.pi * turns)


def parts_of(w):
    return np.stack([np.stack([w.real, -w.imag]), np.stack([w.imag, w.real])])


Y_CLASS = np.array([[h, -h if h else 16] for h in range(GX)])
X_CLASS = np.array([k if k <= 8 else k - 16 for k in range(16)])


def make_tables():
    z = np.arange(NZ)
    kz = np.arange(NZ // 2)
    w = unit((kz[:, None] * z[None, :] % NZ) / NZ)
    zf = np.stack([w.real, w.imag])
    zf[1, 0] = np.where(z % 2 == 0, 1.0, -1.0)
    zb = 2.0 * zf
    zb[:, 0] = zf[:, 0]
    zb = zb / (NX * NY * NZ)
    order = lambda t: t.reshape(2, GY, KZ, NZ).transpose(1, 0, 2, 3).reshape(NZ, NZ)
    g = np.arange(GY)
    wy = parts_of(unit(Y_CLASS.reshape(-1)[:, None] * g[None, :] / GY))
    y_rows = np.einsum("abkg,zw->akzgbw", wy, np.eye(KZ)).reshape(NZ, NZ)
    g = np.arange(GX)
    wx = parts_of(unit(X_CLASS[:, None] * g[None, :] / GX))
    x_rows = np.einsum("abkg,zw->akzgbw", wx, np.eye(KB * KZ)).reshape(NZ, NZ)
    e = np.arange(8)
    w8 = unit((e[:, None] * e[None, :] % 8) / 8)
    y_lanes = np.concatenate([np.kron(np.eye(16), w8.real), np.kron(np.eye(16), w8.imag)], 1)
    x8 = lambda t: np.kron(np.eye(2), np.kron(t, np.eye(8)))
    x_lanes = np.concatenate([x8(w8.real), x8(w8.imag)], 1)
    ty = unit(np.repeat(Y_CLASS.reshape(-1), KZ)[:, None] * np.tile(e, 16)[None, :] / NY)
    tx = unit(
        np.repeat(X_CLASS, KB * KZ)[:, None] * np.tile(np.repeat(e, 8), 2)[None, :] / NX
    )
    ky = np.repeat(Y_CLASS.reshape(-1), KZ)[:, None] + GY * e[None, :]
    slope_y = np.tile(np.sin(2 * np.pi * (ky % NY) / NY), (1, 16))
    kx = np.repeat(X_CLASS, KB * KZ)[:, None] + GX * np.repeat(e, 8)[None, :]
    slope_x = np.tile(np.sin(2 * np.pi * (kx % NX) / NX), (1, 2))
    twist = lambda t, s: np.stack([t.real, -t.imag, s]).astype(np.float32)
    mirror = np.zeros((2, 2, 128, 128), np.float32)
    for m in range(2):
        for n in range(2):
            for f in range(2):
                for a in range(8):
                    for b in range(8):
                        src = f * 64 + (-a - m) % 8 * 8 + (-b - n) % 8
                        mirror[m, n, src, f * 64 + a * 8 + b] = 1.0
    return dict(
        zf=halves(order(zf), 1)[:, : 2 * NZ].reshape(NZ, 2, NZ).swapaxes(0, 1),
        zb=halves(order(zb), 0),
        y_rows=halves(y_rows, 1),
        x_rows=halves(x_rows, 1),
        y_back=halves(y_rows.T, 1),
        x_back=halves(x_rows.T, 1),
        y_lanes=halves(y_lanes, 0),
        x_lanes=halves(x_lanes, 0),
        ty=twist(ty, slope_y),
        tx=twist(tx, slope_x)[:2],
        mirror=np.tile(np.concatenate([mirror[:, 0], mirror[:, 1]], 2), (1, 2, 1)).astype(
            ml_dtypes.bfloat16
        ),
    )


TABLES = make_tables()


def split(x):
    high = x.astype(BF16)
    return high, (x - high.astype(F32)).astype(BF16)


def mm(a, b, ca=1, cb=0):
    return lax.dot_general(a, b, (((ca,), (cb,)), ((), ())), preferred_element_type=F32)


def thrice(x, axis):
    high, low = split(x)
    return jnp.concatenate([high, high, low], axis)


def twice(x, axis):
    return jnp.concatenate(split(x), axis)


def lanes_of(pairs, table, sign):
    count, rows = len(pairs), pairs[0][0].shape[0]
    stacked = jnp.concatenate([p[0] for p in pairs] + [p[1] for p in pairs], 0)
    out = mm(thrice(stacked, 1), table[...])
    result = []
    for i in range(count):
        a = out[i * rows : (i + 1) * rows]
        b = out[(count + i) * rows : (count + i + 1) * rows]
        if sign > 0:
            result.append((a[:, :128] - b[:, 128:], a[:, 128:] + b[:, :128]))
        else:
            result.append((a[:, :128] + b[:, 128:], b[:, :128] - a[:, 128:]))
    return result


def twisted(pairs, twist, sign):
    c, s = twist[0], twist[1]
    if sign > 0:
        return [(a * c + b * s, b * c - a * s) for a, b in pairs]
    return [(a * c - b * s, b * c + a * s) for a, b in pairs]


def halves_of(real, imag):
    return [(real[:, i * 128 : (i + 1) * 128], imag[:, i * 128 : (i + 1) * 128]) for i in range(2)]


def whole_of(pairs):
    return tuple(jnp.concatenate([p[c] for p in pairs], 1) for c in range(2))


def iota(shape, dim):
    return lax.broadcasted_iota(jnp.int32, shape, dim)


def places(route, first, count):
    rows = jnp.concatenate([route[s] for s in range(first, first + count)], 1)
    cell = rows[3:4]
    column = jnp.floor(cell * (1.0 / NZ))
    return rows.astype(BF16), column.astype(BF16), (cell - column * NZ).astype(BF16)


def hot_of(labels, values):
    return jnp.where(labels == values, jnp.ones_like(labels), jnp.zeros_like(labels))


def kz_of(rows):
    row = iota((rows, 128), 0)
    return (KZ * (row >> 3) + (row & 3)).astype(F32)


def odd(k, length):
    k = k & (length - 1)
    u = jnp.where(k < length // 2, k, k - length).astype(F32)
    return u, jnp.where(k == length // 2, 0.0, u)


def ky_of(gx, row, lane):
    second = ((row >> 2) & 1) == 1
    kb = jnp.where(second, jnp.where(gx == 0, 16, -gx), gx)
    return kb + GY * (lane & 7)


def oy_of():
    row, lane = iota((128, 128), 0), iota((128, 128), 1)
    return odd(ky_of(row >> 3, row, lane), NY)[1]


STEP, PICK_STEP = 8, 2


def splat_body(route, target, zf, out):
    width = STEP * CAP * POINTS
    columns = iota((BX * BY, width), 0).astype(BF16)
    levels = iota((NZ, width), 0).astype(BF16)
    cells = BX * BY
    nothing = jnp.zeros((cells, width), BF16)
    blank = jnp.zeros((3 * cells, NZ), F32)
    field = jnp.concatenate([blank, target[...].reshape(cells, NZ)], 0).T
    for first in range(0, GY, STEP):
        rows, column, level = places(route, first, STEP)
        here = hot_of(columns, column)
        weighted = [here * rows[j : j + 1] for j in range(3)] + [nothing]
        field = field + mm(hot_of(levels, level), jnp.concatenate(weighted, 0), 1, 1)
    spread = mm(jnp.concatenate([zf[0], zf[1], zf[0]], 1), thrice(field, 0))
    right = spread[:, 128:]
    right = jnp.where(iota((NZ, 128), 1) < 64, right * kz_of(NZ), right)
    out[...] = jnp.concatenate([spread[:, :128], right], 1).reshape(out.shape)


def swapped(x):
    return pltpu.roll(x, 64, 1)


def low_half(rows=128):
    return iota((rows, 128), 1) < 64


def packed_of(real, imag):
    low = low_half()
    return jnp.where(low, real, swapped(imag)), jnp.where(low, swapped(real), imag)


def weight_of(gx, gy):
    row, lane = iota((128, 128), 0), iota((128, 128), 1)
    gx = row >> 3 if gx is None else gx
    uy, _ = odd(ky_of(gx, row, lane), NY)
    uz = (KZ * gy + (row & 3)).astype(F32)
    square = uy * uy + uz * uz + 1.0
    small = lax.rsqrt(square)
    return small, square * small


BITS, SPLIT, BIAS, EDGE_BITS = 20, 11, 128, 30
ROWS = 18


def scale_of(exponent, bits):
    return jnp.exp2((bits - exponent).astype(F32))


def exponent_of(x):
    top = jnp.broadcast_to(jnp.max(jnp.abs(x), 1, keepdims=True), x.shape)
    power = jnp.floor(jnp.log2(jnp.maximum(top, 1e-26)) + 0.001) + 1.0
    return power.astype(jnp.int32)


def fixed(x, exponent, bits):
    return jnp.floor(x * scale_of(exponent, bits) + 0.5).astype(jnp.int32)


def encode(fields, exponents):
    a, b, c = (fixed(x, e, BITS) for x, e in zip(fields, exponents))
    e = [x + BIAS for x in exponents]
    mark = e[0] | (e[1] << 8) | (e[2] << 16)
    lane = iota((128, 128), 1)
    bit = jnp.where(lane < 24, (mark >> (lane & 31)) & 1, 0)
    first = (a << SPLIT) | (c & 0x7FF)
    second = (b << SPLIT) | ((c >> SPLIT) & 0x3FF) | (bit << 10)
    return first, second


def decode(first, second):
    lane = iota((128, 128), 1)
    bit = ((second >> 10) & 1) << (lane & 7)
    exponents = []
    for i in range(3):
        here = jnp.where((lane >> 3) == i, bit, 0).astype(F32)
        total = jnp.broadcast_to(jnp.sum(here, 1, keepdims=True), here.shape)
        exponents.append(total.astype(jnp.int32) - BIAS)
    a, b = first >> SPLIT, second >> SPLIT
    c = (((second & 0x3FF) << 22) >> SPLIT) | (first & 0x7FF)
    fields = [x.astype(F32) * (1.0 / scale_of(e, BITS)) for x, e in zip((a, b, c), exponents)]
    return fields, exponents


def forward_y_body(got, rows, lanes, twist, out):
    x = mm(rows[...], thrice(got[...].reshape(NZ, NZ), 0))
    pairs = twisted(halves_of(x[:128], x[128:]), twist, 1)
    left, right = lanes_of(pairs, lanes, 1)
    low = low_half()
    oy = oy_of()
    real, imag = (jnp.where(low, left[c], oy * left[c] + swapped(right[c])) for c in range(2))
    target = jnp.where(low, swapped(right[0]), right[1])
    part_x, part_yz = packed_of(real, imag)
    fields = (part_x, part_yz * weight_of(None, lax.axis_index("gy"))[0], target)
    first, second = encode(fields, [exponent_of(x) for x in fields])
    out[:, 0:8, :] = first.reshape(GX, 8, 128)
    out[:, 8:16, :] = second.reshape(GX, 8, 128)


def filters(gx, gy):
    shape = (128, 128)
    row, lane = iota(shape, 0), iota(shape, 1)
    kxb = row >> 3
    ux, ox = odd(kxb + GX * ((lane >> 3) & 7) - jnp.where(kxb > 8, GX, 0), NX)
    uy, _ = odd(ky_of(gx, row, lane), NY)
    kz = KZ * gy + (row & 3)
    uz = kz.astype(F32)
    gain = math.sqrt(float(NX * NY * NZ) * float(BX * BY * NZ) / (float(BLOCKS * POINTS) * 700.0))
    plane = ux * ux + uy * uy

    def base(ksq):
        value = gain * jnp.exp(ksq * (-1.0 / (2.0 * WIDTH**2))) / jnp.maximum(ksq, 1.0)
        return jnp.where(ksq == 0.0, 0.0, value)

    base0 = base(plane + uz * uz)
    base1 = jnp.where(kz == 0, base(plane + float(NZ // 2) ** 2), base0)
    return ox, (base0 + base1) * 0.5, (base0 - base1) * 0.5


def mirrored(pair, gx, mirror):
    x = jnp.concatenate(pair, 0).reshape(2, GX, 8, 128)
    x = jnp.concatenate([x[:, (GX - i) % GX : (GX - i) % GX + 1] for i in range(GX)], 1)
    x = x.reshape(2 * GX, 8, 128)
    x = jnp.where(gx == 0, x, jnp.concatenate([x[:, 4:], x[:, :4]], 1)).reshape(256, 128)
    special = jnp.concatenate([x[64:72], x[192:200]], 0)
    whole, special = (mm(twice(part, 1), mirror[i]) for i, part in enumerate((x, special)))
    parts = [whole[:64], special[:8], whole[72:192], special[8:], whole[200:]]
    whole = jnp.concatenate(parts, 0)
    half_y = (((iota((256, 128), 0) >> 2) & 1) == 1) & (gx == 0)
    whole = jnp.where(half_y, whole[:, 128:], whole[:, :128])
    return whole[:128], -whole[128:]


def turned(pair):
    return -pair[1], pair[0]


def spectrum_body(got, rows, back, lanes, twist, mirror, out, edges):
    gx, gy = lax.axis_index("gx"), lax.axis_index("gy")
    words = (got[:, i * 8 : i * 8 + 8, :].reshape(128, 128) for i in range(2))
    (part_x, part_yz, target), _ = decode(*words)
    weight = weight_of(gx, gy)[1]
    part_yz = part_yz * weight
    x = [*packed_of(part_x, part_yz), target, swapped(target)]
    x = [part.reshape(GX, 8, 128) for part in x]
    x = [jnp.concatenate(x[i : i + 2], 1).reshape(NZ, 128) for i in (0, 2)]
    x = jnp.concatenate(x, 1)
    x = mm(rows[...], thrice(x, 0))
    pairs = twisted(halves_of(x[:128], x[128:]), twist, 1)
    left, right = lanes_of(pairs, lanes, 1)
    ox, mean, diff = filters(gx, gy)
    low = low_half()

    div = [jnp.where(low, ox * left[c], left[c]) for c in range(2)]
    div = turned([d + swapped(d) for d in div])
    target = [jnp.where(low, right[c], swapped(right[c])) for c in range(2)]
    other = mirrored([jnp.where(low, div[c], target[c]) for c in range(2)], gx, mirror)
    div2 = [jnp.where(low, other[c], swapped(other[c])) for c in range(2)]
    target2 = [jnp.where(low, swapped(other[c]), other[c]) for c in range(2)]
    chi = [-(mean * div[c] + diff * div2[c]) for c in range(2)]
    chi2 = [-(mean * div2[c] + diff * div[c]) for c in range(2)]
    h = [
        0.25 * (mean * (chi[c] - target[c]) + diff * (chi2[c] - target2[c])) for c in range(2)
    ]
    h = turned(h)
    pairs = [chi, tuple(jnp.where(low, ox * h[c], h[c]) for c in range(2))]
    pairs = twisted(lanes_of(pairs, lanes, -1), twist, -1)
    both = jnp.concatenate(whole_of(pairs), 0)
    x = mm(back[...], thrice(both, 0)).reshape(GX, 16, NZ)
    chi, _ = packed_of(*(x[:, c : c + 8, :128].reshape(128, 128) for c in (0, 8)))
    gradients = packed_of(*(x[:, c : c + 8, 128:].reshape(128, 128) for c in (0, 8)))

    below = jnp.concatenate([chi[120:], chi[:120]], 0)
    above = jnp.concatenate([chi[8:], chi[:8]], 0)
    lane = iota((128, 128), 1) >> 3
    edge = jnp.where(lane == 0, pltpu.roll(below, 72, 1), 0.0)
    edge = jnp.where(lane == 1, pltpu.roll(above, 8, 1), edge)
    edge = jnp.where(lane == 2, pltpu.roll(below, 24, 1), edge)
    edge = jnp.where(lane == 3, pltpu.roll(above, 88, 1), edge)
    grad_x, h = gradients
    fields = (chi, grad_x, h * weight)
    largest = jnp.maximum(jnp.abs(chi), jnp.abs(edge))
    exponents = [exponent_of(x) for x in (largest,) + fields[1:]]
    first, second = encode(fields, exponents)
    edges[...] = fixed(edge, exponents[0], EDGE_BITS)
    folded = edges[pl.ds(0, 32, stride=4), :]
    for i in range(1, 4):
        piece = pltpu.roll(edges[pl.ds(i, 32, stride=4), :], 32 * i, 1)
        folded = jnp.where((iota((32, 128), 1) >> 5) == i, piece, folded)
    for g in range(GX):
        at = g * ROWS
        out[at : at + 8, :] = first[g * 8 : g * 8 + 8]
        out[at + 8 : at + 16, :] = second[g * 8 : g * 8 + 8]
        out[at + 16 : at + 18, :] = folded[g * 2 : g * 2 + 2]


def inverse_y_body(got, back, lanes, twist, out, edges):
    pick = lambda at, count: [got[g * ROWS + at : g * ROWS + at + count, :] for g in range(GX)]
    first, second = (jnp.concatenate(pick(at, 8), 0) for at in (0, 8))
    folded = jnp.concatenate(pick(16, 2), 0)
    (chi, grad_x, h), exponents = decode(first, second)
    h = h * weight_of(None, lax.axis_index("gy"))[0]
    edges[pl.ds(0, 32, stride=4), :] = folded
    for i in range(1, 4):
        edges[pl.ds(i, 32, stride=4), :] = pltpu.roll(folded, 128 - 32 * i, 1)
    edge = edges[...].astype(F32) * (1.0 / scale_of(exponents[0], EDGE_BITS))
    lane = iota((128, 128), 1) >> 3
    edge48, edge96 = pltpu.roll(edge, 48, 1), pltpu.roll(edge, 96, 1)
    after = jnp.where(lane == 7, edge48, pltpu.roll(chi, 120, 1))
    after = jnp.where(lane == 15, edge96, after)
    before = jnp.where(lane == 0, edge, pltpu.roll(chi, 8, 1))
    before = jnp.where(lane == 8, edge48, before)
    left, right = packed_of(chi, (after - before) * 0.5), packed_of(grad_x, h)
    low = low_half()
    oy = oy_of()
    slope = turned([twist[2] * left[c] for c in range(2)])
    third = tuple(jnp.where(low, slope[c], oy * right[c]) for c in range(2))
    pairs = lanes_of([left, right, third], lanes, -1)
    pairs = twisted(pairs, twist, -1)
    both = jnp.concatenate(whole_of(pairs), 0)
    out[...] = mm(back[...], thrice(both, 0)).reshape(out.shape)


def pick_body(got, zb, route, chi_hbm, slope_hbm, picked, chi, slope, sems):
    fields = got[...].reshape(NZ, 384)
    middle = fields[:, 128:256]
    middle = jnp.where(iota((NZ, 128), 1) < 64, middle, middle * kz_of(NZ))
    fields = jnp.concatenate([fields[:, :128], middle, fields[:, 256:]], 1)
    values = mm(thrice(fields, 0), zb[...], 0, 0)
    cells = BX * BY
    solid, slope_x, grad_x, grad_z, slope_y, grad_y = (
        values[i * cells : (i + 1) * cells] for i in range(6)
    )
    brick = (BX, BY, NZ)
    chi[...] = solid.reshape(brick)
    slope[0] = slope_x.reshape(brick)
    slope[1] = slope_y.reshape(brick)
    slope_z = (pltpu.roll(solid, NZ - 1, 1) - pltpu.roll(solid, 1, 1)) * 0.5
    slope[2] = slope_z.reshape(brick)
    writes = [
        pltpu.make_async_copy(chi, chi_hbm, sems.at[0]),
        pltpu.make_async_copy(slope, slope_hbm, sems.at[1]),
    ]
    for write in writes:
        write.start()
    grads = twice(jnp.concatenate([grad_x, grad_y, grad_z], 0), 1)
    width = PICK_STEP * CAP * POINTS
    columns = iota((cells, width), 0).astype(F32)
    levels = iota((NZ, width), 0).astype(BF16)
    for first in range(0, GY, PICK_STEP):
        _, column, level = places(route, first, PICK_STEP)
        hot = hot_of(levels, level)
        at_level = mm(grads, jnp.concatenate([hot, hot], 0))
        here = columns == column.astype(F32)
        lines = [
            jnp.sum(jnp.where(here, at_level[j * cells : (j + 1) * cells], 0.0), 0, keepdims=True)
            for j in range(3)
        ]
        lines = jnp.concatenate(lines + [jnp.zeros((1, width), F32)], 0)
        for s in range(PICK_STEP):
            picked[first + s] = lines[:, s * 128 : (s + 1) * 128]
    for write in writes:
        write.wait()


def route_body(*refs):
    sources, (out, target, zf, owners), (normals, cells, sems) = refs[:5], refs[5:9], refs[9:]
    fetches = [
        pltpu.make_async_copy(source, place, sems.at[i])
        for i, (source, place) in enumerate(zip(sources[:4], (owners, normals, cells, target)))
    ]
    table = sources[4]
    fetches += [pltpu.make_async_copy(table.at[i], zf.at[i], sems.at[4 + i]) for i in range(2)]
    for fetch in fetches:
        fetch.start()
    for fetch in fetches[:3]:
        fetch.wait()
    square = (BLOCKS, BLOCKS)
    row, column = iota(square, 0), iota(square, 1)
    across = jnp.broadcast_to(owners[...], square)
    down = jnp.sum(jnp.where(row == column, across, 0), 1, keepdims=True)
    earlier = (down == across) & (row < column)
    rank = jnp.sum(jnp.where(earlier, 1, 0), 0, keepdims=True)
    hot = [jnp.where((row == across) & (rank == r), 1.0, 0.0) for r in range(CAP)]
    hot = jnp.concatenate(hot, 1).astype(BF16)
    cell = cells[...]
    parts = [normals[j].astype(F32) for j in range(3)]
    parts += [((cell >> 8) + 1).astype(F32), (cell & 255).astype(F32)]
    blank = jnp.zeros((BLOCKS, POINTS), F32)
    first = [jnp.concatenate([p, blank], 1) for p in parts]
    second = [jnp.concatenate([blank, p], 1) for p in parts]
    values = [jnp.concatenate(lines, 1) for lines in (first, second)]
    lines = mm(hot, jnp.concatenate(values, 0).astype(BF16))
    lines = [lines[:, i * 128 : (i + 1) * 128] for i in range(5)]
    for j in range(3):
        out[:, j, :] = lines[j]
    out[:, 3, :] = (lines[3] - 1.0) * float(NZ) + lines[4]
    for fetch in fetches[3:]:
        fetch.wait()


def return_body(owners, got, out):
    square = (BLOCKS, BLOCKS)
    row, column = iota(square, 0), iota(square, 1)
    across = jnp.broadcast_to(owners[...], square)
    down = jnp.sum(jnp.where(row == column, across, 0), 1, keepdims=True)
    earlier = (down == across) & (column < row)
    rank = jnp.sum(jnp.where(earlier, 1, 0), 1, keepdims=True)
    hot = [jnp.where((down == column) & (rank == r), 1.0, 0.0) for r in range(CAP)]
    hot = jnp.concatenate(hot, 0).astype(BF16)
    x = jnp.concatenate([got[:, j, :] for j in range(3)], 1)
    parts = []
    for _ in range(3):
        parts.append(x.astype(BF16))
        x = x - parts[-1].astype(F32)
    total = mm(jnp.concatenate([hot] * 3, 1), jnp.concatenate(parts, 0))
    for j in range(3):
        lines = total[:, j * 128 : (j + 1) * 128]
        out[j] = (lines[:BLOCKS] + swapped(lines[BLOCKS:]))[:, :POINTS]


VMEM = pl.BlockSpec(memory_space=pltpu.VMEM)
SMEM = pl.BlockSpec(memory_space=pltpu.SMEM)
HBM = pl.BlockSpec(memory_space=pltpu.HBM)


def call(body, name, outs, *operands, specs=None, out_specs=None, scratch=()):
    shapes = [s if hasattr(s, "dtype") else jax.ShapeDtypeStruct(s, F32) for s in outs]
    single = len(shapes) == 1
    return pl.pallas_call(
        body,
        name=name,
        out_shape=shapes[0] if single else shapes,
        in_specs=specs or [VMEM] * len(operands),
        out_specs=out_specs or (VMEM if single else [VMEM] * len(shapes)),
        scratch_shapes=list(scratch),
        compiler_params=pltpu.CompilerParams(vmem_limit_bytes=40 * 1024 * 1024),
    )(*operands)


def kept(x):
    return pltpu.with_memory_space_constraint(x, pltpu.HBM)


def swap(x, axis):
    return lax.all_to_all(x, axis, split_axis=0, concat_axis=0, tiled=True)


def local(normals, owners, cells, target):
    table = {k: jnp.asarray(v) for k, v in TABLES.items()}
    owner = owners.reshape(1, BLOCKS)
    brick = (BX, BY, NZ)
    message = (GY, 4, CAP * POINTS)

    by_part = jnp.moveaxis(normals, 1, 0)
    scratch = (
        pltpu.VMEM(by_part.shape, BF16),
        pltpu.VMEM(cells.shape, jnp.int32),
        pltpu.SemaphoreType.DMA((6,)),
    )
    tables_z = jax.ShapeDtypeStruct(table["zf"].shape, BF16)
    sources = (owner, by_part, cells, target, table["zf"])
    row = jax.ShapeDtypeStruct(owner.shape, jnp.int32)
    sent, target_here, zf, owner_here = call(
        route_body,
        "route",
        [message, brick, tables_z, row],
        *map(kept, sources),
        specs=[HBM] * 5,
        scratch=scratch,
    )
    route = swap(sent, "gy")
    spread = call(splat_body, "splat", [(GY, 8, 256)], route, target_here, zf)
    got = swap(spread, "gy")
    y_args = (table["y_lanes"], table["ty"])
    words = jax.ShapeDtypeStruct((GX, 16, 128), jnp.int32)
    spread = call(forward_y_body, "forward_y", [words], got, table["y_rows"], *y_args)
    got = swap(spread, "gx")
    x_args = [table[k] for k in ("x_rows", "x_back", "x_lanes", "tx", "mirror")]
    words = jax.ShapeDtypeStruct((GX * ROWS, 128), jnp.int32)
    edges = (pltpu.VMEM((128, 128), jnp.int32),)
    spread = call(spectrum_body, "spectrum", [words], got, *x_args, scratch=edges)
    got = swap(spread.reshape(GX, ROWS, 1, 128), "gx").reshape(words.shape)
    y_args = (table["y_back"],) + y_args
    spread = call(inverse_y_body, "inverse_y", [(GY, 8, 384)], got, *y_args, scratch=edges)
    got = swap(spread, "gy")
    bricks = (3,) + brick
    chi, slope, picked = call(
        pick_body,
        "pick",
        [brick, bricks, message],
        got,
        table["zb"],
        route,
        out_specs=[HBM, HBM, VMEM],
        scratch=(pltpu.VMEM(brick, F32), pltpu.VMEM(bricks, F32), pltpu.SemaphoreType.DMA((2,))),
    )
    returned = swap(picked, "gy")
    normal_grad = call(return_body, "deliver", [(3, BLOCKS, POINTS)], owner_here, returned)
    return chi, slope, jnp.moveaxis(normal_grad, 0, 1)


def solution(mesh):
    placed = (
        P(("gx", "gy"), None, None),
        P(("gx", "gy"), None),
        P(("gx", "gy"), None),
        P("gx", "gy", None),
    )
    return jax.shard_map(
        local,
        mesh=mesh,
        in_specs=placed,
        out_specs=(P("gx", "gy", None), P(None, "gx", "gy", None), P(("gx", "gy"), None, None)),
        check_vma=False,
    )
```
